256 devices in a mesh: seq: 32 (over z_lo, y, x), dp: 8 (over z_hi, core).
Axes of the slice: x: 4, y: 4, z: 8 (z_hi: 4, z_lo: 2; z = z_hi * 2 + z_lo), core: 2. Of those that a mesh axis runs over, the one named last changes fastest.
Arguments:
- frames: bfloat16 [8, 4096, 1024], P('dp', 'seq'), may hold values from -6 to 6
- cotangent: bfloat16 [8, 4096, 1024], P('dp', 'seq'), may hold values from -6 to 6
- lengths: int32 [8], P('dp'), may hold values from 2048 to 4096, as said below
- w_qkv: bfloat16 [1024, 1536], replicated
- w_out: bfloat16 [512, 1024], replicated, may hold values from -1.5 to 1.5
- w_up: bfloat16 [1024, 2048], replicated, may hold values from -0.1875 to 0.1875
- w_down: bfloat16 [1024, 1024], replicated, may hold values from -0.1875 to 0.1875
- conv_kernel: float32 [31, 1024], replicated, may hold values from -1 to 1
Outputs:
- layer_out: bfloat16 [8, 4096, 1024], P('dp', 'seq')
- d_frames: bfloat16 [8, 4096, 1024], P('dp', 'seq')
- g_qkv: float32 [1024, 1536], P('dp', 'seq')
- g_out: float32 [512, 1024], P('dp', 'seq')
- g_up: float32 [1024, 2048], P('dp', 'seq')
- g_down: float32 [1024, 1024], P('dp', 'seq')
- g_kernel: float32 [31, 1024], P(None, 'seq')
The draws below stay inside these ranges and needn't reach their ends.
Inputs may be any that keep to these rules, and one draw needn't show every extreme that they name: `lengths`: some recording has all 4096 frames valid and another has 2048.
All inputs are finite; a program needn't handle non-finite values.
Results may differ from the reference program's by a relative error of at most 0.04.
The reference program's roundings to bfloat16 on the way count: a program that leaves them out, or rounds other values in their place, can miss the bound.
Values may be sent and summed in bfloat16 or wider, within the bound.
No kernel may reach another device: no remote copies, remote signals or barrier semaphores. Data moves between devices by JAX's collectives and lax.ppermute only.
A program may use at most 128 MiB of HBM per device.

```python
import jax
import jax.numpy as jnp
from jax import lax

D = 1024
HEADS = 8
HEAD = 64
HID = 2048
KERNEL = 31
BAND = 512
SLICE = 128
INNER = 512
HALF = 1024
REACH = 4
FRAMES = 4096
RECS = 8


def draw_lengths(key, part):
    key = jax.random.fold_in(key, 7)
    pick_key, value_key = jax.random.split(key)
    values = jax.random.randint(value_key, (RECS,), FRAMES // 2, FRAMES + 1, dtype=jnp.int32)
    chosen = jax.random.randint(pick_key, (), 0, RECS, dtype=jnp.int32)
    order = jnp.arange(RECS, dtype=jnp.int32)
    values = jnp.where(order == chosen, FRAMES, values)
    values = jnp.where(order == (chosen + 1) % RECS, FRAMES // 2, values)
    return values


def draw_w_qkv(key, part):
    key = jax.random.fold_in(key, 11)
    query_key, rest_key = jax.random.split(key, 2)
    scale = D ** (-0.5)
    query_part = jax.random.normal(query_key, (D, INNER), jnp.float32) * scale
    rest_part = jax.random.normal(rest_key, (D, 2 * INNER), jnp.float32) * scale
    whole = jnp.concatenate([query_part, rest_part], axis=1)
    return whole.astype(jnp.bfloat16)


def levels(rng, extent, shards, smallest, high):
    def one(position, parts):
        draws = jax.random.uniform(jax.random.fold_in(jax.random.fold_in(rng, 6), position), (parts,), jnp.float32, smallest / len(shards), high / len(shards))
        return jnp.repeat(jnp.exp(draws), extent[position] // parts).reshape((-1,) + (1,) * (len(extent) - position - 1))

    loudness = one(*shards[0])
    for cut in shards[1:]:
        loudness = loudness * one(*cut)
    return loudness


def gaussian(key, extent, scale, bound, shards=(), kind=jnp.bfloat16):
    array = scale * jax.random.normal(key, extent, jnp.float32)
    if shards:
        array = array * levels(key, extent, shards, -0.22, 0.18)
    return jnp.clip(array, -bound, bound).astype(kind)


def setup_inputs(seed: int = 0) -> dict:
    keys = jax.random.split(jax.random.key(seed), 9)
    frames = gaussian(keys[0], (RECS, FRAMES, D), 1.0, 6.0, ((0, 8), (1, 32)))
    cotangent = gaussian(keys[1], (RECS, FRAMES, D), 1.0, 6.0, ((0, 8), (1, 32)))
    lengths = draw_lengths(jax.random.fold_in(keys[8], 71), 0)
    w_qkv = draw_w_qkv(jax.random.fold_in(keys[8], 71), 0)
    w_out = gaussian(keys[4], (INNER, D), (HEAD // 4) ** -0.5, 1.5)
    w_up = gaussian(keys[5], (D, HID), D ** -0.5, 0.1875)
    w_down = gaussian(keys[6], (HALF, D), HALF ** -0.5, 0.1875)
    conv_kernel = gaussian(keys[7], (KERNEL, HALF), KERNEL ** -0.5, 1.0, (), jnp.float32)
    return {"frames": frames, "cotangent": cotangent, "lengths": lengths, "w_qkv": w_qkv, "w_out": w_out, "w_up": w_up, "w_down": w_down, "conv_kernel": conv_kernel}


EPSILON = 1e-05
NEG_LARGE = -1e+30
HALF_ROOT = 0.7071067811865476
NORMAL_PEAK = 0.3989422804014327

def normalize(values):
    row_mean = lax.optimization_barrier(jnp.mean(values, axis=-1, keepdims=True))
    centred = values - row_mean
    inverse = lax.rsqrt(lax.optimization_barrier(jnp.mean(centred * centred, axis=-1, keepdims=True)) + EPSILON)
    return (centred * inverse, inverse)

def norm_back(gradient, unit_rows, inverse):
    return inverse * (gradient - lax.optimization_barrier(jnp.mean(gradient, axis=-1, keepdims=True)) - unit_rows * lax.optimization_barrier(jnp.mean(gradient * unit_rows, axis=-1, keepdims=True)))

def gelu_slope(upper):
    return 0.5 * (1.0 + lax.erf(upper * HALF_ROOT)) + upper * jnp.exp(-0.5 * upper * upper) * NORMAL_PEAK

def band_forward(query_rows, window, query_pos, key_pos, length):
    slice_rows = query_rows.shape[0]
    query_heads = query_rows.astype(jnp.float32).reshape(slice_rows, HEADS, HEAD)
    key_heads = window[:, :INNER].astype(jnp.float32).reshape(-1, HEADS, HEAD)
    value_heads = window[:, INNER:].astype(jnp.float32).reshape(-1, HEADS, HEAD)
    scores = jnp.einsum('shd,whd->hsw', query_heads, key_heads) * HEAD ** (-0.5)
    allowed = (jnp.abs(query_pos[:, None] - key_pos[None, :]) <= BAND) & (key_pos[None, :] >= 0) & (key_pos[None, :] < length)
    scores = jnp.where(allowed[None], scores, NEG_LARGE)
    row_max = lax.optimization_barrier(jnp.max(scores, axis=-1, keepdims=True))
    weights = jnp.where(allowed[None], jnp.exp(scores - row_max), 0.0)
    row_total = jnp.maximum(lax.optimization_barrier(jnp.sum(weights, axis=-1, keepdims=True)), 1.0)
    soft_weights = (weights / row_total).astype(jnp.bfloat16)
    context = jnp.einsum('hsw,whd->shd', soft_weights.astype(jnp.float32), value_heads)
    return (soft_weights, context.reshape(slice_rows, INNER).astype(jnp.bfloat16))

def band_backward(query_rows, window, soft_weights, d_context):
    slice_rows = query_rows.shape[0]
    query_heads = query_rows.astype(jnp.float32).reshape(slice_rows, HEADS, HEAD)
    key_heads = window[:, :INNER].astype(jnp.float32).reshape(-1, HEADS, HEAD)
    value_heads = window[:, INNER:].astype(jnp.float32).reshape(-1, HEADS, HEAD)
    d_heads = d_context.astype(jnp.float32).reshape(slice_rows, HEADS, HEAD)
    d_soft = jnp.einsum('shd,whd->hsw', d_heads, value_heads)
    weights_f = soft_weights.astype(jnp.float32)
    row_dot = lax.optimization_barrier(jnp.sum(weights_f * d_soft, axis=-1, keepdims=True))
    d_scores = (weights_f * (d_soft - row_dot) * HEAD ** (-0.5)).astype(jnp.bfloat16).astype(jnp.float32)
    d_query = jnp.einsum('hsw,whd->shd', d_scores, key_heads).reshape(slice_rows, INNER)
    d_key = jnp.einsum('hsw,shd->whd', d_scores, query_heads).reshape(-1, INNER)
    d_value = jnp.einsum('hsw,shd->whd', weights_f, d_heads).reshape(-1, INNER)
    return (d_query, jnp.concatenate([d_key, d_value], axis=1))

def record(frames, cotangent, length, w_qkv, w_out, w_up, w_down, conv_kernel):
    positions = jnp.arange(FRAMES, dtype=jnp.int32)
    unit_rows, unit_inv = normalize(frames.astype(jnp.float32))
    normed = unit_rows.astype(jnp.bfloat16)
    joined_rows = jnp.dot(normed, w_qkv, preferred_element_type=jnp.float32).astype(jnp.bfloat16)
    query_rows = joined_rows[:, :INNER]
    keyval = jnp.pad(joined_rows[:, INNER:], ((REACH * SLICE, REACH * SLICE), (0, 0)))
    window_rows = (2 * REACH + 1) * SLICE
    block_count = FRAMES // SLICE
    blocks = jnp.arange(block_count, dtype=jnp.int32)

    def pieces(block_index):
        start_row = block_index * SLICE
        query_block = lax.dynamic_slice_in_dim(query_rows, start_row, SLICE, 0)
        window = lax.dynamic_slice_in_dim(keyval, start_row, window_rows, 0)
        query_pos = start_row + jnp.arange(SLICE, dtype=jnp.int32)
        key_pos = start_row - REACH * SLICE + jnp.arange(window_rows, dtype=jnp.int32)
        return (query_block, window, query_pos, key_pos)

    def forward_block(block_index):
        query_block, window, query_pos, key_pos = pieces(block_index)
        return band_forward(query_block, window, query_pos, key_pos, length)[1]
    context = lax.map(forward_block, blocks).reshape(FRAMES, INNER)
    upper = jnp.dot(normed, w_up, preferred_element_type=jnp.float32)
    hidden = jax.nn.gelu(upper, approximate=False).astype(jnp.bfloat16)
    resid_half = hidden[:, :HALF]
    gate_unit, gate_inv = normalize(hidden[:, HALF:].astype(jnp.float32))
    valid_rows = (positions < length)[:, None]
    gating = jnp.where(valid_rows, gate_unit, 0.0).astype(jnp.bfloat16)
    margin = KERNEL // 2
    gating_pad = jnp.pad(gating.astype(jnp.float32), ((margin, margin), (0, 0)))
    conv_out = jnp.zeros((FRAMES, HALF), jnp.float32)
    for offset in range(KERNEL):
        conv_out = conv_out + conv_kernel[offset] * gating_pad[offset:offset + FRAMES]
    gated_rows = (resid_half.astype(jnp.float32) * conv_out).astype(jnp.bfloat16)
    layer_out = (frames.astype(jnp.float32) + jnp.dot(context, w_out, preferred_element_type=jnp.float32) + jnp.dot(gated_rows, w_down, preferred_element_type=jnp.float32)).astype(jnp.bfloat16)
    g_down = jnp.dot(gated_rows.T, cotangent, preferred_element_type=jnp.float32)
    d_gated = jnp.dot(cotangent, w_down.T, preferred_element_type=jnp.float32).astype(jnp.bfloat16)
    d_resid = d_gated.astype(jnp.float32) * conv_out
    d_conv = (d_gated.astype(jnp.float32) * resid_half.astype(jnp.float32)).astype(jnp.bfloat16)
    d_conv_f = d_conv.astype(jnp.float32)
    g_kernel = jnp.stack([lax.optimization_barrier(jnp.sum(gating_pad[offset:offset + FRAMES] * d_conv_f, axis=0)) for offset in range(KERNEL)])
    d_conv_pad = jnp.pad(d_conv_f, ((margin, margin), (0, 0)))
    d_gating = jnp.zeros((FRAMES, HALF), jnp.float32)
    for offset in range(KERNEL):
        d_gating = d_gating + conv_kernel[offset] * d_conv_pad[2 * margin - offset:2 * margin - offset + FRAMES]
    d_gate_half = norm_back(jnp.where(valid_rows, d_gating, 0.0), gate_unit, gate_inv)
    d_upper = (jnp.concatenate([d_resid, d_gate_half], axis=1) * gelu_slope(upper)).astype(jnp.bfloat16)
    g_up = jnp.dot(normed.T, d_upper, preferred_element_type=jnp.float32)
    d_normed = jnp.dot(d_upper, w_up.T, preferred_element_type=jnp.float32)
    g_out = jnp.dot(context.T, cotangent, preferred_element_type=jnp.float32)
    d_context = jnp.dot(cotangent, w_out.T, preferred_element_type=jnp.float32).astype(jnp.bfloat16)
    d_context_blocks = d_context.reshape(block_count, SLICE, INNER)

    def backward_block(block_index):
        query_block, window, query_pos, key_pos = pieces(block_index)
        soft_weights = band_forward(query_block, window, query_pos, key_pos, length)[0]
        return band_backward(query_block, window, soft_weights, d_context_blocks[block_index])
    d_query, d_window = lax.map(backward_block, blocks)
    d_query = d_query.reshape(FRAMES, INNER)
    d_window = d_window.reshape(block_count, 2 * REACH + 1, SLICE, 2 * INNER)
    padded = jnp.pad(d_window, ((REACH, REACH), (0, 0), (0, 0), (0, 0)))
    d_keyval = jnp.zeros((block_count, SLICE, 2 * INNER), jnp.float32)
    for slot in range(2 * REACH + 1):
        d_keyval = d_keyval + padded[2 * REACH - slot:2 * REACH - slot + block_count, slot]
    d_joined = jnp.concatenate([d_query, d_keyval.reshape(FRAMES, 2 * INNER)], axis=1).astype(jnp.bfloat16)
    g_qkv = jnp.dot(normed.T, d_joined, preferred_element_type=jnp.float32)
    d_normed = d_normed + jnp.dot(d_joined, w_qkv.T, preferred_element_type=jnp.float32)
    d_frames = (cotangent.astype(jnp.float32) + norm_back(d_normed, unit_rows, unit_inv)).astype(jnp.bfloat16)
    return (layer_out, d_frames, g_qkv, g_out, g_up, g_down, g_kernel)

def reference(frames, cotangent, lengths, w_qkv, w_out, w_up, w_down, conv_kernel):

    def one_record(inputs):
        return record(inputs[0], inputs[1], inputs[2], w_qkv, w_out, w_up, w_down, conv_kernel)
    results = lax.map(one_record, (frames, cotangent, lengths))
    return (results[0], results[1], lax.optimization_barrier(jnp.sum(results[2], axis=0)), lax.optimization_barrier(jnp.sum(results[3], axis=0)), lax.optimization_barrier(jnp.sum(results[4], axis=0)), lax.optimization_barrier(jnp.sum(results[5], axis=0)), lax.optimization_barrier(jnp.sum(results[6], axis=0)))
```

```python
import jax
import jax.numpy as jnp
from jax import lax
from jax.experimental import pallas as pl
from jax.experimental.pallas import tpu as pltpu
from jax.sharding import PartitionSpec as P

HEAD = 64
BAND = 512
ROWS = 128
GROUP = 4
WINDOW = 2 * BAND + ROWS
MARGIN = 15
TAPS = 31

EPSILON = 1e-05
NEG_LARGE = -1e30
HALF_ROOT = 0.7071067811865476
NORMAL_PEAK = 0.3989422804014327

BF16 = jnp.bfloat16
F32 = jnp.float32
VMEM_LIMIT = 50 * 2**20

X_GROUPS = [[4 * g + x for x in range(4)] for g in range(8)]
Z_GROUPS = [[0, 2, 4, 6], [1, 3, 5, 7]]


def call(body, outs, scratch=(), scalars=0):
    def run(*args):
        specs = [pl.BlockSpec(memory_space=pltpu.SMEM)] * scalars
        specs += [pl.BlockSpec(memory_space=pltpu.VMEM)] * (len(args) - scalars)
        return pl.pallas_call(
            body,
            out_shape=[jax.ShapeDtypeStruct(shape, dtype) for shape, dtype in outs],
            in_specs=specs,
            out_specs=[pl.BlockSpec(memory_space=pltpu.VMEM)] * len(outs),
            scratch_shapes=list(scratch),
            compiler_params=pltpu.CompilerParams(vmem_limit_bytes=VMEM_LIMIT),
        )(*args)

    return run


def dot(left, right, left_dim=1, right_dim=0):
    return lax.dot_general(
        left, right, (((left_dim,), (right_dim,)), ((), ())), preferred_element_type=F32
    )


def normalize(values):
    centred = values - jnp.mean(values, axis=-1, keepdims=True)
    inverse = lax.rsqrt(jnp.mean(centred * centred, axis=-1, keepdims=True) + EPSILON)
    return (centred * inverse, inverse)


def norm_back(gradient, unit_rows, inverse):
    return inverse * (
        gradient
        - jnp.mean(gradient, axis=-1, keepdims=True)
        - unit_rows * jnp.mean(gradient * unit_rows, axis=-1, keepdims=True)
    )


def project_kernel(frames, cotangent, w_qkv, w_out, normed, cot_t, kv, qd):
    unit_rows, _ = normalize(frames[...].astype(F32))
    unit = unit_rows.astype(BF16)
    normed[...] = unit
    joined = dot(unit, w_qkv[...]).astype(BF16)
    d_context = dot(cotangent[...], w_out[...], 1, 1).astype(BF16)
    for pair in range(4):
        lanes = slice(128 * pair, 128 * pair + 128)
        kv[pair, :, :128] = joined[:, 512 + 128 * pair : 640 + 128 * pair]
        kv[pair, :, 128:] = joined[:, 1024 + 128 * pair : 1152 + 128 * pair]
        qd[pair, :, :128] = joined[:, lanes]
        qd[pair, :, 128:] = d_context[:, lanes]
    cot_t[...] = cotangent[...].T


def gate_kernel(
    place, normed, cotangent, w_up, w_down, resid, d_gated, gating, d_conv, unit, inverse, slope, top, bottom
):
    first_frame, length = place[0], place[1]
    upper = dot(normed[...], w_up[...])
    phi = 0.5 * (1.0 + lax.erf(upper * HALF_ROOT))
    slope[...] = phi + upper * jnp.exp(-0.5 * upper * upper) * NORMAL_PEAK
    hidden = (upper * phi).astype(BF16)
    gate_unit, gate_inv = normalize(hidden[:, 1024:].astype(F32))
    unit[...] = gate_unit
    inverse[...] = jnp.broadcast_to(gate_inv, inverse.shape)
    rows = first_frame + lax.broadcasted_iota(jnp.int32, (ROWS, 1024), 0)
    masked = jnp.where(rows < length, gate_unit, 0.0).astype(BF16)
    gating[...] = masked
    resid[...] = hidden[:, :1024]
    back = dot(cotangent[...], w_down[...], 1, 1).astype(BF16)
    d_gated[...] = back
    conv_back = (back.astype(F32) * hidden[:, :1024].astype(F32)).astype(BF16)
    d_conv[...] = conv_back
    top[:, :1024] = masked[:16]
    top[:, 1024:] = conv_back[:16]
    bottom[:, :1024] = masked[112:]
    bottom[:, 1024:] = conv_back[112:]


def conv_kernel_body(
    place, resid, d_gated, gating, d_conv, unit, inverse, slope, before, after, taps,
    gated, d_upper, d_upper_t, g_taps, gate_ext, conv_ext, conv_out, d_gating
):
    first_frame, length = place[0], place[1]
    gate_ext[:16] = before[:, :1024].astype(F32)
    gate_ext[16:144] = gating[...].astype(F32)
    gate_ext[144:] = after[:, :1024].astype(F32)
    conv_ext[:16] = before[:, 1024:].astype(F32)
    conv_ext[16:144] = d_conv[...].astype(F32)
    conv_ext[144:] = after[:, 1024:].astype(F32)
    g_taps[...] = jnp.zeros_like(g_taps)

    def chunk(index, _):
        lanes = pl.ds(pl.multiple_of(index * 128, 128), 128)
        own = conv_ext[16:144, lanes]
        forward = jnp.zeros((ROWS, 128), F32)
        for shift in range(8):
            moved = gate_ext[pl.ds(shift, 152), lanes]
            for step in range(4):
                offset = 8 * step + shift
                if 1 <= offset <= TAPS:
                    part = moved[8 * step : 8 * step + ROWS]
                    forward = forward + taps[offset - 1 : offset, lanes] * part
                    g_taps[offset - 1 : offset, lanes] = jnp.sum(part * own, axis=0, keepdims=True)
        conv_out[:, lanes] = forward
        backward = jnp.zeros((ROWS, 128), F32)
        for shift in range(8):
            moved = conv_ext[pl.ds(shift, 152), lanes]
            for step in range(4):
                offset = 8 * step + shift
                if 1 <= offset <= TAPS:
                    part = moved[8 * step : 8 * step + ROWS]
                    backward = backward + taps[TAPS - offset : TAPS - offset + 1, lanes] * part
        d_gating[:, lanes] = backward
        return 0

    lax.fori_loop(0, 8, chunk, 0)
    conv = conv_out[...]
    gated[...] = (resid[...].astype(F32) * conv).astype(BF16)
    rows = first_frame + lax.broadcasted_iota(jnp.int32, (ROWS, 1024), 0)
    d_gate = jnp.where(rows < length, d_gating[...], 0.0)
    d_gate = norm_back(d_gate, unit[...], inverse[:, :1])
    left = (d_gated[...].astype(F32) * conv * slope[:, :1024]).astype(BF16)
    right = (d_gate * slope[:, 1024:]).astype(BF16)
    d_upper[:, :1024] = left
    d_upper[:, 1024:] = right
    d_upper_t[:1024] = left.T
    d_upper_t[1024:] = right.T


def own_columns(array, core, width):
    parts = [
        array[:, pl.ds(pl.multiple_of(2 * width * z + width * core, width), width)] for z in range(4)
    ]
    return jnp.concatenate(parts, axis=1)


def gate_grads_kernel(
    place, normed, normed_far, gated, gated_far, d_upper_t, d_upper_far, cot_t, cot_far, taps, taps_far, out
):
    core = place[2]
    unit = jnp.concatenate([own_columns(normed, core, 128), own_columns(normed_far, core, 128)], axis=0)
    half = jnp.concatenate([own_columns(gated, core, 128), own_columns(gated_far, core, 128)], axis=0)
    up = dot(jnp.concatenate([d_upper_t[...], d_upper_far[...]], axis=1), unit)
    out[:, :64, :] = up.astype(BF16).reshape(32, 64, 512)
    down = dot(jnp.concatenate([cot_t[...], cot_far[...]], axis=1), half)
    out[:, 64:96, :] = down.astype(BF16).reshape(32, 32, 512)
    total = taps[...] + taps_far[...]
    wide = jnp.concatenate([total, jnp.zeros((96, 1024), F32)], axis=0).T.reshape(32, 32, 128)
    packed = wide[:, :16, :] + pltpu.roll(wide[:, 16:, :], 32, 2)
    packed = packed.astype(BF16)
    for z in range(4):
        out[:, 96:, 128 * z : 128 * z + 128] = packed


def attend_kernel(
    place, qd, kv, before, after, context_dq, d_before, d_after, d_own,
    key, value, key_t, value_t, scores, weights, d_scores, d_key, d_value
):
    group_first, length = place[3], place[1]
    for part, ref in enumerate((before, kv, after)):
        for piece in range(GROUP):
            start = 512 * part + ROWS * piece
            key_block = ref[piece, :, :128]
            value_block = ref[piece, :, 128:]
            key[start : start + ROWS] = key_block
            value[start : start + ROWS] = value_block
            key_t[:, start : start + ROWS] = key_block.T
            value_t[:, start : start + ROWS] = value_block.T
    d_key[...] = jnp.zeros_like(d_key)
    d_value[...] = jnp.zeros_like(d_value)
    lane = lax.broadcasted_iota(jnp.int32, (ROWS, 128), 1)
    first_head = lane < HEAD
    query_index = lax.broadcasted_iota(jnp.int32, (1, 256), 1)
    query_index = jnp.where(query_index < ROWS, query_index, query_index - ROWS)
    chunks = WINDOW // 128
    for block in range(GROUP):
        base = ROWS * block
        low = jnp.maximum(query_index, 512 - group_first - base)
        high = jnp.minimum(query_index + 1024, length - group_first + 511 - base)
        query = qd[block, :, :128].astype(F32) * 0.125
        d_context = qd[block, :, 128:].astype(F32)
        zero = jnp.zeros_like(query)
        query_pair = jnp.concatenate(
            [jnp.where(first_head, query, zero), jnp.where(first_head, zero, query)], axis=0
        ).astype(BF16)
        d_pair = jnp.concatenate(
            [jnp.where(first_head, d_context, zero), jnp.where(first_head, zero, d_context)], axis=0
        ).astype(BF16)

        def allowed_of(index):
            position = 128 * index + lax.broadcasted_iota(jnp.int32, (128, 256), 0)
            return (position >= low) & (position <= high)

        peak = jnp.full((128, 256), NEG_LARGE, F32)
        for index in range(chunks):
            part = dot(key[base + 128 * index : base + 128 * index + 128], query_pair, 1, 1)
            part = jnp.where(allowed_of(index), part, NEG_LARGE)
            scores[128 * index : 128 * index + 128] = part
            peak = jnp.maximum(peak, part)
        peak = jnp.max(peak, axis=0, keepdims=True)
        total = jnp.zeros((128, 256), F32)
        for index in range(chunks):
            part = scores[128 * index : 128 * index + 128]
            part = jnp.where(allowed_of(index), jnp.exp(part - peak), 0.0)
            scores[128 * index : 128 * index + 128] = part
            total = total + part
        scale = 1.0 / jnp.maximum(jnp.sum(total, axis=0, keepdims=True), 1.0)
        for index in range(chunks):
            part = scores[128 * index : 128 * index + 128] * scale
            weights[128 * index : 128 * index + 128] = part.astype(BF16)
        wide = dot(value_t[:, base : base + WINDOW], weights[...])
        context_t = jnp.concatenate([wide[:HEAD, :128], wide[HEAD:, 128:]], axis=0)
        context_dq[block, :, :128] = context_t.T.astype(BF16)
        product = context_t * d_context.T
        row_dot = jnp.concatenate(
            [
                jnp.sum(product[:HEAD], axis=0, keepdims=True),
                jnp.sum(product[HEAD:], axis=0, keepdims=True),
            ],
            axis=1,
        )
        for index in range(chunks):
            part = dot(value[base + 128 * index : base + 128 * index + 128], d_pair, 1, 1)
            part = weights[128 * index : 128 * index + 128].astype(F32) * (part - row_dot)
            d_scores[128 * index : 128 * index + 128] = part.astype(BF16)
        wide = dot(key_t[:, base : base + WINDOW], d_scores[...])
        d_query_t = jnp.concatenate([wide[:HEAD, :128], wide[HEAD:, 128:]], axis=0)
        context_dq[block, :, 128:] = (d_query_t.T * 0.125).astype(BF16)
        d_key[base : base + WINDOW] += dot(d_scores[...], query_pair)
        d_value[base : base + WINDOW] += dot(weights[...], d_pair)
    for piece in range(GROUP):
        for part, ref in enumerate((d_before, d_own, d_after)):
            start = 512 * part + ROWS * piece
            ref[piece, :, :128] = d_key[start : start + ROWS].astype(ref.dtype)
            ref[piece, :, 128:] = d_value[start : start + ROWS].astype(ref.dtype)


def join_kernel(own, from_before, from_after, out):
    out[...] = (own[...] + from_before[...].astype(F32) + from_after[...].astype(F32)).astype(BF16)


def gather_kernel(context_dq, d_kv, joined, joined_t, context):
    for pair in range(4):
        lanes = slice(128 * pair, 128 * pair + 128)
        context[:, lanes] = context_dq[pair, :, :128]
        joined[:, lanes] = context_dq[pair, :, 128:]
        joined[:, 512 + 128 * pair : 640 + 128 * pair] = d_kv[pair, :, :128]
        joined[:, 1024 + 128 * pair : 1152 + 128 * pair] = d_kv[pair, :, 128:]
    joined_t[...] = joined[...].T


def attention_grads_kernel(
    place, normed, normed_far, context, context_far, joined_t, joined_far, cot_t, cot_far, out
):
    core = place[2]
    unit = jnp.concatenate([own_columns(normed, core, 128), own_columns(normed_far, core, 128)], axis=0)
    grad = dot(jnp.concatenate([joined_t[...], joined_far[...]], axis=1), unit)
    out[:, :48, :] = grad.astype(BF16).reshape(32, 48, 512)
    both = jnp.concatenate([context[...], context_far[...]], axis=0).astype(F32)
    lane = lax.broadcasted_iota(jnp.int32, (2 * ROWS, 128), 1)
    keep = (lane < HEAD) == (core == 0)
    parts = []
    for z in range(4):
        block = both[:, 128 * z : 128 * z + 128]
        parts.append(jnp.where(keep, block, pltpu.roll(block, HEAD, 1)))
    doubled = jnp.concatenate(parts, axis=1).astype(BF16)
    grad = dot(jnp.concatenate([cot_t[...], cot_far[...]], axis=1), doubled).reshape(32, 32, 512)
    lane = lax.broadcasted_iota(jnp.int32, (32, 16, 512), 2)
    out[:, 48:, :] = jnp.where((lane & 127) < HEAD, grad[:, :16], grad[:, 16:]).astype(BF16)


def rows_kernel(
    frames, cotangent, context, gated, d_upper, joined, w_qkv, w_out, w_up, w_down, layer_out, d_frames
):
    values = frames[...].astype(F32)
    out = values + dot(context[...], w_out[...]) + dot(gated[...], w_down[...])
    layer_out[...] = out.astype(BF16)
    unit_rows, inverse = normalize(values)
    d_normed = dot(d_upper[...], w_up[...], 1, 1) + dot(joined[...], w_qkv[...], 1, 1)
    d_frames[...] = (cotangent[...].astype(F32) + norm_back(d_normed, unit_rows, inverse)).astype(BF16)


def chunk_sum_kernel(parts, out):
    total = parts[0].astype(F32)
    for index in range(1, parts.shape[0]):
        total = total + parts[index].astype(F32)
    for z in range(4):
        out[z] = total[:, 128 * z : 128 * z + 128].astype(BF16)


def gate_final_kernel(parts, g_up, g_down, g_taps):
    total = parts[0].astype(F32)
    for index in range(1, 4):
        total = total + parts[index].astype(F32)
    turned = total.T
    g_up[...] = turned[:, :64]
    g_down[...] = turned[:, 64:96]
    g_taps[...] = jnp.concatenate([turned[:TAPS, 96:], turned[32 : 32 + TAPS, 96:]], axis=1)


def attention_final_kernel(parts, g_qkv, g_out):
    total = parts[0].astype(F32)
    for index in range(1, 4):
        total = total + parts[index].astype(F32)
    turned = total.T
    g_qkv[...] = turned[:, :48]
    g_out[...] = jnp.concatenate([turned[:HEAD, 48:], turned[HEAD:, 48:]], axis=1)


def shift(array, by):
    return lax.ppermute(array, "seq", [(i, i + by) for i in range(32) if 0 <= i + by < 32])


def other_core(array):
    return lax.ppermute(array, "dp", [(i, i ^ 1) for i in range(8)])


def swap_x(array):
    return lax.all_to_all(array, "seq", 0, 0, axis_index_groups=X_GROUPS)


def local(frames, cotangent, lengths, w_qkv, w_out, w_up, w_down, conv_kernel):
    frames, cotangent = frames[0], cotangent[0]
    seq_index = lax.axis_index("seq")
    core = lax.axis_index("dp") % 2
    place = jnp.stack(
        [seq_index * ROWS, lengths[0], core, (seq_index // GROUP) * (GROUP * ROWS)]
    ).astype(jnp.int32)

    normed, cot_t, kv, qd = call(
        project_kernel,
        [((ROWS, 1024), BF16), ((1024, ROWS), BF16), ((4, ROWS, 256), BF16), ((4, ROWS, 256), BF16)],
    )(frames, cotangent, w_qkv, w_out)
    kv = swap_x(kv)
    qd = swap_x(qd)
    kv_before, kv_after = shift(kv, 4), shift(kv, -4)
    normed_far, cot_far = other_core(normed), other_core(cot_t)

    wide = ((ROWS, 1024), BF16)
    resid, d_gated, gating, d_conv, unit, inverse, slope, top, bottom = call(
        gate_kernel,
        [wide, wide, wide, wide, ((ROWS, 1024), F32), ((ROWS, 128), F32), ((ROWS, 2048), F32),
         ((16, 2048), BF16), ((16, 2048), BF16)],
        scalars=1,
    )(place, normed, cotangent, w_up, w_down)
    before, after = shift(bottom, 1), shift(top, -1)
    gated, d_upper, d_upper_t, g_taps = call(
        conv_kernel_body,
        [wide, ((ROWS, 2048), BF16), ((2048, ROWS), BF16), ((32, 1024), F32)],
        [pltpu.VMEM((160, 1024), F32), pltpu.VMEM((160, 1024), F32),
         pltpu.VMEM((ROWS, 1024), F32), pltpu.VMEM((ROWS, 1024), F32)],
        scalars=1,
    )(place, resid, d_gated, gating, d_conv, unit, inverse, slope, before, after, conv_kernel)
    (gate_grads,) = call(gate_grads_kernel, [((32, 112, 512), BF16)], scalars=1)(
        place, normed, normed_far, gated, other_core(gated), d_upper_t, other_core(d_upper_t),
        cot_t, cot_far, g_taps, other_core(g_taps),
    )
    gate_grads = lax.all_to_all(gate_grads, "seq", 0, 0)

    quad = (4, ROWS, 256)
    context_dq, d_before, d_after, d_own = call(
        attend_kernel,
        [(quad, BF16), (quad, BF16), (quad, BF16), (quad, F32)],
        [pltpu.VMEM((1536, 128), BF16), pltpu.VMEM((1536, 128), BF16),
         pltpu.VMEM((128, 1536), BF16), pltpu.VMEM((128, 1536), BF16),
         pltpu.VMEM((WINDOW, 256), F32), pltpu.VMEM((WINDOW, 256), BF16), pltpu.VMEM((WINDOW, 256), BF16),
         pltpu.VMEM((1536, 128), F32), pltpu.VMEM((1536, 128), F32)],
        scalars=1,
    )(place, qd, kv, kv_before, kv_after)
    context_dq = swap_x(context_dq)
    (d_kv,) = call(join_kernel, [(quad, BF16)])(d_own, shift(d_after, 4), shift(d_before, -4))
    d_kv = swap_x(d_kv)
    joined, joined_t, context = call(
        gather_kernel, [((ROWS, 1536), BF16), ((1536, ROWS), BF16), ((ROWS, 512), BF16)]
    )(context_dq, d_kv)
    (attention_grads,) = call(attention_grads_kernel, [((32, 64, 512), BF16)], scalars=1)(
        place, normed, normed_far, context, other_core(context), joined_t, other_core(joined_t), cot_t, cot_far
    )
    attention_grads = lax.all_to_all(attention_grads, "seq", 0, 0)
    layer_out, d_frames = call(rows_kernel, [wide, wide])(
        frames, cotangent, context, gated, d_upper, joined, w_qkv, w_out, w_up, w_down
    )
    (gate_grads,) = call(chunk_sum_kernel, [((4, 112, 128), BF16)])(gate_grads)
    gate_grads = lax.all_to_all(gate_grads, "dp", 0, 0, axis_index_groups=Z_GROUPS)
    g_up, g_down, g_kernel = call(
        gate_final_kernel, [((128, 64), F32), ((128, 32), F32), ((TAPS, 32), F32)]
    )(gate_grads)
    (attention_grads,) = call(chunk_sum_kernel, [((4, 64, 128), BF16)])(attention_grads)
    attention_grads = lax.all_to_all(attention_grads, "dp", 0, 0, axis_index_groups=Z_GROUPS)
    g_qkv, g_out = call(attention_final_kernel, [((128, 48), F32), ((64, 32), F32)])(attention_grads)
    return (layer_out[None], d_frames[None], g_qkv, g_out, g_up, g_down, g_kernel)


def solution(mesh):
    return jax.shard_map(
        local,
        mesh=mesh,
        in_specs=(P("dp", "seq", None), P("dp", "seq", None), P("dp"), P(), P(), P(), P(), P()),
        out_specs=(
            P("dp", "seq", None),
            P("dp", "seq", None),
            P("dp", "seq"),
            P("dp", "seq"),
            P("dp", "seq"),
            P("dp", "seq"),
            P(None, "seq"),
        ),
        check_vma=False,
    )
```

```python
import jax
import jax.numpy as jnp
from jax import lax
from jax.experimental import pallas as pl
from jax.experimental.pallas import tpu as pltpu
from jax.sharding import PartitionSpec as P

HEAD = 64
BAND = 512
ROWS = 128
GROUP = 4
WINDOW = 2 * BAND + ROWS
MARGIN = 15
TAPS = 31

EPSILON = 1e-05
NEG_LARGE = -1e30
HALF_ROOT = 0.7071067811865476
NORMAL_PEAK = 0.3989422804014327

BF16 = jnp.bfloat16
F32 = jnp.float32
HBM = pltpu.HBM
VMEM_LIMIT = 24 * 2**20

ROW_GROUPS = [[4 * m + x for m in range(8)] for x in range(4)]


def call(body, outs, scratch=(), scalars=0):
    def run(*args):
        specs = [pl.BlockSpec(memory_space=pltpu.SMEM)] * scalars
        specs += [pl.BlockSpec(memory_space=pltpu.VMEM)] * (len(args) - scalars)
        return pl.pallas_call(
            body,
            out_shape=[
                HBM(*out[:2]) if len(out) > 2 else jax.ShapeDtypeStruct(*out) for out in outs
            ],
            in_specs=specs,
            out_specs=[pl.BlockSpec(memory_space=pltpu.VMEM)] * len(outs),
            scratch_shapes=list(scratch),
            compiler_params=pltpu.CompilerParams(vmem_limit_bytes=VMEM_LIMIT),
        )(*args)

    return run


def dot(left, right, left_dim=1, right_dim=0):
    return lax.dot_general(
        left, right, (((left_dim,), (right_dim,)), ((), ())), preferred_element_type=F32
    )


def normalize(values):
    centred = values - jnp.mean(values, axis=-1, keepdims=True)
    inverse = lax.rsqrt(jnp.mean(centred * centred, axis=-1, keepdims=True) + EPSILON)
    return (centred * inverse, inverse)


def norm_back(gradient, unit_rows, inverse):
    return inverse * (
        gradient
        - jnp.mean(gradient, axis=-1, keepdims=True)
        - unit_rows * jnp.mean(gradient * unit_rows, axis=-1, keepdims=True)
    )


def slot(place, turn):
    return (place[4] + 4 - turn) & 3


def span(index, size):
    return pl.ds(pl.multiple_of(index * size, size), size)


def project_kernel(place, frames_0, frames_1, frames_2, frames_3, w_qkv, normed, query, kv):
    x = place[4]
    for turn, ref in enumerate((frames_0, frames_1, frames_2, frames_3)):
        unit_rows, _ = normalize(ref[...].astype(F32))
        normed[span(slot(place, turn), ROWS), :] = unit_rows.astype(BF16)
    weight = jnp.concatenate([w_qkv[:, span(x + 4 * part, 128)] for part in range(3)], axis=1)
    joined = dot(normed[...], weight).astype(BF16)
    query[...] = joined[:, :128].reshape(4, ROWS, 128)
    kv[...] = joined[:, 128:].reshape(4, ROWS, 256)


def gate_kernel(
    place, frames, cotangent, w_up, w_down,
    resid, d_gated, gating, d_conv, unit, inverse, slope, top, bottom
):
    first_frame, length = place[0], place[1]
    unit_rows, _ = normalize(frames[...].astype(F32))
    upper = dot(unit_rows.astype(BF16), w_up[...])
    phi = 0.5 * (1.0 + lax.erf(upper * HALF_ROOT))
    slope[...] = phi + upper * jnp.exp(-0.5 * upper * upper) * NORMAL_PEAK
    hidden = (upper * phi).astype(BF16)
    gate_unit, gate_inv = normalize(hidden[:, 1024:].astype(F32))
    unit[...] = gate_unit
    inverse[...] = jnp.broadcast_to(gate_inv, inverse.shape)
    rows = first_frame + lax.broadcasted_iota(jnp.int32, (ROWS, 1024), 0)
    masked = jnp.where(rows < length, gate_unit, 0.0).astype(BF16)
    gating[...] = masked
    resid[...] = hidden[:, :1024]
    back = dot(cotangent[...], w_down[...], 1, 1).astype(BF16)
    d_gated[...] = back
    conv_back = (back.astype(F32) * hidden[:, :1024].astype(F32)).astype(BF16)
    d_conv[...] = conv_back
    top[:, :1024] = masked[:16]
    top[:, 1024:] = conv_back[:16]
    bottom[:, :1024] = masked[112:]
    bottom[:, 1024:] = conv_back[112:]


def conv_inner_kernel(gating, d_conv, taps, conv_out, d_gating, g_taps, gate_ext, conv_ext):
    for ext, ref in ((gate_ext, gating), (conv_ext, d_conv)):
        ext[:16] = jnp.zeros((16, 1024), F32)
        ext[16:144] = ref[...].astype(F32)
        ext[144:] = jnp.zeros((16, 1024), F32)
    g_taps[...] = jnp.zeros_like(g_taps)

    def chunk(index, _):
        lanes = pl.ds(pl.multiple_of(index * 128, 128), 128)
        own = conv_ext[16:144, lanes]
        forward = jnp.zeros((ROWS, 128), F32)
        for shift in range(8):
            moved = gate_ext[pl.ds(shift, 152), lanes]
            for step in range(4):
                offset = 8 * step + shift
                if 1 <= offset <= TAPS:
                    part = moved[8 * step : 8 * step + ROWS]
                    forward = forward + taps[offset - 1 : offset, lanes] * part
                    g_taps[offset - 1 : offset, lanes] = jnp.sum(part * own, axis=0, keepdims=True)
        conv_out[:, lanes] = forward
        backward = jnp.zeros((ROWS, 128), F32)
        for shift in range(8):
            moved = conv_ext[pl.ds(shift, 152), lanes]
            for step in range(4):
                offset = 8 * step + shift
                if 1 <= offset <= TAPS:
                    part = moved[8 * step : 8 * step + ROWS]
                    backward = backward + taps[TAPS - offset : TAPS - offset + 1, lanes] * part
        d_gating[:, lanes] = backward
        return 0

    lax.fori_loop(0, 8, chunk, 0)


def conv_outer_kernel(
    place, conv_in, d_gating_in, g_taps_in, d_conv, resid, d_gated, unit, inverse, slope, before, after, taps,
    d_upper, out_0, out_1, out_2, out_3, conv_out, d_gating, before_ext, after_ext, g_taps, d_upper_t, g_taps_t
):
    first_frame, length = place[0], place[1]
    conv_out[...] = conv_in[...]
    d_gating[...] = d_gating_in[...]
    g_taps[...] = g_taps_in[...]
    before_ext[:16] = before[...].astype(F32)
    before_ext[16:] = jnp.zeros((16, 2048), F32)
    after_ext[:16] = jnp.zeros((16, 2048), F32)
    after_ext[16:] = after[...].astype(F32)

    def chunk(index, _):
        lanes = pl.ds(pl.multiple_of(index * 128, 128), 128)
        far = pl.ds(pl.multiple_of(index * 128 + 1024, 128), 128)
        for ext, first, skip in ((before_ext, 0, 0), (after_ext, 112, 16)):
            own = d_conv[first : first + 16, lanes].astype(F32)
            forward = conv_out[first : first + 16, lanes]
            backward = d_gating[first : first + 16, lanes]
            for step in range(1, 16):
                offset = step + skip
                part = ext[pl.ds(step, 16), lanes]
                forward = forward + taps[offset - 1 : offset, lanes] * part
                g_taps[offset - 1 : offset, lanes] += jnp.sum(part * own, axis=0, keepdims=True)
                part = ext[pl.ds(step, 16), far]
                backward = backward + taps[TAPS - offset : TAPS - offset + 1, lanes] * part
            conv_out[first : first + 16, lanes] = forward
            d_gating[first : first + 16, lanes] = backward
        return 0

    lax.fori_loop(0, 8, chunk, 0)
    conv = conv_out[...]
    gated = (resid[...].astype(F32) * conv).astype(BF16)
    rows = first_frame + lax.broadcasted_iota(jnp.int32, (ROWS, 1024), 0)
    d_gate = jnp.where(rows < length, d_gating[...], 0.0)
    d_gate = norm_back(d_gate, unit[...], inverse[:, :1])
    left = (d_gated[...].astype(F32) * conv * slope[:, :1024]).astype(BF16)
    right = (d_gate * slope[:, 1024:]).astype(BF16)
    d_upper[:, :1024] = left
    d_upper[:, 1024:] = right
    d_upper_t[:1024] = left.T
    d_upper_t[1024:] = right.T
    turned = jnp.concatenate([g_taps[...], jnp.zeros((96, 1024), F32)], axis=0).T.reshape(32, 32, 128)
    g_taps_t[...] = (turned[:, :16, :] + pltpu.roll(turned[:, 16:, :], 32, 2)).astype(BF16)
    for turn, ref in enumerate((out_0, out_1, out_2, out_3)):
        x = (place[4] + turn) & 3
        for m in range(8):
            ref[64 * m : 64 * m + 64] = d_upper_t[span(4 * m + x, 64), :]
            ref[512 + 16 * m : 528 + 16 * m] = g_taps_t[4 * m + x]
            ref[640 + 128 * m : 768 + 128 * m] = gated[:, 128 * m : 128 * m + 128]


def own_columns(array, core, width):
    parts = [
        array[:, pl.ds(pl.multiple_of(2 * width * z + width * core, width), width)] for z in range(4)
    ]
    return jnp.concatenate(parts, axis=1)


def gate_grads_kernel(
    place, normed, cot_0, cot_1, cot_2, cot_3, gate_0, gate_1, gate_2, gate_3,
    keep, send, cot_own, d_upper_t, gated, cot_t
):
    x, core = place[4], place[2]
    gates = (gate_0, gate_1, gate_2, gate_3)
    g_taps = gate_0[512:640].astype(F32)
    for ref in gates[1:]:
        g_taps = g_taps + ref[512:640].astype(F32)
    g_taps = g_taps.astype(BF16).reshape(8, 16, 128)
    for turn, (gate, cot) in enumerate(zip(gates, (cot_0, cot_1, cot_2, cot_3))):
        here = span(slot(place, turn), 128)
        d_upper_t[:, here] = gate[:512]
        for block in range(8):
            gated[here, 128 * block : 128 * block + 128] = gate[640 + 128 * block : 768 + 128 * block]
        cot_t[:, here] = cot[...].T
    for m in range(8):
        cot_own[32 * m : 32 * m + 32] = cot_t[span(4 * m + x, 32), :]
    for parity, out in ((core, keep), (1 - core, send)):
        grad = dot(d_upper_t[...], own_columns(normed, parity, 128))
        out[:, :64, :] = grad.astype(BF16).reshape(8, 64, 512)
        grad = dot(cot_own[...], own_columns(gated, parity, 128))
        out[:, 64:96, :] = grad.astype(BF16).reshape(8, 32, 512)
        for z in range(4):
            out[:, 96:, 128 * z : 128 * z + 128] = g_taps


def attention_grads_kernel(
    place, normed, cot_own, near_0, near_1, near_2, near_3, far_0, far_1, far_2, far_3,
    keep, send, context_own, joined_own, joined_t, context, rows_t
):
    x, core = place[4], place[2]
    nears, fars = (near_0, near_1, near_2, near_3), (far_0, far_1, far_2, far_3)
    for turn, (near, far) in enumerate(zip(nears, fars)):
        pair = slot(place, turn)
        for block in range(GROUP):
            tokens = slice(128 * block, 128 * block + 128)
            context[tokens, span(pair, 128)] = near[block, :, :128]
            joined_t[span(pair, 128), tokens] = near[block, :, 128:]
            joined_t[span(pair + 4, 128), tokens] = far[block, :, :128]
            joined_t[span(pair + 8, 128), tokens] = far[block, :, 128:]
    for m in range(8):
        rows_t[48 * m : 48 * m + 48] = joined_t[span(4 * m + x, 48), :]
    context_own[...] = context[span(x, ROWS), :]
    joined_own[...] = joined_t[:, span(x, ROWS)]
    lane = lax.broadcasted_iota(jnp.int32, (512, 128), 1)
    blocks, swapped = [], []
    for z in range(4):
        block = context[:, 128 * z : 128 * z + 128].astype(F32)
        blocks.append(block)
        swapped.append(pltpu.roll(block, HEAD, 1))
    lane_out = lax.broadcasted_iota(jnp.int32, (8, 16, 512), 2)
    for parity, out in ((core, keep), (1 - core, send)):
        grad = dot(rows_t[...], own_columns(normed, parity, 128))
        out[:, :48, :] = grad.astype(BF16).reshape(8, 48, 512)
        mine = (lane < HEAD) == (parity == 0)
        doubled = jnp.concatenate(
            [jnp.where(mine, block, other) for block, other in zip(blocks, swapped)], axis=1
        ).astype(BF16)
        grad = dot(cot_own[...], doubled).reshape(8, 32, 512)
        out[:, 48:, :] = jnp.where((lane_out & 127) < HEAD, grad[:, :16], grad[:, 16:]).astype(BF16)


def attend_kernel(
    place, queries, kv, before, after, cot_0, cot_1, cot_2, cot_3, w_out, context_dq, d_before, d_after, d_own,
    d_contexts, key, value, key_t, value_t, scores, weights, d_scores, d_key, d_value
):
    group_first, length = place[3], place[1]
    w_pair = w_out[span(place[4], 128), :]
    for turn, ref in enumerate((cot_0, cot_1, cot_2, cot_3)):
        d_contexts[slot(place, turn)] = dot(ref[...], w_pair, 1, 1).astype(BF16)
    for part, ref in enumerate((before, kv, after)):
        for piece in range(GROUP):
            start = 512 * part + ROWS * piece
            key_block = ref[piece, :, :128]
            value_block = ref[piece, :, 128:]
            key[start : start + ROWS] = key_block
            value[start : start + ROWS] = value_block
            key_t[:, start : start + ROWS] = key_block.T
            value_t[:, start : start + ROWS] = value_block.T
    d_key[...] = jnp.zeros_like(d_key)
    d_value[...] = jnp.zeros_like(d_value)
    lane = lax.broadcasted_iota(jnp.int32, (ROWS, 128), 1)
    first_head = lane < HEAD
    query_index = lax.broadcasted_iota(jnp.int32, (1, 256), 1)
    query_index = jnp.where(query_index < ROWS, query_index, query_index - ROWS)
    chunks = WINDOW // 128
    for block in range(GROUP):
        base = ROWS * block
        low = jnp.maximum(query_index, 512 - group_first - base)
        high = jnp.minimum(query_index + 1024, length - group_first + 511 - base)
        query = queries[block].astype(F32) * 0.125
        d_context = d_contexts[block].astype(F32)
        zero = jnp.zeros_like(query)
        query_pair = jnp.concatenate(
            [jnp.where(first_head, query, zero), jnp.where(first_head, zero, query)], axis=0
        ).astype(BF16)
        d_pair = jnp.concatenate(
            [jnp.where(first_head, d_context, zero), jnp.where(first_head, zero, d_context)], axis=0
        ).astype(BF16)

        def allowed_of(index):
            position = 128 * index + lax.broadcasted_iota(jnp.int32, (128, 256), 0)
            return (position >= low) & (position <= high)

        peak = jnp.full((128, 256), NEG_LARGE, F32)
        for index in range(chunks):
            part = dot(key[base + 128 * index : base + 128 * index + 128], query_pair, 1, 1)
            part = jnp.where(allowed_of(index), part, NEG_LARGE)
            scores[128 * index : 128 * index + 128] = part
            peak = jnp.maximum(peak, part)
        peak = jnp.max(peak, axis=0, keepdims=True)
        total = jnp.zeros((128, 256), F32)
        for index in range(chunks):
            part = scores[128 * index : 128 * index + 128]
            part = jnp.where(allowed_of(index), jnp.exp(part - peak), 0.0)
            scores[128 * index : 128 * index + 128] = part
            total = total + part
        scale = 1.0 / jnp.maximum(jnp.sum(total, axis=0, keepdims=True), 1.0)
        for index in range(chunks):
            part = scores[128 * index : 128 * index + 128] * scale
            weights[128 * index : 128 * index + 128] = part.astype(BF16)
        wide = dot(value_t[:, base : base + WINDOW], weights[...])
        context_t = jnp.concatenate([wide[:HEAD, :128], wide[HEAD:, 128:]], axis=0)
        context_dq[block, :, :128] = context_t.T.astype(BF16)
        product = context_t * d_context.T
        row_dot = jnp.concatenate(
            [
                jnp.sum(product[:HEAD], axis=0, keepdims=True),
                jnp.sum(product[HEAD:], axis=0, keepdims=True),
            ],
            axis=1,
        )
        for index in range(chunks):
            part = dot(value[base + 128 * index : base + 128 * index + 128], d_pair, 1, 1)
            part = weights[128 * index : 128 * index + 128].astype(F32) * (part - row_dot)
            d_scores[128 * index : 128 * index + 128] = part.astype(BF16)
        wide = dot(key_t[:, base : base + WINDOW], d_scores[...])
        d_query_t = jnp.concatenate([wide[:HEAD, :128], wide[HEAD:, 128:]], axis=0)
        context_dq[block, :, 128:] = (d_query_t * 0.125).astype(BF16)
        d_key[base : base + WINDOW] += dot(d_scores[...], query_pair)
        d_value[base : base + WINDOW] += dot(weights[...], d_pair)
    for piece in range(GROUP):
        for part, ref in enumerate((d_before, d_own, d_after)):
            start = 512 * part + ROWS * piece
            ref[piece, :, :128] = d_key[start : start + ROWS].astype(ref.dtype)
            ref[piece, :, 128:] = d_value[start : start + ROWS].astype(ref.dtype)


def join_kernel(own, from_before, from_after, out):
    for piece in range(GROUP):
        total = own[piece] + from_before[piece].astype(F32) + from_after[piece].astype(F32)
        total = total.astype(BF16)
        out[piece, :, :128] = total[:, :128].T
        out[piece, :, 128:] = total[:, 128:].T


def rows_kernel(
    frames, cotangent, context, gate, d_upper, joined_t, w_qkv, w_out, w_up, w_down, layer_out, d_frames
):
    gated = jnp.concatenate([gate[640 + 128 * m : 768 + 128 * m] for m in range(8)], axis=1)
    values = frames[...].astype(F32)
    out = values + dot(context[...], w_out[...]) + dot(gated, w_down[...])
    layer_out[...] = out.astype(BF16)
    unit_rows, inverse = normalize(values)
    d_normed = dot(d_upper[...], w_up[...], 1, 1) + dot(joined_t[...].T, w_qkv[...], 1, 1)
    d_frames[...] = (cotangent[...].astype(F32) + norm_back(d_normed, unit_rows, inverse)).astype(BF16)


def add_kernel(near, far, out):
    out[...] = (near[...].astype(F32) + far[...].astype(F32)).astype(BF16)


def chunk_sum_kernel(place, gate_parts, attention_parts, out_0, out_1, out_2, out_3, total):
    for parts, start in ((gate_parts, 0), (attention_parts, 112)):
        for first in range(0, parts.shape[1], 16):
            rows = slice(first, first + 16)
            acc = parts[0, rows, :].astype(F32)
            for source in range(1, 8):
                acc = acc + parts[source, rows, :].astype(F32)
            for z in range(4):
                total[z, start + first : start + first + 16, :] = acc[:, 128 * z : 128 * z + 128].astype(BF16)
    for turn, ref in enumerate((out_0, out_1, out_2, out_3)):
        ref[...] = total[(place[5] + turn) & 3]


def final_kernel(place, part_0, part_1, part_2, part_3, g_qkv_t, g_out_t, g_up_t, g_down_t, g_taps, ordered):
    for turn, ref in enumerate((part_0, part_1, part_2, part_3)):
        ordered[(place[5] + 4 - turn) & 3] = ref[...].astype(F32)
    total = (ordered[0] + ordered[1]) + (ordered[2] + ordered[3])
    g_up_t[...] = total[:64]
    g_down_t[...] = total[64:96]
    turned = total[96:112].T
    g_taps[...] = jnp.concatenate([turned[:TAPS], turned[32 : 32 + TAPS]], axis=1)
    g_qkv_t[...] = total[112:160]
    g_out_t[:16] = total[160:, :HEAD]
    g_out_t[16:] = total[160:, HEAD:]


def shift(array, by):
    return lax.ppermute(array, "seq", [(i, i + by) for i in range(32) if 0 <= i + by < 32])


def other_core(array):
    return lax.ppermute(array, "dp", [(i, i ^ 1) for i in range(8)])


def swap_rows(array):
    return lax.all_to_all(array, "seq", 0, 0, axis_index_groups=ROW_GROUPS)


def turn_x(pieces):
    return [pieces[0]] + [
        lax.ppermute(pieces[by], "seq", [(i, i // 4 * 4 + (i + by) % 4) for i in range(32)])
        for by in range(1, 4)
    ]


def turn_z(pieces):
    return [pieces[0]] + [
        lax.ppermute(pieces[by], "dp", [(i, (i + 2 * by) % 8) for i in range(8)]) for by in range(1, 4)
    ]


def local(frames, cotangent, lengths, w_qkv, w_out, w_up, w_down, conv_kernel):
    frames, cotangent = frames[0], cotangent[0]
    seq_index = lax.axis_index("seq")
    dp_index = lax.axis_index("dp")
    place = jnp.stack(
        [seq_index * ROWS, lengths[0], dp_index & 1, (seq_index >> 2) * (GROUP * ROWS), seq_index & 3, dp_index >> 1]
    ).astype(jnp.int32)

    wide = ((ROWS, 1024), BF16)
    wide_f = ((ROWS, 1024), F32)
    quad = ((4, ROWS, 256), BF16)
    frames_x = turn_x([frames] * 4)
    resid, d_gated, gating, d_conv, unit, inverse, slope, top, bottom = call(
        gate_kernel,
        [wide + (HBM,), wide + (HBM,), wide, wide, wide_f + (HBM,), ((ROWS, 128), F32, HBM),
         ((ROWS, 2048), F32, HBM), ((16, 2048), BF16), ((16, 2048), BF16)],
        scalars=1,
    )(place, frames, cotangent, w_up, w_down)
    before, after = shift(bottom, 1), shift(top, -1)
    gating, d_conv, cot_later = lax.optimization_barrier((gating, d_conv, cotangent))
    cot_x = turn_x([cot_later] * 4)
    conv_in, d_gating_in, g_taps_in = call(
        conv_inner_kernel,
        [wide_f, wide_f, ((32, 1024), F32)],
        [pltpu.VMEM((160, 1024), F32), pltpu.VMEM((160, 1024), F32)],
    )(gating, d_conv, conv_kernel)
    normed, query, kv = call(
        project_kernel, [((512, 1024), BF16), ((4, ROWS, 128), BF16), quad], scalars=1
    )(place, *frames_x, w_qkv)
    conv_in, normed, kv = lax.optimization_barrier((conv_in, normed, kv))
    kv_before, kv_after = shift(kv, 4), shift(kv, -4)
    gate = ((1664, 128), BF16)
    d_upper, *gate_x = call(
        conv_outer_kernel,
        [((ROWS, 2048), BF16, HBM), gate, gate, gate, gate],
        [pltpu.VMEM((ROWS, 1024), F32), pltpu.VMEM((ROWS, 1024), F32),
         pltpu.VMEM((32, 2048), F32), pltpu.VMEM((32, 2048), F32),
         pltpu.VMEM((32, 1024), F32), pltpu.VMEM((2048, ROWS), BF16), pltpu.VMEM((32, 16, 128), BF16)],
        scalars=1,
    )(place, conv_in, d_gating_in, g_taps_in, d_conv, resid, d_gated, unit, inverse, slope, before, after, conv_kernel)
    query, d_upper, *gate_x = lax.optimization_barrier((query, d_upper, *gate_x))
    gate_x = turn_x(gate_x)
    near, d_before, d_after, d_own = call(
        attend_kernel,
        [quad, quad, quad, ((4, ROWS, 256), F32)],
        [pltpu.VMEM((4, ROWS, 128), BF16),
         pltpu.VMEM((1536, 128), BF16), pltpu.VMEM((1536, 128), BF16),
         pltpu.VMEM((128, 1536), BF16), pltpu.VMEM((128, 1536), BF16),
         pltpu.VMEM((WINDOW, 256), F32), pltpu.VMEM((WINDOW, 256), BF16), pltpu.VMEM((WINDOW, 256), BF16),
         pltpu.VMEM((1536, 128), F32), pltpu.VMEM((1536, 128), F32)],
        scalars=1,
    )(place, query, kv, kv_before, kv_after, *cot_x, w_out)
    from_before, from_after = shift(d_after, 4), shift(d_before, -4)
    near_x = turn_x([near] * 4)
    keep, send, cot_own = call(
        gate_grads_kernel,
        [((8, 112, 512), BF16), ((8, 112, 512), BF16), ((256, 512), BF16)],
        [pltpu.VMEM((512, 512), BF16), pltpu.VMEM((512, 1024), BF16), pltpu.VMEM((1024, 512), BF16)],
        scalars=1,
    )(place, normed, *cot_x, *gate_x)
    (far,) = call(join_kernel, [quad])(d_own, from_before, from_after)
    far_x = turn_x([far] * 4)
    (gate_parts,) = call(add_kernel, [((8, 112, 512), BF16)])(keep, other_core(send))
    gate_parts = swap_rows(gate_parts)
    keep, send, context, joined_t = call(
        attention_grads_kernel,
        [((8, 64, 512), BF16), ((8, 64, 512), BF16), ((ROWS, 512), BF16), ((1536, ROWS), BF16)],
        [pltpu.VMEM((1536, 512), BF16), pltpu.VMEM((512, 512), BF16), pltpu.VMEM((384, 512), BF16)],
        scalars=1,
    )(place, normed, cot_own, *near_x, *far_x)
    (attention_parts,) = call(add_kernel, [((8, 64, 512), BF16)])(keep, other_core(send))
    attention_parts = swap_rows(attention_parts)
    layer_out, d_frames = call(rows_kernel, [wide, wide])(
        frames, cotangent, context, gate_x[0], d_upper, joined_t, w_qkv, w_out, w_up, w_down
    )
    parts = call(
        chunk_sum_kernel, [((176, 128), BF16)] * 4, [pltpu.VMEM((4, 176, 128), BF16)], scalars=1
    )(place, gate_parts, attention_parts)
    g_qkv, g_out, g_up, g_down, g_kernel = call(
        final_kernel,
        [((48, 128), F32), ((32, HEAD), F32), ((64, 128), F32), ((32, 128), F32), ((TAPS, 32), F32)],
        [pltpu.VMEM((4, 176, 128), F32)],
        scalars=1,
    )(place, *turn_z(parts))
    return (layer_out[None], d_frames[None], g_qkv.T, g_out.T, g_up.T, g_down.T, g_kernel)


def solution(mesh):
    return jax.shard_map(
        local,
        mesh=mesh,
        in_specs=(P("dp", "seq", None), P("dp", "seq", None), P("dp"), P(), P(), P(), P(), P()),
        out_specs=(
            P("dp", "seq", None),
            P("dp", "seq", None),
            P("dp", "seq"),
            P("dp", "seq"),
            P("dp", "seq"),
            P("dp", "seq"),
            P(None, "seq"),
        ),
        check_vma=False,
    )
```

```python
import jax
import jax.numpy as jnp
from jax import lax
from jax.experimental import pallas as pl
from jax.experimental.pallas import tpu as pltpu
from jax.sharding import PartitionSpec as P

HEAD = 64
BAND = 512
ROWS = 128
GROUP = 4
WINDOW = 2 * BAND + ROWS
MARGIN = 15
TAPS = 31

EPSILON = 1e-05
NEG_LARGE = -1e30
HALF_ROOT = 0.7071067811865476
NORMAL_PEAK = 0.3989422804014327

BF16 = jnp.bfloat16
F32 = jnp.float32
HBM = pltpu.HBM
VMEM_LIMIT = 24 * 2**20

ROW_GROUPS = [[4 * m + x for m in range(8)] for x in range(4)]


def call(body, outs, scratch=(), scalars=0):
    def run(*args):
        specs = [pl.BlockSpec(memory_space=pltpu.SMEM)] * scalars
        specs += [pl.BlockSpec(memory_space=pltpu.VMEM)] * (len(args) - scalars)
        return pl.pallas_call(
            body,
            out_shape=[
                HBM(*out[:2]) if len(out) > 2 else jax.ShapeDtypeStruct(*out) for out in outs
            ],
            in_specs=specs,
            out_specs=[pl.BlockSpec(memory_space=pltpu.VMEM)] * len(outs),
            scratch_shapes=list(scratch),
            compiler_params=pltpu.CompilerParams(vmem_limit_bytes=VMEM_LIMIT),
        )(*args)

    return run


def in_hbm(*arrays):
    return [pltpu.with_memory_space_constraint(array, HBM) for array in arrays]


def dot(left, right, left_dim=1, right_dim=0):
    return lax.dot_general(
        left, right, (((left_dim,), (right_dim,)), ((), ())), preferred_element_type=F32
    )


def normalize(values):
    centred = values - jnp.mean(values, axis=-1, keepdims=True)
    inverse = lax.rsqrt(jnp.mean(centred * centred, axis=-1, keepdims=True) + EPSILON)
    return (centred * inverse, inverse)


def norm_back(gradient, unit_rows, inverse):
    return inverse * (
        gradient
        - jnp.mean(gradient, axis=-1, keepdims=True)
        - unit_rows * jnp.mean(gradient * unit_rows, axis=-1, keepdims=True)
    )


def locate(lengths):
    seq, dp = lax.axis_index("seq"), lax.axis_index("dp")
    return (seq * ROWS, lengths[0], dp & 1, (seq >> 2) * (GROUP * ROWS), seq & 3, dp >> 1)


def slot(place, turn):
    return (place[4] + 4 - turn) & 3


def span(index, size):
    return pl.ds(pl.multiple_of(index * size, size), size)


def cotangent_kernel(lengths, cotangent, w_out, out_0, out_1, out_2, out_3, d_context, cot_t):
    place = locate(lengths)
    d_context[...] = dot(cotangent[...], w_out[...], 1, 1).astype(BF16)
    cot_t[...] = cotangent[...].T
    for turn, ref in enumerate((out_0, out_1, out_2, out_3)):
        x = (place[4] + turn) & 3
        ref[:128] = d_context[:, span(x, 128)]
        for m in range(8):
            ref[128 + 32 * m : 160 + 32 * m] = cot_t[span(4 * m + x, 32), :]


def project_kernel(lengths, frames_0, frames_1, frames_2, frames_3, w_qkv, normed, query, kv):
    place = locate(lengths)
    x = place[4]
    for turn, ref in enumerate((frames_0, frames_1, frames_2, frames_3)):
        unit_rows, _ = normalize(ref[...].astype(F32))
        normed[span(slot(place, turn), ROWS), :] = unit_rows.astype(BF16)
    weight = jnp.concatenate([w_qkv[:, span(x + 4 * part, 128)] for part in range(3)], axis=1)
    joined = dot(normed[...], weight).astype(BF16)
    query[...] = joined[:, :128].reshape(4, ROWS, 128)
    kv[...] = joined[:, 128:].reshape(4, ROWS, 256)


def gate_kernel(
    lengths, frames, cotangent, w_up, w_down,
    resid, d_gated, gating, d_conv, unit, inverse, slope, top, bottom
):
    place = locate(lengths)
    first_frame, length = place[0], place[1]
    unit_rows, _ = normalize(frames[...].astype(F32))
    upper = dot(unit_rows.astype(BF16), w_up[...])
    phi = 0.5 * (1.0 + lax.erf(upper * HALF_ROOT))
    slope[...] = phi + upper * jnp.exp(-0.5 * upper * upper) * NORMAL_PEAK
    hidden = (upper * phi).astype(BF16)
    gate_unit, gate_inv = normalize(hidden[:, 1024:].astype(F32))
    unit[...] = gate_unit
    inverse[...] = jnp.broadcast_to(gate_inv, inverse.shape)
    rows = first_frame + lax.broadcasted_iota(jnp.int32, (ROWS, 1024), 0)
    masked = jnp.where(rows < length, gate_unit, 0.0).astype(BF16)
    gating[...] = masked
    resid[...] = hidden[:, :1024]
    back = dot(cotangent[...], w_down[...], 1, 1).astype(BF16)
    d_gated[...] = back
    conv_back = (back.astype(F32) * hidden[:, :1024].astype(F32)).astype(BF16)
    d_conv[...] = conv_back
    top[:, :1024] = masked[:16]
    top[:, 1024:] = conv_back[:16]
    bottom[:, :1024] = masked[112:]
    bottom[:, 1024:] = conv_back[112:]


def conv_inner_kernel(gating, d_conv, taps, conv_out, d_gating, g_taps, gate_ext, conv_ext):
    for ext, ref in ((gate_ext, gating), (conv_ext, d_conv)):
        ext[:16] = jnp.zeros((16, 1024), F32)
        ext[16:144] = ref[...].astype(F32)
        ext[144:] = jnp.zeros((16, 1024), F32)
    g_taps[...] = jnp.zeros_like(g_taps)

    def chunk(index, _):
        lanes = pl.ds(pl.multiple_of(index * 128, 128), 128)
        own = conv_ext[16:144, lanes]
        forward = jnp.zeros((ROWS, 128), F32)
        for shift in range(8):
            moved = gate_ext[pl.ds(shift, 152), lanes]
            for step in range(4):
                offset = 8 * step + shift
                if 1 <= offset <= TAPS:
                    part = moved[8 * step : 8 * step + ROWS]
                    forward = forward + taps[offset - 1 : offset, lanes] * part
                    g_taps[offset - 1 : offset, lanes] = jnp.sum(part * own, axis=0, keepdims=True)
        conv_out[:, lanes] = forward
        backward = jnp.zeros((ROWS, 128), F32)
        for shift in range(8):
            moved = conv_ext[pl.ds(shift, 152), lanes]
            for step in range(4):
                offset = 8 * step + shift
                if 1 <= offset <= TAPS:
                    part = moved[8 * step : 8 * step + ROWS]
                    backward = backward + taps[TAPS - offset : TAPS - offset + 1, lanes] * part
        d_gating[:, lanes] = backward
        return 0

    lax.fori_loop(0, 8, chunk, 0)


def conv_outer_kernel(
    lengths, conv_in, d_gating_in, g_taps_in, d_conv, resid, d_gated, unit, inverse, slope, before, after, taps,
    d_upper, out_0, out_1, out_2, out_3, conv_out, d_gating, before_ext, after_ext, g_taps, d_upper_t, g_taps_t
):
    place = locate(lengths)
    first_frame, length = place[0], place[1]
    conv_out[...] = conv_in[...]
    d_gating[...] = d_gating_in[...]
    g_taps[...] = g_taps_in[...]
    before_ext[:16] = before[...].astype(F32)
    before_ext[16:] = jnp.zeros((16, 2048), F32)
    after_ext[:16] = jnp.zeros((16, 2048), F32)
    after_ext[16:] = after[...].astype(F32)

    def chunk(index, _):
        lanes = pl.ds(pl.multiple_of(index * 128, 128), 128)
        far = pl.ds(pl.multiple_of(index * 128 + 1024, 128), 128)
        for ext, first, skip in ((before_ext, 0, 0), (after_ext, 112, 16)):
            own = d_conv[first : first + 16, lanes].astype(F32)
            forward = conv_out[first : first + 16, lanes]
            backward = d_gating[first : first + 16, lanes]
            for step in range(1, 16):
                offset = step + skip
                part = ext[pl.ds(step, 16), lanes]
                forward = forward + taps[offset - 1 : offset, lanes] * part
                g_taps[offset - 1 : offset, lanes] += jnp.sum(part * own, axis=0, keepdims=True)
                part = ext[pl.ds(step, 16), far]
                backward = backward + taps[TAPS - offset : TAPS - offset + 1, lanes] * part
            conv_out[first : first + 16, lanes] = forward
            d_gating[first : first + 16, lanes] = backward
        return 0

    lax.fori_loop(0, 8, chunk, 0)
    conv = conv_out[...]
    gated = (resid[...].astype(F32) * conv).astype(BF16)
    rows = first_frame + lax.broadcasted_iota(jnp.int32, (ROWS, 1024), 0)
    d_gate = jnp.where(rows < length, d_gating[...], 0.0)
    d_gate = norm_back(d_gate, unit[...], inverse[:, :1])
    left = (d_gated[...].astype(F32) * conv * slope[:, :1024]).astype(BF16)
    right = (d_gate * slope[:, 1024:]).astype(BF16)
    d_upper[:, :1024] = left
    d_upper[:, 1024:] = right
    d_upper_t[:1024] = left.T
    d_upper_t[1024:] = right.T
    turned = jnp.concatenate([g_taps[...], jnp.zeros((96, 1024), F32)], axis=0).T.reshape(32, 32, 128)
    g_taps_t[...] = (turned[:, :16, :] + pltpu.roll(turned[:, 16:, :], 32, 2)).astype(BF16)
    for turn, ref in enumerate((out_0, out_1, out_2, out_3)):
        x = (place[4] + turn) & 3
        for m in range(8):
            ref[64 * m : 64 * m + 64] = d_upper_t[span(4 * m + x, 64), :]
            ref[512 + 16 * m : 528 + 16 * m] = g_taps_t[4 * m + x]
            ref[640 + 128 * m : 768 + 128 * m] = gated[:, 128 * m : 128 * m + 128]


def own_columns(array, core, width):
    parts = [
        array[:, pl.ds(pl.multiple_of(2 * width * z + width * core, width), width)] for z in range(4)
    ]
    return jnp.concatenate(parts, axis=1)


def gate_grads_kernel(
    lengths, normed, cot_0, cot_1, cot_2, cot_3, gate_0, gate_1, gate_2, gate_3,
    keep, send, cot_own, d_upper_t, gated
):
    place = locate(lengths)
    x, core = place[4], place[2]
    gates = (gate_0, gate_1, gate_2, gate_3)
    g_taps = gate_0[512:640].astype(F32)
    for ref in gates[1:]:
        g_taps = g_taps + ref[512:640].astype(F32)
    g_taps = g_taps.astype(BF16).reshape(8, 16, 128)
    for turn, (gate, cot) in enumerate(zip(gates, (cot_0, cot_1, cot_2, cot_3))):
        here = span(slot(place, turn), 128)
        d_upper_t[:, here] = gate[:512]
        for block in range(8):
            gated[here, 128 * block : 128 * block + 128] = gate[640 + 128 * block : 768 + 128 * block]
        cot_own[:, here] = cot[128:]
    for parity, out in ((core, keep), (1 - core, send)):
        grad = dot(d_upper_t[...], own_columns(normed, parity, 128))
        out[:, :64, :] = grad.astype(BF16).reshape(8, 64, 512)
        grad = dot(cot_own[...], own_columns(gated, parity, 128))
        out[:, 64:96, :] = grad.astype(BF16).reshape(8, 32, 512)
        for z in range(4):
            out[:, 96:, 128 * z : 128 * z + 128] = g_taps


def attention_grads_kernel(
    lengths, gate_keep, gate_send, normed, cot_own, near_0, near_1, near_2, near_3, far_0, far_1, far_2, far_3,
    keep, send, context, rows_t
):
    place = locate(lengths)
    core = place[2]
    for turn, near in enumerate((near_0, near_1, near_2, near_3)):
        context[:, span(slot(place, turn), 128)] = near[...].reshape(512, 128)
    for x in range(4):

        @pl.when(place[4] == x)
        def _():
            for turn, far in enumerate((far_0, far_1, far_2, far_3)):
                for index, (_, there) in enumerate(unit_rows_of((x - turn) % 4, x)):
                    rows_t[16 * there : 16 * there + 16] = far[16 * index : 16 * index + 16]

    lane = lax.broadcasted_iota(jnp.int32, (512, 128), 1)
    blocks, swapped = [], []
    for z in range(4):
        block = context[:, 128 * z : 128 * z + 128].astype(F32)
        blocks.append(block)
        swapped.append(pltpu.roll(block, HEAD, 1))
    lane_out = lax.broadcasted_iota(jnp.int32, (8, 16, 512), 2)
    for parity, gate, out in ((core, gate_keep, keep), (1 - core, gate_send, send)):
        out[:, :112, :] = gate[...]
        grad = dot(rows_t[...], own_columns(normed, parity, 128))
        out[:, 112:160, :] = grad.astype(BF16).reshape(8, 48, 512)
        mine = (lane < HEAD) == (parity == 0)
        doubled = jnp.concatenate(
            [jnp.where(mine, block, other) for block, other in zip(blocks, swapped)], axis=1
        ).astype(BF16)
        grad = dot(cot_own[...], doubled).reshape(8, 32, 512)
        out[:, 160:, :] = jnp.where((lane_out & 127) < HEAD, grad[:, :16], grad[:, 16:]).astype(BF16)


def attend_kernel(
    lengths, queries, kv, before, after, cot_0, cot_1, cot_2, cot_3, context_out, d_query, d_before, d_after, d_own,
    d_contexts, key, value, key_t, value_t, scores, weights, d_scores, d_key, d_value
):
    place = locate(lengths)
    group_first, length = place[3], place[1]
    for turn, ref in enumerate((cot_0, cot_1, cot_2, cot_3)):
        d_contexts[slot(place, turn)] = ref[:128]
    for part, ref in enumerate((before, kv, after)):
        for piece in range(GROUP):
            start = 512 * part + ROWS * piece
            key_block = ref[piece, :, :128]
            value_block = ref[piece, :, 128:]
            key[start : start + ROWS] = key_block
            value[start : start + ROWS] = value_block
            key_t[:, start : start + ROWS] = key_block.T
            value_t[:, start : start + ROWS] = value_block.T
    d_key[...] = jnp.zeros_like(d_key)
    d_value[...] = jnp.zeros_like(d_value)
    lane = lax.broadcasted_iota(jnp.int32, (ROWS, 128), 1)
    first_head = lane < HEAD
    query_index = lax.broadcasted_iota(jnp.int32, (1, 256), 1)
    query_index = jnp.where(query_index < ROWS, query_index, query_index - ROWS)
    chunks = WINDOW // 128
    for block in range(GROUP):
        base = ROWS * block
        low = jnp.maximum(query_index, 512 - group_first - base)
        high = jnp.minimum(query_index + 1024, length - group_first + 511 - base)
        query = queries[block].astype(F32) * 0.125
        d_context = d_contexts[block].astype(F32)
        zero = jnp.zeros_like(query)
        query_pair = jnp.concatenate(
            [jnp.where(first_head, query, zero), jnp.where(first_head, zero, query)], axis=0
        ).astype(BF16)
        d_pair = jnp.concatenate(
            [jnp.where(first_head, d_context, zero), jnp.where(first_head, zero, d_context)], axis=0
        ).astype(BF16)

        def allowed_of(index):
            position = 128 * index + lax.broadcasted_iota(jnp.int32, (128, 256), 0)
            return (position >= low) & (position <= high)

        peak = jnp.full((128, 256), NEG_LARGE, F32)
        for index in range(chunks):
            part = dot(key[base + 128 * index : base + 128 * index + 128], query_pair, 1, 1)
            part = jnp.where(allowed_of(index), part, NEG_LARGE)
            scores[128 * index : 128 * index + 128] = part
            peak = jnp.maximum(peak, part)
        peak = jnp.max(peak, axis=0, keepdims=True)
        total = jnp.zeros((128, 256), F32)
        for index in range(chunks):
            part = scores[128 * index : 128 * index + 128]
            part = jnp.where(allowed_of(index), jnp.exp(part - peak), 0.0)
            scores[128 * index : 128 * index + 128] = part
            total = total + part
        scale = 1.0 / jnp.maximum(jnp.sum(total, axis=0, keepdims=True), 1.0)
        for index in range(chunks):
            part = scores[128 * index : 128 * index + 128] * scale
            weights[128 * index : 128 * index + 128] = part.astype(BF16)
        wide = dot(value_t[:, base : base + WINDOW], weights[...])
        context_t = jnp.concatenate([wide[:HEAD, :128], wide[HEAD:, 128:]], axis=0)
        context_out[block] = context_t.T.astype(BF16)
        product = context_t * d_context.T
        row_dot = jnp.concatenate(
            [
                jnp.sum(product[:HEAD], axis=0, keepdims=True),
                jnp.sum(product[HEAD:], axis=0, keepdims=True),
            ],
            axis=1,
        )
        for index in range(chunks):
            part = dot(value[base + 128 * index : base + 128 * index + 128], d_pair, 1, 1)
            part = weights[128 * index : 128 * index + 128].astype(F32) * (part - row_dot)
            d_scores[128 * index : 128 * index + 128] = part.astype(BF16)
        wide = dot(key_t[:, base : base + WINDOW], d_scores[...])
        d_query_t = jnp.concatenate([wide[:HEAD, :128], wide[HEAD:, 128:]], axis=0)
        d_query[:, base : base + 128] = (d_query_t * 0.125).astype(BF16)
        d_key[base : base + WINDOW] += dot(d_scores[...], query_pair)
        d_value[base : base + WINDOW] += dot(weights[...], d_pair)
    for piece in range(GROUP):
        for part, ref in enumerate((d_before, d_own, d_after)):
            start = 512 * part + ROWS * piece
            ref[piece, :, :128] = d_key[start : start + ROWS].astype(ref.dtype)
            ref[piece, :, 128:] = d_value[start : start + ROWS].astype(ref.dtype)


def unit_rows_of(source, target):
    units = [32 * part + 8 * source + row for part in range(3) for row in range(8)]
    wanted = [unit for unit in units if (unit // 3) % 4 == target]
    return [(units.index(unit), unit // 12 * 3 + unit % 3) for unit in wanted]


def join_kernel(
    lengths, d_query, own, from_before, from_after,
    unit_0, unit_1, unit_2, unit_3, back_0, back_1, back_2, back_3, joined_t
):
    place = locate(lengths)
    joined_t[:128] = d_query[...]
    for piece in range(GROUP):
        total = own[piece] + from_before[piece].astype(F32) + from_after[piece].astype(F32)
        total = total.astype(BF16)
        joined_t[128:256, 128 * piece : 128 * piece + 128] = total[:, :128].T
        joined_t[256:, 128 * piece : 128 * piece + 128] = total[:, 128:].T
    for turn, ref in enumerate((back_0, back_1, back_2, back_3)):
        ref[...] = joined_t[:, span((place[4] + turn) & 3, 128)]
    for x in range(4):

        @pl.when(place[4] == x)
        def _():
            for turn, ref in enumerate((unit_0, unit_1, unit_2, unit_3)):
                for index, (here, _) in enumerate(unit_rows_of(x, (x + turn) % 4)):
                    ref[16 * index : 16 * index + 16] = joined_t[16 * here : 16 * here + 16]


def rows_kernel(
    lengths, frames, cotangent, near_0, near_1, near_2, near_3, back_0, back_1, back_2, back_3, gate, d_upper,
    w_qkv, w_out, w_up, w_down, layer_out, d_frames, context, joined_t
):
    place = locate(lengths)
    for turn, near in enumerate((near_0, near_1, near_2, near_3)):
        context[:, span(slot(place, turn), 128)] = near[place[4]]
    for turn, back in enumerate((back_0, back_1, back_2, back_3)):
        pair = slot(place, turn)
        for part in range(3):
            joined_t[span(pair + 4 * part, 128), :] = back[128 * part : 128 * part + 128]
    gated = jnp.concatenate([gate[640 + 128 * m : 768 + 128 * m] for m in range(8)], axis=1)
    values = frames[...].astype(F32)
    out = values + dot(context[...], w_out[...]) + dot(gated, w_down[...])
    layer_out[...] = out.astype(BF16)
    unit_rows, inverse = normalize(values)
    d_normed = dot(d_upper[...], w_up[...], 1, 1) + dot(joined_t[...].T, w_qkv[...], 1, 1)
    d_frames[...] = (cotangent[...].astype(F32) + norm_back(d_normed, unit_rows, inverse)).astype(BF16)


def add_kernel(near, far, out):
    out[...] = (near[...].astype(F32) + far[...].astype(F32)).astype(BF16)


def chunk_sum_kernel(lengths, parts, out_0, out_1, out_2, out_3, total):
    place = locate(lengths)
    for first in range(0, parts.shape[1], 16):
        rows = slice(first, first + 16)
        acc = parts[0, rows, :].astype(F32)
        for source in range(1, 8):
            acc = acc + parts[source, rows, :].astype(F32)
        for z in range(4):
            total[z, rows, :] = acc[:, 128 * z : 128 * z + 128].astype(BF16)
    for turn, ref in enumerate((out_0, out_1, out_2, out_3)):
        ref[...] = total[(place[5] + turn) & 3]


def final_kernel(lengths, part_0, part_1, part_2, part_3, g_qkv_t, g_out_t, g_up_t, g_down_t, g_taps, ordered):
    place = locate(lengths)
    for turn, ref in enumerate((part_0, part_1, part_2, part_3)):
        ordered[(place[5] + 4 - turn) & 3] = ref[...].astype(F32)
    total = (ordered[0] + ordered[1]) + (ordered[2] + ordered[3])
    g_up_t[...] = total[:64]
    g_down_t[...] = total[64:96]
    turned = total[96:112].T
    g_taps[...] = jnp.concatenate([turned[:TAPS], turned[32 : 32 + TAPS]], axis=1)
    g_qkv_t[...] = total[112:160]
    g_out_t[:16] = total[160:, :HEAD]
    g_out_t[16:] = total[160:, HEAD:]


def shift(array, by):
    return lax.ppermute(array, "seq", [(i, i + by) for i in range(32) if 0 <= i + by < 32])


def other_core(array):
    return lax.ppermute(array, "dp", [(i, i ^ 1) for i in range(8)])


def swap_rows(array):
    return lax.all_to_all(array, "seq", 0, 0, axis_index_groups=ROW_GROUPS)


def turn_x(pieces):
    return [pieces[0]] + [
        lax.ppermute(pieces[by], "seq", [(i, i // 4 * 4 + (i + by) % 4) for i in range(32)])
        for by in range(1, 4)
    ]


def turn_z(pieces):
    return [pieces[0]] + [
        lax.ppermute(pieces[by], "dp", [(i, (i + 2 * by) % 8) for i in range(8)]) for by in range(1, 4)
    ]


def local(frames, cotangent, lengths, w_qkv, w_out, w_up, w_down, conv_kernel):
    frames, cotangent = frames[0], cotangent[0]
    wide = ((ROWS, 1024), BF16)
    wide_f = ((ROWS, 1024), F32)
    quad = ((4, ROWS, 256), BF16)
    frames_x = turn_x([frames] * 4)
    resid, d_gated, gating, d_conv, unit, inverse, slope, top, bottom = call(
        gate_kernel,
        [wide, wide, wide, wide, wide_f, ((ROWS, 128), F32), ((ROWS, 2048), F32),
         ((16, 2048), BF16), ((16, 2048), BF16)],
        scalars=1,
    )(lengths, *in_hbm(frames, cotangent, w_up, w_down))
    before, after = shift(bottom, 1), shift(top, -1)
    gating, frames_x, cot_later = lax.optimization_barrier((gating, frames_x, cotangent))
    small = ((384, 128), BF16)
    cot_x = turn_x(
        call(
            cotangent_kernel, [small] * 4, [pltpu.VMEM((ROWS, 512), BF16), pltpu.VMEM((1024, ROWS), BF16)], scalars=1
        )(lengths, cot_later, w_out)
    )
    normed, query, kv = call(
        project_kernel, [((512, 1024), BF16), ((4, ROWS, 128), BF16), quad], scalars=1
    )(lengths, *frames_x, w_qkv)
    gating, kv = lax.optimization_barrier((gating, kv))
    kv_before, kv_after = shift(kv, 4), shift(kv, -4)
    conv_in, d_gating_in, g_taps_in = call(
        conv_inner_kernel,
        [wide_f, wide_f, ((32, 1024), F32)],
        [pltpu.VMEM((160, 1024), F32), pltpu.VMEM((160, 1024), F32)],
    )(gating, d_conv, conv_kernel)
    conv_in, kv_before, kv_after, cot_x = lax.optimization_barrier((conv_in, kv_before, kv_after, cot_x))
    gate = ((1664, 128), BF16)
    d_upper, *gate_x = call(
        conv_outer_kernel,
        [((ROWS, 2048), BF16, HBM), gate, gate, gate, gate],
        [pltpu.VMEM((ROWS, 1024), F32), pltpu.VMEM((ROWS, 1024), F32),
         pltpu.VMEM((32, 2048), F32), pltpu.VMEM((32, 2048), F32),
         pltpu.VMEM((32, 1024), F32), pltpu.VMEM((2048, ROWS), BF16), pltpu.VMEM((32, 16, 128), BF16)],
        scalars=1,
    )(lengths, conv_in, d_gating_in, g_taps_in, d_conv, resid, d_gated, unit, inverse, slope, before, after, conv_kernel)
    query, gate_x = lax.optimization_barrier((query, gate_x))
    gate_x = turn_x(gate_x)
    near, d_query, d_before, d_after, d_own = call(
        attend_kernel,
        [((4, ROWS, 128), BF16), ((ROWS, 512), BF16), quad, quad, ((4, ROWS, 256), F32)],
        [pltpu.VMEM((4, ROWS, 128), BF16),
         pltpu.VMEM((1536, 128), BF16), pltpu.VMEM((1536, 128), BF16),
         pltpu.VMEM((128, 1536), BF16), pltpu.VMEM((128, 1536), BF16),
         pltpu.VMEM((WINDOW, 256), F32), pltpu.VMEM((WINDOW, 256), BF16), pltpu.VMEM((WINDOW, 256), BF16),
         pltpu.VMEM((1536, 128), F32), pltpu.VMEM((1536, 128), F32)],
        scalars=1,
    )(lengths, query, kv, kv_before, kv_after, *cot_x)
    from_before, from_after = shift(d_after, 4), shift(d_before, -4)
    near_x = turn_x([near] * 4)
    gate_x, d_own = lax.optimization_barrier((gate_x, d_own))
    keep, send, cot_own = call(
        gate_grads_kernel,
        [((8, 112, 512), BF16), ((8, 112, 512), BF16), ((256, 512), BF16)],
        [pltpu.VMEM((512, 512), BF16), pltpu.VMEM((512, 1024), BF16)],
        scalars=1,
    )(lengths, normed, *cot_x, *gate_x)
    keep, d_own = lax.optimization_barrier((keep, d_own))
    *far, back_0, back_1, back_2, back_3 = call(
        join_kernel, [((96, 512), BF16)] * 4 + [small] * 4, [pltpu.VMEM((384, 512), BF16)], scalars=1
    )(lengths, d_query, d_own, from_before, from_after)
    far_x = turn_x(far)
    keep, send = call(
        attention_grads_kernel,
        [((8, 176, 512), BF16), ((8, 176, 512), BF16)],
        [pltpu.VMEM((512, 512), BF16), pltpu.VMEM((384, 512), BF16)],
        scalars=1,
    )(lengths, keep, send, normed, cot_own, *near_x, *far_x)
    keep, *back = lax.optimization_barrier((keep, back_0, back_1, back_2, back_3))
    back_x = turn_x(back)
    (parts,) = call(add_kernel, [((8, 176, 512), BF16, HBM)])(keep, other_core(send))
    parts = swap_rows(parts)
    layer_out, d_frames = call(
        rows_kernel, [wide, wide], [pltpu.VMEM((ROWS, 512), BF16), pltpu.VMEM((1536, ROWS), BF16)], scalars=1
    )(
        lengths, frames, cotangent, *near_x, *back_x, gate_x[0], d_upper, *in_hbm(w_qkv, w_out, w_up, w_down)
    )
    parts, layer_out, d_frames = lax.optimization_barrier((parts, layer_out, d_frames))
    parts = call(
        chunk_sum_kernel, [((176, 128), BF16)] * 4, [pltpu.VMEM((4, 176, 128), BF16)], scalars=1
    )(lengths, parts)
    g_qkv, g_out, g_up, g_down, g_kernel = call(
        final_kernel,
        [((48, 128), F32), ((32, HEAD), F32), ((64, 128), F32), ((32, 128), F32), ((TAPS, 32), F32)],
        [pltpu.VMEM((4, 176, 128), F32)],
        scalars=1,
    )(lengths, *turn_z(parts))
    return (layer_out[None], d_frames[None], g_qkv.T, g_out.T, g_up.T, g_down.T, g_kernel)


def solution(mesh):
    return jax.shard_map(
        local,
        mesh=mesh,
        in_specs=(P("dp", "seq", None), P("dp", "seq", None), P("dp"), P(), P(), P(), P(), P()),
        out_specs=(
            P("dp", "seq", None),
            P("dp", "seq", None),
            P("dp", "seq"),
            P("dp", "seq"),
            P("dp", "seq"),
            P("dp", "seq"),
            P(None, "seq"),
        ),
        check_vma=False,
    )
```

```python
import jax
import jax.numpy as jnp
from jax import lax
from jax.experimental import pallas as pl
from jax.experimental.pallas import tpu as pltpu
from jax.sharding import PartitionSpec as P

HEAD = 64
BAND = 512
ROWS = 128
GROUP = 4
WINDOW = 2 * BAND + ROWS
MARGIN = 15
TAPS = 31

EPSILON = 1e-05
NEG_LARGE = -1e30
HALF_ROOT = 0.7071067811865476
NORMAL_PEAK = 0.3989422804014327

BF16 = jnp.bfloat16
F32 = jnp.float32
HBM = pltpu.HBM
VMEM_LIMIT = 24 * 2**20

ROW_GROUPS = [[4 * m + x for m in range(8)] for x in range(4)]


def call(body, outs, scratch=(), scalars=0):
    def run(*args):
        specs = [pl.BlockSpec(memory_space=pltpu.SMEM)] * scalars
        specs += [pl.BlockSpec(memory_space=pltpu.VMEM)] * (len(args) - scalars)
        return pl.pallas_call(
            body,
            out_shape=[
                HBM(*out[:2]) if len(out) > 2 else jax.ShapeDtypeStruct(*out) for out in outs
            ],
            in_specs=specs,
            out_specs=[pl.BlockSpec(memory_space=pltpu.VMEM)] * len(outs),
            scratch_shapes=list(scratch),
            compiler_params=pltpu.CompilerParams(vmem_limit_bytes=VMEM_LIMIT),
        )(*args)

    return run


def in_hbm(*arrays):
    return [pltpu.with_memory_space_constraint(array, HBM) for array in arrays]


def dot(left, right, left_dim=1, right_dim=0):
    return lax.dot_general(
        left, right, (((left_dim,), (right_dim,)), ((), ())), preferred_element_type=F32
    )


def normalize(values):
    centred = values - jnp.mean(values, axis=-1, keepdims=True)
    inverse = lax.rsqrt(jnp.mean(centred * centred, axis=-1, keepdims=True) + EPSILON)
    return (centred * inverse, inverse)


def norm_back(gradient, unit_rows, inverse):
    return inverse * (
        gradient
        - jnp.mean(gradient, axis=-1, keepdims=True)
        - unit_rows * jnp.mean(gradient * unit_rows, axis=-1, keepdims=True)
    )


def locate(lengths):
    seq, dp = lax.axis_index("seq"), lax.axis_index("dp")
    return (seq * ROWS, lengths[0], dp & 1, (seq >> 2) * (GROUP * ROWS), seq & 3, dp >> 1)


def slot(place, turn):
    return (place[4] + 4 - turn) & 3


def span(index, size):
    return pl.ds(pl.multiple_of(index * size, size), size)


def send_kernel(lengths, frames, cotangent, w_out, out_0, out_1, out_2, out_3, d_context, cot_t):
    place = locate(lengths)
    d_context[...] = dot(cotangent[...], w_out[...], 1, 1).astype(BF16)
    cot_t[...] = cotangent[...].T
    for turn, ref in enumerate((out_0, out_1, out_2, out_3)):
        x = (place[4] + turn) & 3
        ref[:, :1024] = frames[...]
        ref[:, 1024:1152] = d_context[:, span(x, 128)]
        for m in range(8):
            lanes = slice(1152 + 128 * (m // 4), 1280 + 128 * (m // 4))
            ref[32 * (m % 4) : 32 * (m % 4) + 32, lanes] = cot_t[span(4 * m + x, 32), :]


def project_kernel(lengths, frames_0, frames_1, frames_2, frames_3, w_qkv, normed, query, kv):
    place = locate(lengths)
    x = place[4]
    for turn, ref in enumerate((frames_0, frames_1, frames_2, frames_3)):
        unit_rows, _ = normalize(ref[:, :1024].astype(F32))
        normed[span(slot(place, turn), ROWS), :] = unit_rows.astype(BF16)
    weight = jnp.concatenate([w_qkv[:, span(x + 4 * part, 128)] for part in range(3)], axis=1)
    joined = dot(normed[...], weight).astype(BF16)
    query[...] = joined[:, :128].reshape(4, ROWS, 128)
    kv[...] = joined[:, 128:].reshape(4, ROWS, 256)


def gate_kernel(
    lengths, frames, cotangent, w_up, w_down,
    resid, d_gated, gating, d_conv, unit, inverse, slope, top, bottom
):
    place = locate(lengths)
    first_frame, length = place[0], place[1]
    unit_rows, _ = normalize(frames[...].astype(F32))
    upper = dot(unit_rows.astype(BF16), w_up[...])
    phi = 0.5 * (1.0 + lax.erf(upper * HALF_ROOT))
    slope[...] = phi + upper * jnp.exp(-0.5 * upper * upper) * NORMAL_PEAK
    hidden = (upper * phi).astype(BF16)
    gate_unit, gate_inv = normalize(hidden[:, 1024:].astype(F32))
    unit[...] = gate_unit
    inverse[...] = jnp.broadcast_to(gate_inv, inverse.shape)
    rows = first_frame + lax.broadcasted_iota(jnp.int32, (ROWS, 1024), 0)
    masked = jnp.where(rows < length, gate_unit, 0.0).astype(BF16)
    gating[...] = masked
    resid[...] = hidden[:, :1024]
    back = dot(cotangent[...], w_down[...], 1, 1).astype(BF16)
    d_gated[...] = back
    conv_back = (back.astype(F32) * hidden[:, :1024].astype(F32)).astype(BF16)
    d_conv[...] = conv_back
    top[:, :1024] = masked[:16]
    top[:, 1024:] = conv_back[:16]
    bottom[:, :1024] = masked[112:]
    bottom[:, 1024:] = conv_back[112:]


def conv_inner_kernel(gating, d_conv, taps, conv_out, d_gating, g_taps, gate_ext, conv_ext):
    for ext, ref in ((gate_ext, gating), (conv_ext, d_conv)):
        ext[:16] = jnp.zeros((16, 1024), F32)
        ext[16:144] = ref[...].astype(F32)
        ext[144:] = jnp.zeros((16, 1024), F32)
    g_taps[...] = jnp.zeros_like(g_taps)

    def chunk(index, _):
        lanes = pl.ds(pl.multiple_of(index * 128, 128), 128)
        for first in (0, 64):
            own = conv_ext[16 + first : 80 + first, lanes]
            forward = jnp.zeros((64, 128), F32)
            for shift in range(8):
                moved = gate_ext[pl.ds(first + shift, 88), lanes]
                for step in range(4):
                    offset = 8 * step + shift
                    if 1 <= offset <= TAPS:
                        part = moved[8 * step : 8 * step + 64]
                        forward = forward + taps[offset - 1 : offset, lanes] * part
                        g_taps[offset - 1 : offset, lanes] += jnp.sum(part * own, axis=0, keepdims=True)
            conv_out[first : first + 64, lanes] = forward
            backward = jnp.zeros((64, 128), F32)
            for shift in range(8):
                moved = conv_ext[pl.ds(first + shift, 88), lanes]
                for step in range(4):
                    offset = 8 * step + shift
                    if 1 <= offset <= TAPS:
                        part = moved[8 * step : 8 * step + 64]
                        backward = backward + taps[TAPS - offset : TAPS - offset + 1, lanes] * part
            d_gating[first : first + 64, lanes] = backward
        return 0

    lax.fori_loop(0, 8, chunk, 0)


def conv_outer_kernel(
    lengths, conv_in, d_gating_in, g_taps_in, d_conv, resid, d_gated, unit, inverse, slope, before, after, taps,
    d_upper, out_0, out_1, out_2, out_3, conv_out, d_gating, before_ext, after_ext, g_taps, d_upper_t, g_taps_t
):
    place = locate(lengths)
    first_frame, length = place[0], place[1]
    conv_out[...] = conv_in[...]
    d_gating[...] = d_gating_in[...]
    g_taps[...] = g_taps_in[...]
    before_ext[:16] = before[...].astype(F32)
    before_ext[16:] = jnp.zeros((16, 2048), F32)
    after_ext[:16] = jnp.zeros((16, 2048), F32)
    after_ext[16:] = after[...].astype(F32)

    def chunk(index, _):
        lanes = pl.ds(pl.multiple_of(index * 128, 128), 128)
        far = pl.ds(pl.multiple_of(index * 128 + 1024, 128), 128)
        for ext, first, skip in ((before_ext, 0, 0), (after_ext, 112, 16)):
            own = d_conv[first : first + 16, lanes].astype(F32)
            forward = conv_out[first : first + 16, lanes]
            backward = d_gating[first : first + 16, lanes]
            for step in range(1, 16):
                offset = step + skip
                part = ext[pl.ds(step, 16), lanes]
                forward = forward + taps[offset - 1 : offset, lanes] * part
                g_taps[offset - 1 : offset, lanes] += jnp.sum(part * own, axis=0, keepdims=True)
                part = ext[pl.ds(step, 16), far]
                backward = backward + taps[TAPS - offset : TAPS - offset + 1, lanes] * part
            conv_out[first : first + 16, lanes] = forward
            d_gating[first : first + 16, lanes] = backward
        return 0

    lax.fori_loop(0, 8, chunk, 0)
    conv = conv_out[...]
    gated = (resid[...].astype(F32) * conv).astype(BF16)
    rows = first_frame + lax.broadcasted_iota(jnp.int32, (ROWS, 1024), 0)
    d_gate = jnp.where(rows < length, d_gating[...], 0.0)
    d_gate = norm_back(d_gate, unit[...], inverse[:, :1])
    left = (d_gated[...].astype(F32) * conv * slope[:, :1024]).astype(BF16)
    right = (d_gate * slope[:, 1024:]).astype(BF16)
    d_upper[:, :1024] = left
    d_upper[:, 1024:] = right
    d_upper_t[:1024] = left.T
    d_upper_t[1024:] = right.T
    turned = jnp.concatenate([g_taps[...], jnp.zeros((96, 1024), F32)], axis=0).T.reshape(32, 32, 128)
    g_taps_t[...] = (turned[:, :16, :] + pltpu.roll(turned[:, 16:, :], 32, 2)).astype(BF16)
    for turn, ref in enumerate((out_0, out_1, out_2, out_3)):
        x = (place[4] + turn) & 3
        for m in range(8):
            ref[64 * m : 64 * m + 64] = d_upper_t[span(4 * m + x, 64), :]
            ref[512 + 16 * m : 528 + 16 * m] = g_taps_t[4 * m + x]
            ref[640 + 128 * m : 768 + 128 * m] = gated[:, 128 * m : 128 * m + 128]


def own_columns(array, core, width):
    parts = [
        array[:, pl.ds(pl.multiple_of(2 * width * z + width * core, width), width)] for z in range(4)
    ]
    return jnp.concatenate(parts, axis=1)


def gate_grads_kernel(
    lengths, normed, cot_0, cot_1, cot_2, cot_3, gate_0, gate_1, gate_2, gate_3,
    keep, send, cot_own, d_upper_t, gated
):
    place = locate(lengths)
    x, core = place[4], place[2]
    gates = (gate_0, gate_1, gate_2, gate_3)
    g_taps = gate_0[512:640].astype(F32)
    for ref in gates[1:]:
        g_taps = g_taps + ref[512:640].astype(F32)
    g_taps = g_taps.astype(BF16).reshape(8, 16, 128)
    for turn, (gate, cot) in enumerate(zip(gates, (cot_0, cot_1, cot_2, cot_3))):
        here = span(slot(place, turn), 128)
        d_upper_t[:, here] = gate[:512]
        for block in range(8):
            gated[here, 128 * block : 128 * block + 128] = gate[640 + 128 * block : 768 + 128 * block]
        cot_own[:128, here] = cot[:, 1152:1280]
        cot_own[128:, here] = cot[:, 1280:]
    for parity, out in ((core, keep), (1 - core, send)):
        grad = dot(d_upper_t[...], own_columns(normed, parity, 128))
        out[:, :64, :] = grad.astype(BF16).reshape(8, 64, 512)
        grad = dot(cot_own[...], own_columns(gated, parity, 128))
        out[:, 64:96, :] = grad.astype(BF16).reshape(8, 32, 512)
        for z in range(4):
            out[:, 96:, 128 * z : 128 * z + 128] = g_taps


def attention_grads_kernel(
    lengths, normed, cot_own, far_0, far_1, far_2, far_3,
    keep, send, context, rows_t
):
    place = locate(lengths)
    core = place[2]
    for turn, far in enumerate((far_0, far_1, far_2, far_3)):
        for block in range(GROUP):
            tokens = slice(128 * block, 128 * block + 128)
            context[tokens, span(slot(place, turn), 128)] = far[96:, tokens]
    for x in range(4):

        @pl.when(place[4] == x)
        def _():
            for turn, far in enumerate((far_0, far_1, far_2, far_3)):
                for index, (_, there) in enumerate(unit_rows_of((x - turn) % 4, x)):
                    rows_t[16 * there : 16 * there + 16] = far[16 * index : 16 * index + 16]

    lane = lax.broadcasted_iota(jnp.int32, (512, 128), 1)
    blocks, swapped = [], []
    for z in range(4):
        block = context[:, 128 * z : 128 * z + 128].astype(F32)
        blocks.append(block)
        swapped.append(pltpu.roll(block, HEAD, 1))
    lane_out = lax.broadcasted_iota(jnp.int32, (8, 16, 512), 2)
    for parity, out in ((core, keep), (1 - core, send)):
        grad = dot(rows_t[...], own_columns(normed, parity, 128))
        out[:, :48, :] = grad.astype(BF16).reshape(8, 48, 512)
        mine = (lane < HEAD) == (parity == 0)
        doubled = jnp.concatenate(
            [jnp.where(mine, block, other) for block, other in zip(blocks, swapped)], axis=1
        ).astype(BF16)
        grad = dot(cot_own[...], doubled).reshape(8, 32, 512)
        out[:, 48:, :] = jnp.where((lane_out & 127) < HEAD, grad[:, :16], grad[:, 16:]).astype(BF16)


def attend_kernel(
    lengths, queries, kv, before, after, cot_0, cot_1, cot_2, cot_3, context_out, d_query, d_before, d_after, d_own,
    d_contexts, key, value, key_t, value_t, scores, weights, d_scores, d_key, d_value
):
    place = locate(lengths)
    group_first, length = place[3], place[1]
    for turn, ref in enumerate((cot_0, cot_1, cot_2, cot_3)):
        d_contexts[slot(place, turn)] = ref[:, 1024:1152]
    for part, ref in enumerate((before, kv, after)):
        for piece in range(GROUP):
            start = 512 * part + ROWS * piece
            key_block = ref[piece, :, :128]
            value_block = ref[piece, :, 128:]
            key[start : start + ROWS] = key_block
            value[start : start + ROWS] = value_block
            key_t[:, start : start + ROWS] = key_block.T
            value_t[:, start : start + ROWS] = value_block.T
    d_key[...] = jnp.zeros_like(d_key)
    d_value[...] = jnp.zeros_like(d_value)
    lane = lax.broadcasted_iota(jnp.int32, (ROWS, 128), 1)
    first_head = lane < HEAD
    query_index = lax.broadcasted_iota(jnp.int32, (1, 256), 1)
    query_index = jnp.where(query_index < ROWS, query_index, query_index - ROWS)
    chunks = WINDOW // 128
    for block in range(GROUP):
        base = ROWS * block
        low = jnp.maximum(query_index, 512 - group_first - base)
        high = jnp.minimum(query_index + 1024, length - group_first + 511 - base)
        query = queries[block].astype(F32) * 0.125
        d_context = d_contexts[block].astype(F32)
        zero = jnp.zeros_like(query)
        query_pair = jnp.concatenate(
            [jnp.where(first_head, query, zero), jnp.where(first_head, zero, query)], axis=0
        ).astype(BF16)
        d_pair = jnp.concatenate(
            [jnp.where(first_head, d_context, zero), jnp.where(first_head, zero, d_context)], axis=0
        ).astype(BF16)

        def allowed_of(index):
            position = 128 * index + lax.broadcasted_iota(jnp.int32, (128, 256), 0)
            return (position >= low) & (position <= high)

        peak = jnp.full((128, 256), NEG_LARGE, F32)
        for index in range(chunks):
            part = dot(key[base + 128 * index : base + 128 * index + 128], query_pair, 1, 1)
            part = jnp.where(allowed_of(index), part, NEG_LARGE)
            scores[128 * index : 128 * index + 128] = part
            peak = jnp.maximum(peak, part)
        peak = jnp.max(peak, axis=0, keepdims=True)
        total = jnp.zeros((128, 256), F32)
        for index in range(chunks):
            part = scores[128 * index : 128 * index + 128]
            part = jnp.where(allowed_of(index), jnp.exp(part - peak), 0.0)
            scores[128 * index : 128 * index + 128] = part
            total = total + part
        scale = 1.0 / jnp.maximum(jnp.sum(total, axis=0, keepdims=True), 1.0)
        for index in range(chunks):
            part = scores[128 * index : 128 * index + 128] * scale
            weights[128 * index : 128 * index + 128] = part.astype(BF16)
        wide = dot(value_t[:, base : base + WINDOW], weights[...])
        context_t = jnp.concatenate([wide[:HEAD, :128], wide[HEAD:, 128:]], axis=0)
        context_out[block] = context_t.T.astype(BF16)
        product = context_t * d_context.T
        row_dot = jnp.concatenate(
            [
                jnp.sum(product[:HEAD], axis=0, keepdims=True),
                jnp.sum(product[HEAD:], axis=0, keepdims=True),
            ],
            axis=1,
        )
        for index in range(chunks):
            part = dot(value[base + 128 * index : base + 128 * index + 128], d_pair, 1, 1)
            part = weights[128 * index : 128 * index + 128].astype(F32) * (part - row_dot)
            d_scores[128 * index : 128 * index + 128] = part.astype(BF16)
        wide = dot(key_t[:, base : base + WINDOW], d_scores[...])
        d_query_t = jnp.concatenate([wide[:HEAD, :128], wide[HEAD:, 128:]], axis=0)
        d_query[:, base : base + 128] = (d_query_t * 0.125).astype(BF16)
        d_key[base : base + WINDOW] += dot(d_scores[...], query_pair)
        d_value[base : base + WINDOW] += dot(weights[...], d_pair)
    for piece in range(GROUP):
        for part, ref in enumerate((d_before, d_own, d_after)):
            start = 512 * part + ROWS * piece
            ref[piece, :, :128] = d_key[start : start + ROWS].astype(ref.dtype)
            ref[piece, :, 128:] = d_value[start : start + ROWS].astype(ref.dtype)


def unit_rows_of(source, target):
    units = [32 * part + 8 * source + row for part in range(3) for row in range(8)]
    wanted = [unit for unit in units if (unit // 3) % 4 == target]
    return [(units.index(unit), unit // 12 * 3 + unit % 3) for unit in wanted]


def join_kernel(
    lengths, context, d_query, own, from_before, from_after,
    unit_0, unit_1, unit_2, unit_3, back_0, back_1, back_2, back_3, joined_t
):
    place = locate(lengths)
    joined_t[:128] = d_query[...]
    for piece in range(GROUP):
        total = own[piece] + from_before[piece].astype(F32) + from_after[piece].astype(F32)
        total = total.astype(BF16)
        joined_t[128:256, 128 * piece : 128 * piece + 128] = total[:, :128].T
        joined_t[256:, 128 * piece : 128 * piece + 128] = total[:, 128:].T
    for turn, ref in enumerate((back_0, back_1, back_2, back_3)):
        ref[...] = joined_t[:, span((place[4] + turn) & 3, 128)]
    for ref in (unit_0, unit_1, unit_2, unit_3):
        for block in range(GROUP):
            ref[96:, 128 * block : 128 * block + 128] = context[block]
    for x in range(4):

        @pl.when(place[4] == x)
        def _():
            for turn, ref in enumerate((unit_0, unit_1, unit_2, unit_3)):
                for index, (here, _) in enumerate(unit_rows_of(x, (x + turn) % 4)):
                    ref[16 * index : 16 * index + 16] = joined_t[16 * here : 16 * here + 16]


def gate_rows_kernel(frames, gate, d_upper, w_up, w_down, layer_part, d_normed):
    gated = jnp.concatenate([gate[640 + 128 * m : 768 + 128 * m] for m in range(8)], axis=1)
    layer_part[...] = frames[...].astype(F32) + dot(gated, w_down[...])
    d_normed[...] = dot(d_upper[...], w_up[...], 1, 1)


def rows_kernel(
    lengths, frames, cotangent, far_0, far_1, far_2, far_3, back_0, back_1, back_2, back_3, layer_part, d_normed,
    w_qkv, w_out, layer_out, d_frames, context, joined_t
):
    place = locate(lengths)
    for turn, far in enumerate((far_0, far_1, far_2, far_3)):
        context[:, span(slot(place, turn), 128)] = far[96:, span(place[4], 128)]
    for turn, back in enumerate((back_0, back_1, back_2, back_3)):
        pair = slot(place, turn)
        for part in range(3):
            joined_t[span(pair + 4 * part, 128), :] = back[128 * part : 128 * part + 128]
    layer_out[...] = (layer_part[...] + dot(context[...], w_out[...])).astype(BF16)
    unit_rows, inverse = normalize(frames[...].astype(F32))
    d_rows = d_normed[...] + dot(joined_t[...].T, w_qkv[...], 1, 1)
    d_frames[...] = (cotangent[...].astype(F32) + norm_back(d_rows, unit_rows, inverse)).astype(BF16)


def add_kernel(gate, gate_far, attention, attention_far, out):
    out[:, :112] = (gate[...].astype(F32) + gate_far[...].astype(F32)).astype(BF16)
    out[:, 112:] = (attention[...].astype(F32) + attention_far[...].astype(F32)).astype(BF16)


def chunk_sum_kernel(lengths, parts, out_0, out_1, out_2, out_3, total):
    place = locate(lengths)
    for first in range(0, parts.shape[1], 16):
        rows = slice(first, first + 16)
        acc = parts[0, rows, :].astype(F32)
        for source in range(1, 8):
            acc = acc + parts[source, rows, :].astype(F32)
        for z in range(4):
            total[z, rows, :] = acc[:, 128 * z : 128 * z + 128].astype(BF16)
    for turn, ref in enumerate((out_0, out_1, out_2, out_3)):
        ref[...] = total[(place[5] + turn) & 3]


def final_kernel(lengths, part_0, part_1, part_2, part_3, g_qkv_t, g_out_t, g_up_t, g_down_t, g_taps, ordered):
    place = locate(lengths)
    for turn, ref in enumerate((part_0, part_1, part_2, part_3)):
        ordered[(place[5] + 4 - turn) & 3] = ref[...].astype(F32)
    total = (ordered[0] + ordered[1]) + (ordered[2] + ordered[3])
    g_up_t[...] = total[:64]
    g_down_t[...] = total[64:96]
    turned = total[96:112].T
    g_taps[...] = jnp.concatenate([turned[:TAPS], turned[32 : 32 + TAPS]], axis=1)
    g_qkv_t[...] = total[112:160]
    g_out_t[:16] = total[160:, :HEAD]
    g_out_t[16:] = total[160:, HEAD:]


def shift(array, by):
    return lax.ppermute(array, "seq", [(i, i + by) for i in range(32) if 0 <= i + by < 32])


def other_core(array):
    return lax.ppermute(array, "dp", [(i, i ^ 1) for i in range(8)])


def swap_rows(array):
    return lax.all_to_all(array, "seq", 0, 0, axis_index_groups=ROW_GROUPS)


def turn_x(pieces):
    return [pieces[0]] + [
        lax.ppermute(pieces[by], "seq", [(i, i // 4 * 4 + (i + by) % 4) for i in range(32)])
        for by in range(1, 4)
    ]


def turn_z(pieces):
    return [pieces[0]] + [
        lax.ppermute(pieces[by], "dp", [(i, (i + 2 * by) % 8) for i in range(8)]) for by in range(1, 4)
    ]


def local(frames, cotangent, lengths, w_qkv, w_out, w_up, w_down, conv_kernel):
    frames, cotangent = frames[0], cotangent[0]
    wide = ((ROWS, 1024), BF16)
    wide_f = ((ROWS, 1024), F32)
    quad = ((4, ROWS, 256), BF16)
    piece = ((ROWS, 1408), BF16)
    pieces = call(
        send_kernel, [piece] * 4, [pltpu.VMEM((ROWS, 512), BF16), pltpu.VMEM((1024, ROWS), BF16)], scalars=1
    )(lengths, *in_hbm(frames, cotangent, w_out))
    pieces, frames_later = lax.optimization_barrier((pieces, frames))
    in_x = turn_x(pieces)
    resid, d_gated, gating, d_conv, unit, inverse, slope, top, bottom = call(
        gate_kernel,
        [wide, wide, wide, wide, wide_f, ((ROWS, 128), F32), ((ROWS, 2048), F32),
         ((16, 2048), BF16), ((16, 2048), BF16)],
        scalars=1,
    )(lengths, *in_hbm(frames_later, cotangent, w_up, w_down))
    before, after = shift(bottom, 1), shift(top, -1)
    conv_in, d_gating_in, g_taps_in = call(
        conv_inner_kernel,
        [wide_f, wide_f, ((32, 1024), F32)],
        [pltpu.VMEM((160, 1024), F32), pltpu.VMEM((160, 1024), F32)],
    )(gating, d_conv, conv_kernel)
    gate = ((1664, 128), BF16)
    d_upper, *gate_x = call(
        conv_outer_kernel,
        [((ROWS, 2048), BF16, HBM), gate, gate, gate, gate],
        [pltpu.VMEM((ROWS, 1024), F32), pltpu.VMEM((ROWS, 1024), F32),
         pltpu.VMEM((32, 2048), F32), pltpu.VMEM((32, 2048), F32),
         pltpu.VMEM((32, 1024), F32), pltpu.VMEM((2048, ROWS), BF16), pltpu.VMEM((32, 16, 128), BF16)],
        scalars=1,
    )(lengths, conv_in, d_gating_in, g_taps_in, d_conv, resid, d_gated, unit, inverse, slope, before, after, conv_kernel)
    in_x, gate_x = lax.optimization_barrier((in_x, gate_x))
    normed, query, kv = call(
        project_kernel, [((512, 1024), BF16), ((4, ROWS, 128), BF16), quad], scalars=1
    )(lengths, *in_x, w_qkv)
    kv_before, kv_after = shift(kv, 4), shift(kv, -4)
    gate_x = turn_x(gate_x)
    context, d_query, d_before, d_after, d_own = call(
        attend_kernel,
        [((4, ROWS, 128), BF16), ((ROWS, 512), BF16), quad, quad, ((4, ROWS, 256), F32)],
        [pltpu.VMEM((4, ROWS, 128), BF16),
         pltpu.VMEM((1536, 128), BF16), pltpu.VMEM((1536, 128), BF16),
         pltpu.VMEM((128, 1536), BF16), pltpu.VMEM((128, 1536), BF16),
         pltpu.VMEM((WINDOW, 256), F32), pltpu.VMEM((WINDOW, 256), BF16), pltpu.VMEM((WINDOW, 256), BF16),
         pltpu.VMEM((1536, 128), F32), pltpu.VMEM((1536, 128), F32)],
        scalars=1,
    )(lengths, query, kv, kv_before, kv_after, *in_x)
    from_before, from_after = shift(d_after, 4), shift(d_before, -4)
    frames_later, d_own = lax.optimization_barrier((frames, d_own))
    layer_part, d_normed = call(gate_rows_kernel, [wide_f + (HBM,), wide_f + (HBM,)])(
        *in_hbm(frames_later), gate_x[0], *in_hbm(d_upper), w_up, w_down
    )
    gate_x, d_normed, d_own = lax.optimization_barrier((gate_x, d_normed, d_own))
    small = ((384, 128), BF16)
    *far, back_0, back_1, back_2, back_3 = call(
        join_kernel, [((224, 512), BF16)] * 4 + [small + (HBM,)] * 4, [pltpu.VMEM((384, 512), BF16)], scalars=1
    )(lengths, context, d_query, d_own, from_before, from_after)
    far, gate_x = lax.optimization_barrier((far, gate_x))
    far_x = turn_x(far)
    keep, send, cot_own = call(
        gate_grads_kernel,
        [((8, 112, 512), BF16), ((8, 112, 512), BF16), ((256, 512), BF16)],
        [pltpu.VMEM((512, 512), BF16), pltpu.VMEM((512, 1024), BF16)],
        scalars=1,
    )(lengths, normed, *in_x, *gate_x)
    gate_far = other_core(send)
    attention_keep, send = call(
        attention_grads_kernel,
        [((8, 64, 512), BF16), ((8, 64, 512), BF16)],
        [pltpu.VMEM((512, 512), BF16), pltpu.VMEM((384, 512), BF16)],
        scalars=1,
    )(lengths, normed, cot_own, *far_x)
    send, *back = lax.optimization_barrier((send, back_0, back_1, back_2, back_3))
    back_x = turn_x(back)
    (parts,) = call(add_kernel, [((8, 176, 512), BF16, HBM)])(keep, gate_far, attention_keep, other_core(send))
    parts = swap_rows(parts)
    layer_out, d_frames = call(
        rows_kernel, [wide, wide], [pltpu.VMEM((ROWS, 512), BF16), pltpu.VMEM((1536, ROWS), BF16)], scalars=1
    )(
        lengths, frames, cotangent, *far_x, *back_x, layer_part, d_normed, *in_hbm(w_qkv, w_out)
    )
    parts, layer_out, d_frames = lax.optimization_barrier((parts, layer_out, d_frames))
    parts = call(
        chunk_sum_kernel, [((176, 128), BF16)] * 4, [pltpu.VMEM((4, 176, 128), BF16)], scalars=1
    )(lengths, parts)
    g_qkv, g_out, g_up, g_down, g_kernel = call(
        final_kernel,
        [((48, 128), F32), ((32, HEAD), F32), ((64, 128), F32), ((32, 128), F32), ((TAPS, 32), F32)],
        [pltpu.VMEM((4, 176, 128), F32)],
        scalars=1,
    )(lengths, *turn_z(parts))
    return (layer_out[None], d_frames[None], g_qkv.T, g_out.T, g_up.T, g_down.T, g_kernel)


def solution(mesh):
    return jax.shard_map(
        local,
        mesh=mesh,
        in_specs=(P("dp", "seq", None), P("dp", "seq", None), P("dp"), P(), P(), P(), P(), P()),
        out_specs=(
            P("dp", "seq", None),
            P("dp", "seq", None),
            P("dp", "seq"),
            P("dp", "seq"),
            P("dp", "seq"),
            P("dp", "seq"),
            P(None, "seq"),
        ),
        check_vma=False,
    )
```

```python
import jax
import jax.numpy as jnp
from jax import lax
from jax.experimental import pallas as pl
from jax.experimental.pallas import tpu as pltpu
from jax.sharding import Mesh, PartitionSpec as P

HEAD = 64
BAND = 512
ROWS = 128
GROUP = 4
WINDOW = 2 * BAND + ROWS
MARGIN = 15
TAPS = 31

EPSILON = 1e-05
NEG_LARGE = -3e38
HALF_ROOT = 0.7071067811865476
NORMAL_PEAK = 0.3989422804014327

BF16 = jnp.bfloat16
F32 = jnp.float32
HBM = pltpu.HBM
VMEM_LIMIT = 24 * 2**20


def call(body, outs, scratch=(), scalars=0):
    def run(*args):
        specs = [pl.BlockSpec(memory_space=pltpu.SMEM)] * scalars
        specs += [pl.BlockSpec(memory_space=pltpu.VMEM)] * (len(args) - scalars)
        return pl.pallas_call(
            body,
            out_shape=[
                HBM(*out[:2]) if len(out) > 2 else jax.ShapeDtypeStruct(*out) for out in outs
            ],
            in_specs=specs,
            out_specs=[pl.BlockSpec(memory_space=pltpu.VMEM)] * len(outs),
            scratch_shapes=list(scratch),
            compiler_params=pltpu.CompilerParams(vmem_limit_bytes=VMEM_LIMIT),
        )(*args)

    return run


def in_hbm(*arrays):
    return [pltpu.with_memory_space_constraint(array, HBM) for array in arrays]


def dot(left, right, left_dim=1, right_dim=0):
    return lax.dot_general(
        left, right, (((left_dim,), (right_dim,)), ((), ())), preferred_element_type=F32
    )


def normalize(values):
    centred = values - jnp.mean(values, axis=-1, keepdims=True)
    inverse = lax.rsqrt(jnp.mean(centred * centred, axis=-1, keepdims=True) + EPSILON)
    return (centred * inverse, inverse)


def norm_back(gradient, unit_rows, inverse):
    return inverse * (
        gradient
        - jnp.mean(gradient, axis=-1, keepdims=True)
        - unit_rows * jnp.mean(gradient * unit_rows, axis=-1, keepdims=True)
    )


def locate(lengths):
    z_low, y, x = lax.axis_index("z_low"), lax.axis_index("y"), lax.axis_index("x")
    row = 4 * z_low + y
    return ((4 * row + x) * ROWS, lengths[0], lax.axis_index("core"), row * (GROUP * ROWS), x, lax.axis_index("z_high"))


def slot(place, turn):
    return (place[4] + 4 - turn) & 3


def span(index, size):
    return pl.ds(pl.multiple_of(index * size, size), size)


def send_kernel(lengths, frames, cotangent, w_out, out_0, out_1, out_2, out_3, d_context, cot_t):
    place = locate(lengths)
    d_context[...] = dot(cotangent[...], w_out[...], 1, 1).astype(BF16)
    cot_t[...] = cotangent[...].T
    for turn, ref in enumerate((out_0, out_1, out_2, out_3)):
        x = (place[4] + turn) & 3
        ref[:, :1024] = frames[...]
        ref[:, 1024:1152] = d_context[:, span(x, 128)]
        for m in range(8):
            lanes = slice(1152 + 128 * (m // 4), 1280 + 128 * (m // 4))
            ref[32 * (m % 4) : 32 * (m % 4) + 32, lanes] = cot_t[span(4 * m + x, 32), :]


def project_kernel(lengths, frames_0, frames_1, frames_2, frames_3, w_qkv, normed, query, kv):
    place = locate(lengths)
    x = place[4]
    for turn, ref in enumerate((frames_0, frames_1, frames_2, frames_3)):
        unit_rows, _ = normalize(ref[:, :1024].astype(F32))
        normed[span(slot(place, turn), ROWS), :] = unit_rows.astype(BF16)
    weight = jnp.concatenate([w_qkv[:, span(x + 4 * part, 128)] for part in range(3)], axis=1)
    joined = dot(normed[...], weight).astype(BF16)
    query[...] = joined[:, :128].reshape(4, ROWS, 128)
    kv[...] = joined[:, 128:].reshape(4, ROWS, 256)


def gate_kernel(
    lengths, frames, cotangent, w_up, w_down,
    resid, d_gated, gating, d_conv, unit, inverse, slope, top, bottom
):
    place = locate(lengths)
    first_frame, length = place[0], place[1]
    unit_rows, _ = normalize(frames[...].astype(F32))
    upper = dot(unit_rows.astype(BF16), w_up[...])
    phi = 0.5 * (1.0 + lax.erf(upper * HALF_ROOT))
    slope[...] = phi + upper * jnp.exp(-0.5 * upper * upper) * NORMAL_PEAK
    hidden = (upper * phi).astype(BF16)
    gate_unit, gate_inv = normalize(hidden[:, 1024:].astype(F32))
    unit[...] = gate_unit
    inverse[...] = jnp.broadcast_to(gate_inv, inverse.shape)
    rows = first_frame + lax.broadcasted_iota(jnp.int32, (ROWS, 1024), 0)
    masked = jnp.where(rows < length, gate_unit, 0.0).astype(BF16)
    gating[...] = masked
    resid[...] = hidden[:, :1024]
    back = dot(cotangent[...], w_down[...], 1, 1).astype(BF16)
    d_gated[...] = back
    conv_back = (back.astype(F32) * hidden[:, :1024].astype(F32)).astype(BF16)
    d_conv[...] = conv_back
    top[:, :1024] = masked[:16]
    top[:, 1024:] = conv_back[:16]
    bottom[:, :1024] = masked[112:]
    bottom[:, 1024:] = conv_back[112:]


def conv_inner_kernel(gating, d_conv, taps, conv_out, d_gating, g_taps, gate_ext, conv_ext, sums):
    for ext, ref in ((gate_ext, gating), (conv_ext, d_conv)):
        ext[:, :16] = jnp.zeros((8, 16, 128), F32)
        ext[:, 144:] = jnp.zeros((8, 16, 128), F32)
        for block in range(8):
            ext[block, 16:144] = ref[:, 128 * block : 128 * block + 128].astype(F32)
    sums[...] = jnp.zeros_like(sums)

    def chunk(index, _):
        lanes = pl.ds(pl.multiple_of(index * 128, 128), 128)
        for first in (0, 64):
            own = conv_ext[index, 16 + first : 80 + first, :]
            forward = jnp.zeros((64, 128), F32)
            for shift in range(8):
                moved = gate_ext[index, pl.ds(first + shift, 88), :]
                for step in range(4):
                    offset = 8 * step + shift
                    if 1 <= offset <= TAPS:
                        part = moved[8 * step : 8 * step + 64]
                        forward = forward + taps[offset - 1 : offset, lanes] * part
                        sums[offset - 1, :, lanes] += jnp.sum((part * own).reshape(8, 8, 128), axis=0)
            conv_out[first : first + 64, lanes] = forward
            backward = jnp.zeros((64, 128), F32)
            for shift in range(8):
                moved = conv_ext[index, pl.ds(first + shift, 88), :]
                for step in range(4):
                    offset = 8 * step + shift
                    if 1 <= offset <= TAPS:
                        part = moved[8 * step : 8 * step + 64]
                        backward = backward + taps[TAPS - offset : TAPS - offset + 1, lanes] * part
            d_gating[first : first + 64, lanes] = backward
        return 0

    lax.fori_loop(0, 8, chunk, 0)
    g_taps[...] = jnp.sum(sums[...], axis=1)


def conv_outer_kernel(
    lengths, conv_in, d_gating_in, g_taps_in, d_conv, resid, d_gated, unit, inverse, slope, before, after, taps,
    d_upper, out_0, out_1, out_2, out_3, conv_out, d_gating, before_ext, after_ext, g_taps, d_upper_t, g_taps_t
):
    place = locate(lengths)
    first_frame, length = place[0], place[1]
    conv_out[...] = conv_in[...]
    d_gating[...] = d_gating_in[...]
    g_taps[...] = g_taps_in[...]
    before_ext[:16] = before[...].astype(F32)
    before_ext[16:] = jnp.zeros((16, 2048), F32)
    after_ext[:16] = jnp.zeros((16, 2048), F32)
    after_ext[16:] = after[...].astype(F32)

    def chunk(index, _):
        lanes = pl.ds(pl.multiple_of(index * 128, 128), 128)
        far = pl.ds(pl.multiple_of(index * 128 + 1024, 128), 128)
        for ext, first, skip in ((before_ext, 0, 0), (after_ext, 112, 16)):
            own = d_conv[first : first + 16, lanes].astype(F32)
            forward = conv_out[first : first + 16, lanes]
            backward = d_gating[first : first + 16, lanes]
            for step in range(1, 16):
                offset = step + skip
                part = ext[pl.ds(step, 16), lanes]
                forward = forward + taps[offset - 1 : offset, lanes] * part
                g_taps[offset - 1 : offset, lanes] += jnp.sum(part * own, axis=0, keepdims=True)
                part = ext[pl.ds(step, 16), far]
                backward = backward + taps[TAPS - offset : TAPS - offset + 1, lanes] * part
            conv_out[first : first + 16, lanes] = forward
            d_gating[first : first + 16, lanes] = backward
        return 0

    lax.fori_loop(0, 8, chunk, 0)
    conv = conv_out[...]
    gated = (resid[...].astype(F32) * conv).astype(BF16)
    rows = first_frame + lax.broadcasted_iota(jnp.int32, (ROWS, 1024), 0)
    d_gate = jnp.where(rows < length, d_gating[...], 0.0)
    d_gate = norm_back(d_gate, unit[...], inverse[:, :1])
    left = (d_gated[...].astype(F32) * conv * slope[:, :1024]).astype(BF16)
    right = (d_gate * slope[:, 1024:]).astype(BF16)
    d_upper[:, :1024] = left
    d_upper[:, 1024:] = right
    d_upper_t[:1024] = left.T
    d_upper_t[1024:] = right.T
    turned = jnp.concatenate([g_taps[...], jnp.zeros((96, 1024), F32)], axis=0).T.reshape(32, 32, 128)
    g_taps_t[...] = (turned[:, :16, :] + pltpu.roll(turned[:, 16:, :], 32, 2)).astype(BF16)
    for turn, ref in enumerate((out_0, out_1, out_2, out_3)):
        x = (place[4] + turn) & 3
        for m in range(8):
            ref[64 * m : 64 * m + 64] = d_upper_t[span(4 * m + x, 64), :]
            ref[512 + 16 * m : 528 + 16 * m] = g_taps_t[4 * m + x]
            ref[640 + 128 * m : 768 + 128 * m] = gated[:, 128 * m : 128 * m + 128]


def own_columns(array, core, width):
    parts = [
        array[:, pl.ds(pl.multiple_of(2 * width * z + width * core, width), width)] for z in range(4)
    ]
    return jnp.concatenate(parts, axis=1)


def gate_grads_kernel(
    lengths, normed, cot_0, cot_1, cot_2, cot_3, gate_0, gate_1, gate_2, gate_3,
    keep, send, cot_own, d_upper_t, gated
):
    place = locate(lengths)
    x, core = place[4], place[2]
    gates = (gate_0, gate_1, gate_2, gate_3)
    g_taps = gate_0[512:640].astype(F32)
    for ref in gates[1:]:
        g_taps = g_taps + ref[512:640].astype(F32)
    g_taps = g_taps.astype(BF16).reshape(8, 16, 128)
    for turn, (gate, cot) in enumerate(zip(gates, (cot_0, cot_1, cot_2, cot_3))):
        here = span(slot(place, turn), 128)
        d_upper_t[:, here] = gate[:512]
        for block in range(8):
            gated[here, 128 * block : 128 * block + 128] = gate[640 + 128 * block : 768 + 128 * block]
        cot_own[:128, here] = cot[:, 1152:1280]
        cot_own[128:, here] = cot[:, 1280:]
    for parity, out in ((core, keep), (1 - core, send)):
        grad = dot(d_upper_t[...], own_columns(normed, parity, 128))
        out[:, :64, :] = grad.astype(BF16).reshape(8, 64, 512)
        grad = dot(cot_own[...], own_columns(gated, parity, 128))
        out[:, 64:96, :] = grad.astype(BF16).reshape(8, 32, 512)
        for z in range(4):
            out[:, 96:, 128 * z : 128 * z + 128] = g_taps


def attention_grads_kernel(
    lengths, normed, cot_own, far_0, far_1, far_2, far_3,
    keep, send, context, rows_t
):
    place = locate(lengths)
    core = place[2]
    for turn, far in enumerate((far_0, far_1, far_2, far_3)):
        for block in range(GROUP):
            tokens = slice(128 * block, 128 * block + 128)
            context[tokens, span(slot(place, turn), 128)] = far[96:, tokens]
    for x in range(4):

        @pl.when(place[4] == x)
        def _():
            for turn, far in enumerate((far_0, far_1, far_2, far_3)):
                for index, (_, there) in enumerate(unit_rows_of((x - turn) % 4, x)):
                    rows_t[16 * there : 16 * there + 16] = far[16 * index : 16 * index + 16]

    lane = lax.broadcasted_iota(jnp.int32, (512, 128), 1)
    blocks, swapped = [], []
    for z in range(4):
        block = context[:, 128 * z : 128 * z + 128].astype(F32)
        blocks.append(block)
        swapped.append(pltpu.roll(block, HEAD, 1))
    lane_out = lax.broadcasted_iota(jnp.int32, (8, 16, 512), 2)
    for parity, out in ((core, keep), (1 - core, send)):
        grad = dot(rows_t[...], own_columns(normed, parity, 128))
        out[:, :48, :] = grad.astype(BF16).reshape(8, 48, 512)
        mine = (lane < HEAD) == (parity == 0)
        doubled = jnp.concatenate(
            [jnp.where(mine, block, other) for block, other in zip(blocks, swapped)], axis=1
        ).astype(BF16)
        grad = dot(cot_own[...], doubled).reshape(8, 32, 512)
        out[:, 48:, :] = jnp.where((lane_out & 127) < HEAD, grad[:, :16], grad[:, 16:]).astype(BF16)


def attend_kernel(
    lengths, queries, kv, before, after, cot_0, cot_1, cot_2, cot_3, context_out, d_query, d_before, d_after, d_own,
    d_contexts, key, value, key_t, value_t, scores, weights, d_scores, d_key, d_value
):
    place = locate(lengths)
    group_first, length = place[3], place[1]
    for turn, ref in enumerate((cot_0, cot_1, cot_2, cot_3)):
        d_contexts[slot(place, turn)] = ref[:, 1024:1152]
    for part, ref in enumerate((before, kv, after)):
        for piece in range(GROUP):
            start = 512 * part + ROWS * piece
            key_block = ref[piece, :, :128]
            value_block = ref[piece, :, 128:]
            key[start : start + ROWS] = key_block
            value[start : start + ROWS] = value_block
            key_t[:, start : start + ROWS] = key_block.T
            value_t[:, start : start + ROWS] = value_block.T
    d_key[...] = jnp.zeros_like(d_key)
    d_value[...] = jnp.zeros_like(d_value)
    lane = lax.broadcasted_iota(jnp.int32, (ROWS, 128), 1)
    first_head = lane < HEAD
    query_index = lax.broadcasted_iota(jnp.int32, (1, 256), 1)
    query_index = jnp.where(query_index < ROWS, query_index, query_index - ROWS)
    chunks = WINDOW // 128
    for block in range(GROUP):
        base = ROWS * block
        low = jnp.maximum(query_index, 512 - group_first - base)
        high = jnp.minimum(query_index + 1024, length - group_first + 511 - base)
        query = queries[block].astype(F32) * 0.125
        d_context = d_contexts[block].astype(F32)
        zero = jnp.zeros_like(query)
        query_pair = jnp.concatenate(
            [jnp.where(first_head, query, zero), jnp.where(first_head, zero, query)], axis=0
        ).astype(BF16)
        d_pair = jnp.concatenate(
            [jnp.where(first_head, d_context, zero), jnp.where(first_head, zero, d_context)], axis=0
        ).astype(BF16)

        def allowed_of(index):
            position = 128 * index + lax.broadcasted_iota(jnp.int32, (128, 256), 0)
            return (position >= low) & (position <= high)

        peak = jnp.full((128, 256), NEG_LARGE, F32)
        for index in range(chunks):
            part = dot(key[base + 128 * index : base + 128 * index + 128], query_pair, 1, 1)
            part = jnp.where(allowed_of(index), part, NEG_LARGE)
            scores[128 * index : 128 * index + 128] = part
            peak = jnp.maximum(peak, part)
        peak = jnp.max(peak, axis=0, keepdims=True)
        total = jnp.zeros((128, 256), F32)
        for index in range(chunks):
            part = scores[128 * index : 128 * index + 128]
            part = jnp.exp(part - peak)
            scores[128 * index : 128 * index + 128] = part
            total = total + part
        some = jnp.maximum(low, 0) <= jnp.minimum(high, WINDOW - 1)
        scale = jnp.where(some, 1.0 / jnp.maximum(jnp.sum(total, axis=0, keepdims=True), 1.0), 0.0)
        for index in range(chunks):
            part = scores[128 * index : 128 * index + 128] * scale
            weights[128 * index : 128 * index + 128] = part.astype(BF16)
        wide = dot(value_t[:, base : base + WINDOW], weights[...])
        context_t = jnp.concatenate([wide[:HEAD, :128], wide[HEAD:, 128:]], axis=0)
        context_out[block] = context_t.T.astype(BF16)
        product = context_t * d_context.T
        row_dot = jnp.concatenate(
            [
                jnp.sum(product[:HEAD], axis=0, keepdims=True),
                jnp.sum(product[HEAD:], axis=0, keepdims=True),
            ],
            axis=1,
        )
        for index in range(chunks):
            part = dot(value[base + 128 * index : base + 128 * index + 128], d_pair, 1, 1)
            part = weights[128 * index : 128 * index + 128].astype(F32) * (part - row_dot)
            d_scores[128 * index : 128 * index + 128] = part.astype(BF16)
        wide = dot(key_t[:, base : base + WINDOW], d_scores[...])
        d_query_t = jnp.concatenate([wide[:HEAD, :128], wide[HEAD:, 128:]], axis=0)
        d_query[:, base : base + 128] = (d_query_t * 0.125).astype(BF16)
        d_key[base : base + WINDOW] += dot(d_scores[...], query_pair)
        d_value[base : base + WINDOW] += dot(weights[...], d_pair)
    for piece in range(GROUP):
        for part, ref in enumerate((d_before, d_own, d_after)):
            start = 512 * part + ROWS * piece
            ref[piece, :, :128] = d_key[start : start + ROWS].astype(ref.dtype)
            ref[piece, :, 128:] = d_value[start : start + ROWS].astype(ref.dtype)


def unit_rows_of(source, target):
    units = [32 * part + 8 * source + row for part in range(3) for row in range(8)]
    wanted = [unit for unit in units if (unit // 3) % 4 == target]
    return [(units.index(unit), unit // 12 * 3 + unit % 3) for unit in wanted]


def join_kernel(
    lengths, context, d_query, own, from_before, from_after,
    unit_0, unit_1, unit_2, unit_3, back_0, back_1, back_2, back_3, joined_t
):
    place = locate(lengths)
    joined_t[:128] = d_query[...]
    for piece in range(GROUP):
        total = own[piece] + from_before[piece].astype(F32) + from_after[piece].astype(F32)
        total = total.astype(BF16)
        joined_t[128:256, 128 * piece : 128 * piece + 128] = total[:, :128].T
        joined_t[256:, 128 * piece : 128 * piece + 128] = total[:, 128:].T
    for turn, ref in enumerate((back_0, back_1, back_2, back_3)):
        ref[...] = joined_t[:, span((place[4] + turn) & 3, 128)]
    for ref in (unit_0, unit_1, unit_2, unit_3):
        for block in range(GROUP):
            ref[96:, 128 * block : 128 * block + 128] = context[block]
    for x in range(4):

        @pl.when(place[4] == x)
        def _():
            for turn, ref in enumerate((unit_0, unit_1, unit_2, unit_3)):
                for index, (here, _) in enumerate(unit_rows_of(x, (x + turn) % 4)):
                    ref[16 * index : 16 * index + 16] = joined_t[16 * here : 16 * here + 16]


def gate_rows_kernel(frames, gate, d_upper, w_up, w_down, layer_part, d_normed):
    gated = jnp.concatenate([gate[640 + 128 * m : 768 + 128 * m] for m in range(8)], axis=1)
    layer_part[...] = frames[...].astype(F32) + dot(gated, w_down[...])
    d_normed[...] = dot(d_upper[...], w_up[...], 1, 1)


def rows_kernel(
    lengths, frames, cotangent, far_0, far_1, far_2, far_3, back_0, back_1, back_2, back_3, layer_part, d_normed,
    w_qkv, w_out, layer_out, d_frames, context, joined_t
):
    place = locate(lengths)
    for turn, far in enumerate((far_0, far_1, far_2, far_3)):
        context[:, span(slot(place, turn), 128)] = far[96:, span(place[4], 128)]
    for turn, back in enumerate((back_0, back_1, back_2, back_3)):
        pair = slot(place, turn)
        for part in range(3):
            joined_t[span(pair + 4 * part, 128), :] = back[128 * part : 128 * part + 128]
    layer_out[...] = (layer_part[...] + dot(context[...], w_out[...])).astype(BF16)
    unit_rows, inverse = normalize(frames[...].astype(F32))
    d_rows = d_normed[...] + dot(joined_t[...].T, w_qkv[...], 1, 1)
    d_frames[...] = (cotangent[...].astype(F32) + norm_back(d_rows, unit_rows, inverse)).astype(BF16)


def add_kernel(gate, gate_far, attention, attention_far, out):
    out[:, :112] = (gate[...].astype(F32) + gate_far[...].astype(F32)).astype(BF16)
    out[:, 112:] = (attention[...].astype(F32) + attention_far[...].astype(F32)).astype(BF16)


def chunk_sum_kernel(lengths, parts, out_0, out_1, out_2, out_3, total):
    place = locate(lengths)
    for first in range(0, parts.shape[1], 16):
        rows = slice(first, first + 16)
        acc = parts[0, rows, :].astype(F32)
        for source in range(1, 8):
            acc = acc + parts[source, rows, :].astype(F32)
        for z in range(4):
            total[z, rows, :] = acc[:, 128 * z : 128 * z + 128].astype(BF16)
    for turn, ref in enumerate((out_0, out_1, out_2, out_3)):
        ref[...] = total[(place[5] + turn) & 3]


def final_kernel(lengths, part_0, part_1, part_2, part_3, g_qkv_t, g_out_t, g_up_t, g_down_t, g_taps, ordered):
    place = locate(lengths)
    for turn, ref in enumerate((part_0, part_1, part_2, part_3)):
        ordered[(place[5] + 4 - turn) & 3] = ref[...].astype(F32)
    total = (ordered[0] + ordered[1]) + (ordered[2] + ordered[3])
    g_up_t[...] = total[:64]
    g_down_t[...] = total[64:96]
    turned = total[96:112].T
    g_taps[...] = jnp.concatenate([turned[:TAPS], turned[32 : 32 + TAPS]], axis=1)
    g_qkv_t[...] = total[112:160]
    g_out_t[:16] = total[160:, :HEAD]
    g_out_t[16:] = total[160:, HEAD:]


SEQ = ("z_low", "y", "x")


def shift(array, by):
    return lax.ppermute(array, SEQ, [(i, i + by) for i in range(32) if 0 <= i + by < 32])


def other_core(array):
    return lax.ppermute(array, "core", [(0, 1), (1, 0)])


def turn_x(pieces):
    return [pieces[0]] + [
        lax.ppermute(pieces[by], "x", [(i, (i + by) % 4) for i in range(4)]) for by in range(1, 4)
    ]


def turn_z(pieces):
    return [pieces[0]] + [
        lax.ppermute(pieces[by], "z_high", [(i, (i + by) % 4) for i in range(4)]) for by in range(1, 4)
    ]


def local(frames, cotangent, lengths, w_qkv, w_out, w_up, w_down, conv_kernel):
    frames, cotangent = frames[0], cotangent[0]
    wide = ((ROWS, 1024), BF16)
    wide_f = ((ROWS, 1024), F32)
    quad = ((4, ROWS, 256), BF16)
    piece = ((ROWS, 1408), BF16)
    pieces = call(
        send_kernel, [piece] * 4, [pltpu.VMEM((ROWS, 512), BF16), pltpu.VMEM((1024, ROWS), BF16)], scalars=1
    )(lengths, *in_hbm(frames, cotangent, w_out))
    pieces, frames_later = lax.optimization_barrier((pieces, frames))
    in_x = turn_x(pieces)
    resid, d_gated, gating, d_conv, unit, inverse, slope, top, bottom = call(
        gate_kernel,
        [wide, wide, wide, wide, wide_f, ((ROWS, 128), F32), ((ROWS, 2048), F32),
         ((16, 2048), BF16), ((16, 2048), BF16)],
        scalars=1,
    )(lengths, *in_hbm(frames_later, cotangent, w_up, w_down))
    before, after = shift(bottom, 1), shift(top, -1)
    conv_in, d_gating_in, g_taps_in = call(
        conv_inner_kernel,
        [wide_f, wide_f, ((32, 1024), F32)],
        [pltpu.VMEM((8, 160, 128), F32), pltpu.VMEM((8, 160, 128), F32), pltpu.VMEM((32, 8, 1024), F32)],
    )(gating, d_conv, conv_kernel)
    in_x, conv_in, before, after = lax.optimization_barrier((in_x, conv_in, before, after))
    normed, query, kv = call(
        project_kernel, [((512, 1024), BF16), ((4, ROWS, 128), BF16), quad], scalars=1
    )(lengths, *in_x, w_qkv)
    kv_before, kv_after = shift(kv, 4), shift(kv, -4)
    conv_in, kv = lax.optimization_barrier((conv_in, kv))
    gate = ((1664, 128), BF16)
    d_upper, *gate_x = call(
        conv_outer_kernel,
        [((ROWS, 2048), BF16, HBM), gate, gate, gate, gate],
        [pltpu.VMEM((ROWS, 1024), F32), pltpu.VMEM((ROWS, 1024), F32),
         pltpu.VMEM((32, 2048), F32), pltpu.VMEM((32, 2048), F32),
         pltpu.VMEM((32, 1024), F32), pltpu.VMEM((2048, ROWS), BF16), pltpu.VMEM((32, 16, 128), BF16)],
        scalars=1,
    )(lengths, conv_in, d_gating_in, g_taps_in, d_conv, resid, d_gated, unit, inverse, slope, before, after, conv_kernel)
    gate_x, kv_before = lax.optimization_barrier((gate_x, kv_before))
    gate_x = turn_x(gate_x)
    context, d_query, d_before, d_after, d_own = call(
        attend_kernel,
        [((4, ROWS, 128), BF16), ((ROWS, 512), BF16), quad, quad, ((4, ROWS, 256), F32)],
        [pltpu.VMEM((4, ROWS, 128), BF16),
         pltpu.VMEM((1536, 128), BF16), pltpu.VMEM((1536, 128), BF16),
         pltpu.VMEM((128, 1536), BF16), pltpu.VMEM((128, 1536), BF16),
         pltpu.VMEM((WINDOW, 256), F32), pltpu.VMEM((WINDOW, 256), BF16), pltpu.VMEM((WINDOW, 256), BF16),
         pltpu.VMEM((1536, 128), F32), pltpu.VMEM((1536, 128), F32)],
        scalars=1,
    )(lengths, query, kv, kv_before, kv_after, *in_x)
    from_before, from_after = shift(d_after, 4), shift(d_before, -4)
    gate_x, d_own = lax.optimization_barrier((gate_x, d_own))
    small = ((384, 128), BF16)
    *far, back_0, back_1, back_2, back_3 = call(
        join_kernel, [((224, 512), BF16)] * 4 + [small + (HBM,)] * 4, [pltpu.VMEM((384, 512), BF16)], scalars=1
    )(lengths, context, d_query, d_own, from_before, from_after)
    far, gate_x = lax.optimization_barrier((far, gate_x))
    far_x = turn_x(far)
    keep, send, cot_own = call(
        gate_grads_kernel,
        [((8, 112, 512), BF16), ((8, 112, 512), BF16), ((256, 512), BF16)],
        [pltpu.VMEM((512, 512), BF16), pltpu.VMEM((512, 1024), BF16)],
        scalars=1,
    )(lengths, normed, *in_x, *gate_x)
    gate_far = other_core(send)
    attention_keep, send = call(
        attention_grads_kernel,
        [((8, 64, 512), BF16), ((8, 64, 512), BF16)],
        [pltpu.VMEM((512, 512), BF16), pltpu.VMEM((384, 512), BF16)],
        scalars=1,
    )(lengths, normed, cot_own, *far_x)
    send, frames_later, *back = lax.optimization_barrier((send, frames, back_0, back_1, back_2, back_3))
    back_x = turn_x(back)
    layer_part, d_normed = call(gate_rows_kernel, [wide_f, wide_f])(
        frames_later, gate_x[0], *in_hbm(d_upper, w_up, w_down)
    )
    (parts,) = call(add_kernel, [((8, 176, 512), BF16, HBM)])(keep, gate_far, attention_keep, other_core(send))
    parts = lax.all_to_all(parts, ("z_low", "y"), 0, 0)
    layer_out, d_frames = call(
        rows_kernel, [wide, wide], [pltpu.VMEM((ROWS, 512), BF16), pltpu.VMEM((1536, ROWS), BF16)], scalars=1
    )(
        lengths, frames, cotangent, *far_x, *back_x, layer_part, d_normed, *in_hbm(w_qkv, w_out)
    )
    parts, layer_out, d_frames = lax.optimization_barrier((parts, layer_out, d_frames))
    parts = call(
        chunk_sum_kernel, [((176, 128), BF16)] * 4, [pltpu.VMEM((4, 176, 128), BF16)], scalars=1
    )(lengths, parts)
    g_qkv, g_out, g_up, g_down, g_kernel = call(
        final_kernel,
        [((48, 128), F32), ((32, HEAD), F32), ((64, 128), F32), ((32, 128), F32), ((TAPS, 32), F32)],
        [pltpu.VMEM((4, 176, 128), F32)],
        scalars=1,
    )(lengths, *turn_z(parts))
    return (layer_out[None], d_frames[None], g_qkv.T, g_out.T, g_up.T, g_down.T, g_kernel)


def solution(mesh):
    split = Mesh(mesh.devices.reshape(2, 4, 4, 4, 2), SEQ + ("z_high", "core"))
    dp = ("z_high", "core")
    return jax.shard_map(
        local,
        mesh=split,
        in_specs=(P(dp, SEQ, None), P(dp, SEQ, None), P(dp), P(), P(), P(), P(), P()),
        out_specs=(
            P(dp, SEQ, None),
            P(dp, SEQ, None),
            P(dp, SEQ),
            P(dp, SEQ),
            P(dp, SEQ),
            P(dp, SEQ),
            P(None, SEQ),
        ),
        check_vma=False,
    )
```

```python
import jax
import jax.numpy as jnp
from jax import lax
from jax.experimental import pallas as pl
from jax.experimental.pallas import tpu as pltpu
from jax.sharding import Mesh, PartitionSpec as P

HEAD = 64
BAND = 512
ROWS = 128
GROUP = 4
WINDOW = 2 * BAND + ROWS
MARGIN = 15
TAPS = 31

EPSILON = 1e-05
NEG_LARGE = -3e38
HALF_ROOT = 0.7071067811865476
NORMAL_PEAK = 0.3989422804014327

BF16 = jnp.bfloat16
F32 = jnp.float32
HBM = pltpu.HBM
VMEM_LIMIT = 24 * 2**20


def call(body, outs, scratch=(), scalars=0, left=0):
    def run(*args):
        specs = [pl.BlockSpec(memory_space=pltpu.SMEM)] * scalars
        specs += [pl.BlockSpec(memory_space=pltpu.VMEM)] * (len(args) - scalars - left)
        specs += [pl.BlockSpec(memory_space=HBM)] * left
        return pl.pallas_call(
            body,
            out_shape=[
                HBM(*out[:2]) if len(out) > 2 else jax.ShapeDtypeStruct(*out) for out in outs
            ],
            in_specs=specs,
            out_specs=[pl.BlockSpec(memory_space=pltpu.VMEM)] * len(outs),
            scratch_shapes=list(scratch),
            compiler_params=pltpu.CompilerParams(vmem_limit_bytes=VMEM_LIMIT),
        )(*args)

    return run


def in_hbm(*arrays):
    return [pltpu.with_memory_space_constraint(array, HBM) for array in arrays]


def dot(left, right, left_dim=1, right_dim=0):
    return lax.dot_general(
        left, right, (((left_dim,), (right_dim,)), ((), ())), preferred_element_type=F32
    )


def normalize(values):
    centred = values - jnp.mean(values, axis=-1, keepdims=True)
    inverse = lax.rsqrt(jnp.mean(centred * centred, axis=-1, keepdims=True) + EPSILON)
    return (centred * inverse, inverse)


def norm_back(gradient, unit_rows, inverse):
    return inverse * (
        gradient
        - jnp.mean(gradient, axis=-1, keepdims=True)
        - unit_rows * jnp.mean(gradient * unit_rows, axis=-1, keepdims=True)
    )


def locate(lengths):
    z_low, y, x = lax.axis_index("z_low"), lax.axis_index("y"), lax.axis_index("x")
    row = 4 * z_low + y
    return ((4 * row + x) * ROWS, lengths[0], lax.axis_index("core"), row * (GROUP * ROWS), x, lax.axis_index("z_high"), y, z_low)


def slot(place, turn):
    return (place[4] + 4 - turn) & 3


def span(index, size):
    return pl.ds(pl.multiple_of(index * size, size), size)


def send_kernel(lengths, frames, cotangent, w_out, out_0, out_1, out_2, out_3, d_context, cot_t):
    place = locate(lengths)
    d_context[...] = dot(cotangent[...], w_out[...], 1, 1).astype(BF16)
    cot_t[...] = cotangent[...].T
    for turn, ref in enumerate((out_0, out_1, out_2, out_3)):
        x = (place[4] + turn) & 3
        ref[:, :1024] = frames[...]
        ref[:, 1024:1152] = d_context[:, span(x, 128)]
        for m in range(8):
            lanes = slice(1152 + 128 * (m // 4), 1280 + 128 * (m // 4))
            ref[32 * (m % 4) : 32 * (m % 4) + 32, lanes] = cot_t[span(4 * m + x, 32), :]


def project_kernel(lengths, frames_0, frames_1, frames_2, frames_3, w_qkv, normed, query, kv):
    place = locate(lengths)
    x = place[4]
    for turn, ref in enumerate((frames_0, frames_1, frames_2, frames_3)):
        unit_rows, _ = normalize(ref[:, :1024].astype(F32))
        normed[span(slot(place, turn), ROWS), :] = unit_rows.astype(BF16)
    weight = jnp.concatenate([w_qkv[:, span(x + 4 * part, 128)] for part in range(3)], axis=1)
    joined = dot(normed[...], weight).astype(BF16)
    query[...] = joined[:, :128].reshape(4, ROWS, 128)
    kv[...] = joined[:, 128:].reshape(4, ROWS, 256)


def gate_kernel(
    lengths, frames, cotangent, w_up, w_down,
    resid, d_gated, gating, d_conv, unit, inverse, slope, top, bottom,
    up, down, copied
):
    place = locate(lengths)
    first_frame, length = place[0], place[1]
    copies = [
        pltpu.make_async_copy(w_up.at[:, pl.ds(1024 * half, 1024)], up.at[half], copied.at[half]) for half in (1, 0)
    ] + [pltpu.make_async_copy(w_down, down, copied.at[2])]
    for copy in copies:
        copy.start()
    unit_rows, _ = normalize(frames[...].astype(F32))
    unit_rows = unit_rows.astype(BF16)
    hidden = [None, None]
    for half, copy in ((1, copies[0]), (0, copies[1])):
        copy.wait()
        upper = dot(unit_rows, up[half])
        phi = 0.5 * (1.0 + lax.erf(upper * HALF_ROOT))
        slope[:, 1024 * half : 1024 * half + 1024] = phi + upper * jnp.exp(-0.5 * upper * upper) * NORMAL_PEAK
        hidden[half] = (upper * phi).astype(BF16)
    gate_unit, gate_inv = normalize(hidden[1].astype(F32))
    unit[...] = gate_unit
    inverse[...] = jnp.broadcast_to(gate_inv, inverse.shape)
    rows = first_frame + lax.broadcasted_iota(jnp.int32, (ROWS, 1024), 0)
    masked = jnp.where(rows < length, gate_unit, 0.0).astype(BF16)
    gating[...] = masked
    resid[...] = hidden[0]
    copies[2].wait()
    back = dot(cotangent[...], down[...], 1, 1).astype(BF16)
    d_gated[...] = back
    conv_back = (back.astype(F32) * hidden[0].astype(F32)).astype(BF16)
    d_conv[...] = conv_back
    top[:, :1024] = masked[:16]
    top[:, 1024:] = conv_back[:16]
    bottom[:, :1024] = masked[112:]
    bottom[:, 1024:] = conv_back[112:]


def conv_inner_kernel(gating, d_conv, taps, conv_out, d_gating, g_taps, gate_ext, conv_ext, sums):
    for ext, ref in ((gate_ext, gating), (conv_ext, d_conv)):
        ext[:, :16] = jnp.zeros((8, 16, 128), F32)
        ext[:, 144:] = jnp.zeros((8, 16, 128), F32)
        for block in range(8):
            ext[block, 16:144] = ref[:, 128 * block : 128 * block + 128].astype(F32)
    sums[...] = jnp.zeros_like(sums)

    def chunk(index, _):
        lanes = pl.ds(pl.multiple_of(index * 128, 128), 128)
        for first in (0, 64):
            own = conv_ext[index, 16 + first : 80 + first, :]
            forward = jnp.zeros((64, 128), F32)
            for shift in range(8):
                moved = gate_ext[index, pl.ds(first + shift, 88), :]
                for step in range(4):
                    offset = 8 * step + shift
                    if 1 <= offset <= TAPS:
                        part = moved[8 * step : 8 * step + 64]
                        forward = forward + taps[offset - 1 : offset, lanes] * part
                        sums[offset - 1, :, lanes] += jnp.sum((part * own).reshape(8, 8, 128), axis=0)
            conv_out[first : first + 64, lanes] = forward
            backward = jnp.zeros((64, 128), F32)
            for shift in range(8):
                moved = conv_ext[index, pl.ds(first + shift, 88), :]
                for step in range(4):
                    offset = 8 * step + shift
                    if 1 <= offset <= TAPS:
                        part = moved[8 * step : 8 * step + 64]
                        backward = backward + taps[TAPS - offset : TAPS - offset + 1, lanes] * part
            d_gating[first : first + 64, lanes] = backward
        return 0

    lax.fori_loop(0, 8, chunk, 0)
    g_taps[...] = jnp.sum(sums[...], axis=1)


def conv_outer_kernel(
    lengths, conv_in, d_gating_in, g_taps_in, d_conv, resid, d_gated, unit, inverse, slope, before, after, taps,
    d_upper, out_0, out_1, out_2, out_3, conv_out, d_gating, before_ext, after_ext, g_taps, d_upper_t, g_taps_t
):
    place = locate(lengths)
    first_frame, length = place[0], place[1]
    conv_out[...] = conv_in[...]
    d_gating[...] = d_gating_in[...]
    g_taps[...] = g_taps_in[...]
    before_ext[:, 16:] = jnp.zeros((16, 16, 128), F32)
    after_ext[:, :16] = jnp.zeros((16, 16, 128), F32)
    for block in range(16):
        before_ext[block, :16] = before[:, 128 * block : 128 * block + 128].astype(F32)
        after_ext[block, 16:] = after[:, 128 * block : 128 * block + 128].astype(F32)

    def chunk(index, _):
        lanes = pl.ds(pl.multiple_of(index * 128, 128), 128)
        for ext, first, skip in ((before_ext, 0, 0), (after_ext, 112, 16)):
            own = d_conv[first : first + 16, lanes].astype(F32)
            forward = conv_out[first : first + 16, lanes]
            backward = d_gating[first : first + 16, lanes]
            for step in range(1, 16):
                offset = step + skip
                part = ext[index, pl.ds(step, 16), :]
                forward = forward + taps[offset - 1 : offset, lanes] * part
                g_taps[offset - 1 : offset, lanes] += jnp.sum(part * own, axis=0, keepdims=True)
                part = ext[index + 8, pl.ds(step, 16), :]
                backward = backward + taps[TAPS - offset : TAPS - offset + 1, lanes] * part
            conv_out[first : first + 16, lanes] = forward
            d_gating[first : first + 16, lanes] = backward
        return 0

    lax.fori_loop(0, 8, chunk, 0)
    conv = conv_out[...]
    gated = (resid[...].astype(F32) * conv).astype(BF16)
    rows = first_frame + lax.broadcasted_iota(jnp.int32, (ROWS, 1024), 0)
    d_gate = jnp.where(rows < length, d_gating[...], 0.0)
    d_gate = norm_back(d_gate, unit[...], inverse[:, :1])
    left = (d_gated[...].astype(F32) * conv * slope[:, :1024]).astype(BF16)
    right = (d_gate * slope[:, 1024:]).astype(BF16)
    d_upper[:, :1024] = left
    d_upper[:, 1024:] = right
    d_upper_t[:1024] = left.T
    d_upper_t[1024:] = right.T
    turned = jnp.concatenate([g_taps[...], jnp.zeros((96, 1024), F32)], axis=0).T.reshape(32, 32, 128)
    g_taps_t[...] = (turned[:, :16, :] + pltpu.roll(turned[:, 16:, :], 32, 2)).astype(BF16)
    for turn, ref in enumerate((out_0, out_1, out_2, out_3)):
        x = (place[4] + turn) & 3
        for m in range(8):
            ref[64 * m : 64 * m + 64] = d_upper_t[span(4 * m + x, 64), :]
            ref[512 + 16 * m : 528 + 16 * m] = g_taps_t[4 * m + x]
            ref[640 + 128 * m : 768 + 128 * m] = gated[:, 128 * m : 128 * m + 128]


def own_columns(array, core, width):
    parts = [
        array[:, pl.ds(pl.multiple_of(2 * width * z + width * core, width), width)] for z in range(4)
    ]
    return jnp.concatenate(parts, axis=1)


def gate_grads_kernel(
    lengths, normed, cot_0, cot_1, cot_2, cot_3, gate_0, gate_1, gate_2, gate_3,
    keep, send, cot_own, d_upper_t, gated
):
    place = locate(lengths)
    x, core = place[4], place[2]
    gates = (gate_0, gate_1, gate_2, gate_3)
    g_taps = gate_0[512:640].astype(F32)
    for ref in gates[1:]:
        g_taps = g_taps + ref[512:640].astype(F32)
    g_taps = g_taps.astype(BF16).reshape(8, 16, 128)
    for turn, (gate, cot) in enumerate(zip(gates, (cot_0, cot_1, cot_2, cot_3))):
        here = span(slot(place, turn), 128)
        d_upper_t[:, here] = gate[:512]
        for block in range(8):
            gated[here, 128 * block : 128 * block + 128] = gate[640 + 128 * block : 768 + 128 * block]
        cot_own[:128, here] = cot[:, 1152:1280]
        cot_own[128:, here] = cot[:, 1280:]
    for parity, out in ((core, keep), (1 - core, send)):
        grad = dot(d_upper_t[...], own_columns(normed, parity, 128))
        out[:, :64, :] = grad.astype(BF16).reshape(8, 64, 512)
        grad = dot(cot_own[...], own_columns(gated, parity, 128))
        out[:, 64:96, :] = grad.astype(BF16).reshape(8, 32, 512)
        for z in range(4):
            out[:, 96:, 128 * z : 128 * z + 128] = g_taps


def attention_grads_kernel(
    lengths, normed, cot_own, far_0, far_1, far_2, far_3,
    keep, send, context, rows_t
):
    place = locate(lengths)
    core = place[2]
    for turn, far in enumerate((far_0, far_1, far_2, far_3)):
        for block in range(GROUP):
            tokens = slice(128 * block, 128 * block + 128)
            context[tokens, span(slot(place, turn), 128)] = far[96:224, tokens]
    for x in range(4):

        @pl.when(place[4] == x)
        def _():
            for turn, far in enumerate((far_0, far_1, far_2, far_3)):
                for index, (_, there) in enumerate(unit_rows_of((x - turn) % 4, x)):
                    rows_t[16 * there : 16 * there + 16] = far[16 * index : 16 * index + 16]

    lane = lax.broadcasted_iota(jnp.int32, (512, 128), 1)
    blocks, swapped = [], []
    for z in range(4):
        block = context[:, 128 * z : 128 * z + 128].astype(F32)
        blocks.append(block)
        swapped.append(pltpu.roll(block, HEAD, 1))
    lane_out = lax.broadcasted_iota(jnp.int32, (8, 16, 512), 2)
    for parity, out in ((core, keep), (1 - core, send)):
        grad = dot(rows_t[...], own_columns(normed, parity, 128))
        out[:, :48, :] = grad.astype(BF16).reshape(8, 48, 512)
        mine = (lane < HEAD) == (parity == 0)
        doubled = jnp.concatenate(
            [jnp.where(mine, block, other) for block, other in zip(blocks, swapped)], axis=1
        ).astype(BF16)
        grad = dot(cot_own[...], doubled).reshape(8, 32, 512)
        out[:, 48:, :] = jnp.where((lane_out & 127) < HEAD, grad[:, :16], grad[:, 16:]).astype(BF16)


def attend_kernel(
    lengths, queries, kv, before, after, cot_0, cot_1, cot_2, cot_3, context_out, d_query, d_before, d_after, d_own,
    d_contexts, key, value, key_t, value_t, scores, weights, d_scores, d_key, d_value
):
    place = locate(lengths)
    group_first, length = place[3], place[1]
    for turn, ref in enumerate((cot_0, cot_1, cot_2, cot_3)):
        d_contexts[slot(place, turn)] = ref[:, 1024:1152]
    for part, ref in enumerate((before, kv, after)):
        for piece in range(GROUP):
            start = 512 * part + ROWS * piece
            key_block = ref[piece, :, :128]
            value_block = ref[piece, :, 128:]
            key[start : start + ROWS] = key_block
            value[start : start + ROWS] = value_block
            key_t[:, start : start + ROWS] = key_block.T
            value_t[:, start : start + ROWS] = value_block.T
    d_key[...] = jnp.zeros_like(d_key)
    d_value[...] = jnp.zeros_like(d_value)
    lane = lax.broadcasted_iota(jnp.int32, (ROWS, 128), 1)
    first_head = lane < HEAD
    query_index = lax.broadcasted_iota(jnp.int32, (1, 256), 1)
    query_index = jnp.where(query_index < ROWS, query_index, query_index - ROWS)
    chunks = WINDOW // 128
    for block in range(GROUP):
        base = ROWS * block
        low = jnp.maximum(query_index, 512 - group_first - base)
        high = jnp.minimum(query_index + 1024, length - group_first + 511 - base)
        query = queries[block].astype(F32) * 0.125
        d_context = d_contexts[block].astype(F32)
        zero = jnp.zeros_like(query)
        query_pair = jnp.concatenate(
            [jnp.where(first_head, query, zero), jnp.where(first_head, zero, query)], axis=0
        ).astype(BF16)
        d_pair = jnp.concatenate(
            [jnp.where(first_head, d_context, zero), jnp.where(first_head, zero, d_context)], axis=0
        ).astype(BF16)

        def allowed_of(index):
            position = 128 * index + lax.broadcasted_iota(jnp.int32, (128, 256), 0)
            return (position >= low) & (position <= high)

        peak = jnp.full((128, 256), NEG_LARGE, F32)
        for index in range(chunks):
            part = dot(key[base + 128 * index : base + 128 * index + 128], query_pair, 1, 1)
            part = jnp.where(allowed_of(index), part, NEG_LARGE)
            scores[128 * index : 128 * index + 128] = part
            peak = jnp.maximum(peak, part)
        peak = jnp.max(peak, axis=0, keepdims=True)
        total = jnp.zeros((128, 256), F32)
        for index in range(chunks):
            part = scores[128 * index : 128 * index + 128]
            part = jnp.exp(part - peak)
            scores[128 * index : 128 * index + 128] = part
            total = total + part
        some = jnp.maximum(low, 0) <= jnp.minimum(high, WINDOW - 1)
        scale = jnp.where(some, 1.0 / jnp.maximum(jnp.sum(total, axis=0, keepdims=True), 1.0), 0.0)
        for index in range(chunks):
            part = scores[128 * index : 128 * index + 128] * scale
            weights[128 * index : 128 * index + 128] = part.astype(BF16)
        wide = dot(value_t[:, base : base + WINDOW], weights[...])
        context_t = jnp.concatenate([wide[:HEAD, :128], wide[HEAD:, 128:]], axis=0)
        context_out[block] = context_t.T.astype(BF16)
        product = context_t * d_context.T
        row_dot = jnp.concatenate(
            [
                jnp.sum(product[:HEAD], axis=0, keepdims=True),
                jnp.sum(product[HEAD:], axis=0, keepdims=True),
            ],
            axis=1,
        )
        for index in range(chunks):
            part = dot(value[base + 128 * index : base + 128 * index + 128], d_pair, 1, 1)
            part = weights[128 * index : 128 * index + 128].astype(F32) * (part - row_dot)
            d_scores[128 * index : 128 * index + 128] = part.astype(BF16)
        wide = dot(key_t[:, base : base + WINDOW], d_scores[...])
        d_query_t = jnp.concatenate([wide[:HEAD, :128], wide[HEAD:, 128:]], axis=0)
        d_query[:, base : base + 128] = (d_query_t * 0.125).astype(BF16)
        d_key[base : base + WINDOW] += dot(d_scores[...], query_pair)
        d_value[base : base + WINDOW] += dot(weights[...], d_pair)
    for piece in range(GROUP):
        for part, ref in enumerate((d_before, d_own, d_after)):
            start = 512 * part + ROWS * piece
            ref[piece, :, :128] = d_key[start : start + ROWS].astype(ref.dtype)
            ref[piece, :, 128:] = d_value[start : start + ROWS].astype(ref.dtype)


def unit_rows_of(source, target):
    units = [32 * part + 8 * source + row for part in range(3) for row in range(8)]
    wanted = [unit for unit in units if (unit // 3) % 4 == target]
    return [(units.index(unit), unit // 12 * 3 + unit % 3) for unit in wanted]


def join_kernel(
    lengths, context, d_query, own, from_before, from_after,
    unit_0, unit_1, unit_2, unit_3, joined_t
):
    place = locate(lengths)
    joined_t[:128] = d_query[...]
    for piece in range(GROUP):
        total = own[piece] + from_before[piece].astype(F32) + from_after[piece].astype(F32)
        total = total.astype(BF16)
        joined_t[128:256, 128 * piece : 128 * piece + 128] = total[:, :128].T
        joined_t[256:, 128 * piece : 128 * piece + 128] = total[:, 128:].T
    for turn, ref in enumerate((unit_0, unit_1, unit_2, unit_3)):
        for block in range(GROUP):
            lanes = slice(128 * block, 128 * block + 128)
            ref[96:224, lanes] = context[block]
            ref[224:, lanes] = joined_t[96 * block : 96 * block + 96, span((place[4] + turn) & 3, 128)]
    for x in range(4):

        @pl.when(place[4] == x)
        def _():
            for turn, ref in enumerate((unit_0, unit_1, unit_2, unit_3)):
                for index, (here, _) in enumerate(unit_rows_of(x, (x + turn) % 4)):
                    ref[16 * index : 16 * index + 16] = joined_t[16 * here : 16 * here + 16]


def gate_rows_kernel(frames, gate, d_upper, w_up, w_down, layer_part, d_normed):
    gated = jnp.concatenate([gate[640 + 128 * m : 768 + 128 * m] for m in range(8)], axis=1)
    layer_part[...] = frames[...].astype(F32) + dot(gated, w_down[...])
    d_normed[...] = dot(d_upper[...], w_up[...], 1, 1)


def rows_kernel(
    lengths, frames, cotangent, far_0, far_1, far_2, far_3, layer_part, d_normed,
    w_qkv, w_out, layer_out, d_frames, context, joined_t, back
):
    place = locate(lengths)
    for turn, far in enumerate((far_0, far_1, far_2, far_3)):
        pair = slot(place, turn)
        context[:, span(pair, 128)] = far[96:224, span(place[4], 128)]
        for block in range(4):
            back[96 * block : 96 * block + 96] = far[224:, 128 * block : 128 * block + 128]
        for part in range(3):
            joined_t[span(pair + 4 * part, 128), :] = back[128 * part : 128 * part + 128]
    layer_out[...] = (layer_part[...] + dot(context[...], w_out[...])).astype(BF16)
    unit_rows, inverse = normalize(frames[...].astype(F32))
    d_rows = d_normed[...] + dot(joined_t[...].T, w_qkv[...], 1, 1)
    d_frames[...] = (cotangent[...].astype(F32) + norm_back(d_rows, unit_rows, inverse)).astype(BF16)


def add_kernel(near, far, out):
    out[...] = (near[...].astype(F32) + far[...].astype(F32)).astype(BF16)


def turn_add_kernel(lengths, near, far, out_0, out_1, out_2, out_3):
    place = locate(lengths)
    for turn, ref in enumerate((out_0, out_1, out_2, out_3)):
        for z_low in range(2):
            m = 4 * z_low + ((place[6] + turn) & 3)
            ref[z_low] = (near[m].astype(F32) + far[m].astype(F32)).astype(BF16)


def gate_sum_kernel(lengths, part_0, part_1, part_2, part_3, keep, send):
    place = locate(lengths)
    for out, z_low in ((keep, place[7]), (send, 1 - place[7])):
        total = part_0[z_low].astype(F32)
        for part in (part_1, part_2, part_3):
            total = total + part[z_low].astype(F32)
        out[...] = total.astype(BF16)


def chunk_sum_kernel(lengths, gate, gate_far, parts, out_0, out_1, out_2, out_3, total):
    place = locate(lengths)
    for first in range(0, 176, 16):
        rows = slice(first, first + 16)
        if first < 112:
            acc = gate[rows].astype(F32) + gate_far[rows].astype(F32)
        else:
            acc = parts[0, first - 112 : first - 96].astype(F32)
            for source in range(1, 8):
                acc = acc + parts[source, first - 112 : first - 96].astype(F32)
        for z in range(4):
            total[z, rows, :] = acc[:, 128 * z : 128 * z + 128].astype(BF16)
    for turn, ref in enumerate((out_0, out_1, out_2, out_3)):
        ref[...] = total[(place[5] + turn) & 3]


def final_kernel(lengths, part_0, part_1, part_2, part_3, g_qkv_t, g_out_t, g_up_t, g_down_t, g_taps, ordered):
    place = locate(lengths)
    for turn, ref in enumerate((part_0, part_1, part_2, part_3)):
        ordered[(place[5] + 4 - turn) & 3] = ref[...].astype(F32)
    total = (ordered[0] + ordered[1]) + (ordered[2] + ordered[3])
    g_up_t[...] = total[:64]
    g_down_t[...] = total[64:96]
    turned = total[96:112].T
    g_taps[...] = jnp.concatenate([turned[:TAPS], turned[32 : 32 + TAPS]], axis=1)
    g_qkv_t[...] = total[112:160]
    g_out_t[:16] = total[160:, :HEAD]
    g_out_t[16:] = total[160:, HEAD:]


SEQ = ("z_low", "y", "x")


def shift(array, by):
    return lax.ppermute(array, SEQ, [(i, i + by) for i in range(32) if 0 <= i + by < 32])


def other_core(array):
    return lax.ppermute(array, "core", [(0, 1), (1, 0)])


def turn_x(pieces):
    return [pieces[0]] + [
        lax.ppermute(pieces[by], "x", [(i, (i + by) % 4) for i in range(4)]) for by in range(1, 4)
    ]


def turn_y(pieces):
    return [pieces[0]] + [
        lax.ppermute(pieces[by], "y", [(i, (i + by) % 4) for i in range(4)]) for by in range(1, 4)
    ]


def turn_z(pieces):
    return [pieces[0]] + [
        lax.ppermute(pieces[by], "z_high", [(i, (i + by) % 4) for i in range(4)]) for by in range(1, 4)
    ]


def local(frames, cotangent, lengths, w_qkv, w_out, w_up, w_down, conv_kernel):
    frames, cotangent = frames[0], cotangent[0]
    wide = ((ROWS, 1024), BF16)
    wide_f = ((ROWS, 1024), F32)
    quad = ((4, ROWS, 256), BF16)
    piece = ((ROWS, 1408), BF16)
    pieces = call(
        send_kernel, [piece] * 4, [pltpu.VMEM((ROWS, 512), BF16), pltpu.VMEM((1024, ROWS), BF16)], scalars=1
    )(lengths, *in_hbm(frames, cotangent, w_out))
    pieces, frames_later = lax.optimization_barrier((pieces, frames))
    in_x = turn_x(pieces)
    resid, d_gated, gating, d_conv, unit, inverse, slope, top, bottom = call(
        gate_kernel,
        [wide, wide, wide, wide, wide_f, ((ROWS, 128), F32), ((ROWS, 2048), F32),
         ((16, 2048), BF16), ((16, 2048), BF16)],
        [pltpu.VMEM((2, 1024, 1024), BF16), pltpu.VMEM((1024, 1024), BF16), pltpu.SemaphoreType.DMA((3,))],
        scalars=1,
        left=2,
    )(lengths, *in_hbm(frames_later, cotangent, w_up, w_down))
    before, after = shift(bottom, 1), shift(top, -1)
    conv_in, d_gating_in, g_taps_in = call(
        conv_inner_kernel,
        [wide_f, wide_f, ((32, 1024), F32)],
        [pltpu.VMEM((8, 160, 128), F32), pltpu.VMEM((8, 160, 128), F32), pltpu.VMEM((32, 8, 1024), F32)],
    )(gating, d_conv, conv_kernel)
    in_x, conv_in, before, after = lax.optimization_barrier((in_x, conv_in, before, after))
    normed, query, kv = call(
        project_kernel, [((512, 1024), BF16), ((4, ROWS, 128), BF16), quad], scalars=1
    )(lengths, *in_x, w_qkv)
    kv_before, kv_after = shift(kv, 4), shift(kv, -4)
    conv_in, kv = lax.optimization_barrier((conv_in, kv))
    gate = ((1664, 128), BF16)
    d_upper, *gate_x = call(
        conv_outer_kernel,
        [((ROWS, 2048), BF16, HBM), gate, gate, gate, gate],
        [pltpu.VMEM((ROWS, 1024), F32), pltpu.VMEM((ROWS, 1024), F32),
         pltpu.VMEM((16, 32, 128), F32), pltpu.VMEM((16, 32, 128), F32),
         pltpu.VMEM((32, 1024), F32), pltpu.VMEM((2048, ROWS), BF16), pltpu.VMEM((32, 16, 128), BF16)],
        scalars=1,
    )(lengths, conv_in, d_gating_in, g_taps_in, d_conv, resid, d_gated, unit, inverse, slope, before, after, conv_kernel)
    gate_x, kv_before = lax.optimization_barrier((gate_x, kv_before))
    gate_x = turn_x(gate_x)
    context, d_query, d_before, d_after, d_own = call(
        attend_kernel,
        [((4, ROWS, 128), BF16), ((ROWS, 512), BF16), quad, quad, ((4, ROWS, 256), F32)],
        [pltpu.VMEM((4, ROWS, 128), BF16),
         pltpu.VMEM((1536, 128), BF16), pltpu.VMEM((1536, 128), BF16),
         pltpu.VMEM((128, 1536), BF16), pltpu.VMEM((128, 1536), BF16),
         pltpu.VMEM((WINDOW, 256), F32), pltpu.VMEM((WINDOW, 256), BF16), pltpu.VMEM((WINDOW, 256), BF16),
         pltpu.VMEM((1536, 128), F32), pltpu.VMEM((1536, 128), F32)],
        scalars=1,
    )(lengths, query, kv, kv_before, kv_after, *in_x)
    from_before, from_after = shift(d_after, 4), shift(d_before, -4)
    frames_later, d_own = lax.optimization_barrier((frames, d_own))
    layer_part, d_normed = call(gate_rows_kernel, [wide_f + (HBM,), wide_f + (HBM,)])(
        *in_hbm(frames_later), gate_x[0], *in_hbm(d_upper), w_up, w_down
    )
    gate_x, d_normed, d_own = lax.optimization_barrier((gate_x, d_normed, d_own))
    far = call(join_kernel, [((320, 512), BF16)] * 4, [pltpu.VMEM((384, 512), BF16)], scalars=1)(
        lengths, context, d_query, d_own, from_before, from_after
    )
    far, gate_x = lax.optimization_barrier((far, gate_x))
    far_x = turn_x(far)
    keep, send, cot_own = call(
        gate_grads_kernel,
        [((8, 112, 512), BF16), ((8, 112, 512), BF16), ((256, 512), BF16)],
        [pltpu.VMEM((512, 512), BF16), pltpu.VMEM((512, 1024), BF16)],
        scalars=1,
    )(lengths, normed, *in_x, *gate_x)
    gate_y = turn_y(
        call(turn_add_kernel, [((2, 112, 512), BF16)] * 4, scalars=1)(lengths, keep, other_core(send))
    )
    far_x, gate_y = lax.optimization_barrier((far_x, gate_y))
    attention_keep, send = call(
        attention_grads_kernel,
        [((8, 64, 512), BF16), ((8, 64, 512), BF16)],
        [pltpu.VMEM((512, 512), BF16), pltpu.VMEM((384, 512), BF16)],
        scalars=1,
    )(lengths, normed, cot_own, *far_x)
    send, gate_y = lax.optimization_barrier((send, gate_y))
    gate_keep, gate_send = call(gate_sum_kernel, [((112, 512), BF16, HBM)] * 2, scalars=1)(lengths, *gate_y)
    attention_keep, gate_send = lax.optimization_barrier((attention_keep, gate_send))
    (parts,) = call(add_kernel, [((8, 64, 512), BF16, HBM)])(attention_keep, other_core(send))
    parts = lax.all_to_all(parts, ("z_low", "y"), 0, 0)
    gate_far = lax.ppermute(gate_send, "z_low", [(0, 1), (1, 0)])
    layer_out, d_frames = call(
        rows_kernel,
        [wide, wide],
        [pltpu.VMEM((ROWS, 512), BF16), pltpu.VMEM((1536, ROWS), BF16), pltpu.VMEM((384, ROWS), BF16)],
        scalars=1,
    )(
        lengths, frames, cotangent, *far_x, layer_part, d_normed, *in_hbm(w_qkv, w_out)
    )
    parts, layer_out, d_frames = lax.optimization_barrier((parts, layer_out, d_frames))
    parts = call(
        chunk_sum_kernel, [((176, 128), BF16)] * 4, [pltpu.VMEM((4, 176, 128), BF16)], scalars=1
    )(lengths, gate_keep, gate_far, parts)
    g_qkv, g_out, g_up, g_down, g_kernel = call(
        final_kernel,
        [((48, 128), F32), ((32, HEAD), F32), ((64, 128), F32), ((32, 128), F32), ((TAPS, 32), F32)],
        [pltpu.VMEM((4, 176, 128), F32)],
        scalars=1,
    )(lengths, *turn_z(parts))
    return (layer_out[None], d_frames[None], g_qkv.T, g_out.T, g_up.T, g_down.T, g_kernel)


def solution(mesh):
    split = Mesh(mesh.devices.reshape(2, 4, 4, 4, 2), SEQ + ("z_high", "core"))
    dp = ("z_high", "core")
    return jax.shard_map(
        local,
        mesh=split,
        in_specs=(P(dp, SEQ, None), P(dp, SEQ, None), P(dp), P(), P(), P(), P(), P()),
        out_specs=(
            P(dp, SEQ, None),
            P(dp, SEQ, None),
            P(dp, SEQ),
            P(dp, SEQ),
            P(dp, SEQ),
            P(dp, SEQ),
            P(None, SEQ),
        ),
        check_vma=False,
    )
```

```python
import jax
import jax.numpy as jnp
from jax import lax
from jax.experimental import pallas as pl
from jax.experimental.pallas import tpu as pltpu
from jax.sharding import Mesh, PartitionSpec as P

HEAD = 64
BAND = 512
ROWS = 128
GROUP = 4
WINDOW = 2 * BAND + ROWS
MARGIN = 15
TAPS = 31

EPSILON = 1e-05
NEG_LARGE = -3e38
HALF_ROOT = 0.7071067811865476
NORMAL_PEAK = 0.3989422804014327

BF16 = jnp.bfloat16
F32 = jnp.float32
HBM = pltpu.HBM
VMEM_LIMIT = 24 * 2**20


def call(body, outs, scratch=(), scalars=0, left=0):
    def run(*args):
        specs = [pl.BlockSpec(memory_space=pltpu.SMEM)] * scalars
        specs += [pl.BlockSpec(memory_space=pltpu.VMEM)] * (len(args) - scalars - left)
        specs += [pl.BlockSpec(memory_space=HBM)] * left
        return pl.pallas_call(
            body,
            out_shape=[
                HBM(*out[:2]) if len(out) > 2 else jax.ShapeDtypeStruct(*out) for out in outs
            ],
            in_specs=specs,
            out_specs=[pl.BlockSpec(memory_space=pltpu.VMEM)] * len(outs),
            scratch_shapes=list(scratch),
            compiler_params=pltpu.CompilerParams(vmem_limit_bytes=VMEM_LIMIT),
        )(*args)

    return run


def in_hbm(*arrays):
    return [pltpu.with_memory_space_constraint(array, HBM) for array in arrays]


def dot(left, right, left_dim=1, right_dim=0):
    return lax.dot_general(
        left, right, (((left_dim,), (right_dim,)), ((), ())), preferred_element_type=F32
    )


def normalize(values):
    centred = values - jnp.mean(values, axis=-1, keepdims=True)
    inverse = lax.rsqrt(jnp.mean(centred * centred, axis=-1, keepdims=True) + EPSILON)
    return (centred * inverse, inverse)


def norm_back(gradient, unit_rows, inverse):
    return inverse * (
        gradient
        - jnp.mean(gradient, axis=-1, keepdims=True)
        - unit_rows * jnp.mean(gradient * unit_rows, axis=-1, keepdims=True)
    )


def locate(lengths):
    z_low, y, x = lax.axis_index("z_low"), lax.axis_index("y"), lax.axis_index("x")
    row = 4 * z_low + y
    return ((4 * row + x) * ROWS, lengths[0], lax.axis_index("core"), row * (GROUP * ROWS), x, lax.axis_index("z_high"), y, z_low)


def slot(place, turn):
    return (place[4] + 4 - turn) & 3


def span(index, size):
    return pl.ds(pl.multiple_of(index * size, size), size)


def send_kernel(lengths, frames, cotangent, w_out, out_0, out_1, out_2, out_3, d_context, cot_t):
    place = locate(lengths)
    d_context[...] = dot(cotangent[...], w_out[...], 1, 1).astype(BF16)
    cot_t[...] = cotangent[...].T
    for turn, ref in enumerate((out_0, out_1, out_2, out_3)):
        x = (place[4] + turn) & 3
        ref[:, :1024] = frames[...]
        ref[:, 1024:1152] = d_context[:, span(x, 128)]
        for m in range(8):
            lanes = slice(1152 + 128 * (m // 4), 1280 + 128 * (m // 4))
            ref[32 * (m % 4) : 32 * (m % 4) + 32, lanes] = cot_t[span(4 * m + x, 32), :]


def project_kernel(lengths, frames_0, frames_1, frames_2, frames_3, w_qkv, normed, query, kv):
    place = locate(lengths)
    x = place[4]
    for turn, ref in enumerate((frames_0, frames_1, frames_2, frames_3)):
        unit_rows, _ = normalize(ref[:, :1024].astype(F32))
        normed[span(slot(place, turn), ROWS), :] = unit_rows.astype(BF16)
    weight = jnp.concatenate([w_qkv[:, span(x + 4 * part, 128)] for part in range(3)], axis=1)
    joined = dot(normed[...], weight).astype(BF16)
    query[...] = joined[:, :128].reshape(4, ROWS, 128)
    kv[...] = joined[:, 128:].reshape(4, ROWS, 256)


def gate_kernel(
    lengths, frames, cotangent, w_up, w_down,
    resid, d_gated, gating, d_conv, unit, inverse, slope, top, bottom,
    up, down, copied
):
    place = locate(lengths)
    first_frame, length = place[0], place[1]
    copies = [
        pltpu.make_async_copy(w_up.at[:, pl.ds(1024 * half, 1024)], up.at[half], copied.at[half]) for half in (1, 0)
    ] + [pltpu.make_async_copy(w_down, down, copied.at[2])]
    for copy in copies:
        copy.start()
    unit_rows, _ = normalize(frames[...].astype(F32))
    unit_rows = unit_rows.astype(BF16)
    hidden = [None, None]
    for half, copy in ((1, copies[0]), (0, copies[1])):
        copy.wait()
        upper = dot(unit_rows, up[half])
        phi = 0.5 * (1.0 + lax.erf(upper * HALF_ROOT))
        slope[:, 1024 * half : 1024 * half + 1024] = phi + upper * jnp.exp(-0.5 * upper * upper) * NORMAL_PEAK
        hidden[half] = (upper * phi).astype(BF16)
    gate_unit, gate_inv = normalize(hidden[1].astype(F32))
    unit[...] = gate_unit
    inverse[...] = jnp.broadcast_to(gate_inv, inverse.shape)
    rows = first_frame + lax.broadcasted_iota(jnp.int32, (ROWS, 1024), 0)
    masked = jnp.where(rows < length, gate_unit, 0.0).astype(BF16)
    gating[...] = masked
    resid[...] = hidden[0]
    copies[2].wait()
    back = dot(cotangent[...], down[...], 1, 1).astype(BF16)
    d_gated[...] = back
    conv_back = (back.astype(F32) * hidden[0].astype(F32)).astype(BF16)
    d_conv[...] = conv_back
    top[:, :1024] = masked[:16]
    top[:, 1024:] = conv_back[:16]
    bottom[:, :1024] = masked[112:]
    bottom[:, 1024:] = conv_back[112:]


def conv_inner_kernel(gating, d_conv, taps, conv_out, d_gating, g_taps, gate_ext, conv_ext, sums):
    for ext, ref in ((gate_ext, gating), (conv_ext, d_conv)):
        ext[:, :16] = jnp.zeros((8, 16, 128), F32)
        ext[:, 144:] = jnp.zeros((8, 16, 128), F32)
        for block in range(8):
            ext[block, 16:144] = ref[:, 128 * block : 128 * block + 128].astype(F32)
    sums[...] = jnp.zeros_like(sums)

    def chunk(index, _):
        lanes = pl.ds(pl.multiple_of(index * 128, 128), 128)
        for first in (0, 64):
            own = conv_ext[index, 16 + first : 80 + first, :]
            forward = jnp.zeros((64, 128), F32)
            for shift in range(8):
                moved = gate_ext[index, pl.ds(first + shift, 88), :]
                for step in range(4):
                    offset = 8 * step + shift
                    if 1 <= offset <= TAPS:
                        part = moved[8 * step : 8 * step + 64]
                        forward = forward + taps[offset - 1 : offset, lanes] * part
                        sums[offset - 1, :, lanes] += jnp.sum((part * own).reshape(8, 8, 128), axis=0)
            conv_out[first : first + 64, lanes] = forward
            backward = jnp.zeros((64, 128), F32)
            for shift in range(8):
                moved = conv_ext[index, pl.ds(first + shift, 88), :]
                for step in range(4):
                    offset = 8 * step + shift
                    if 1 <= offset <= TAPS:
                        part = moved[8 * step : 8 * step + 64]
                        backward = backward + taps[TAPS - offset : TAPS - offset + 1, lanes] * part
            d_gating[first : first + 64, lanes] = backward
        return 0

    lax.fori_loop(0, 8, chunk, 0)
    g_taps[...] = jnp.sum(sums[...], axis=1)


def conv_outer_kernel(
    lengths, conv_in, d_gating_in, g_taps_in, d_conv, resid, d_gated, unit, inverse, slope, before, after, taps,
    d_upper, out_0, out_1, out_2, out_3, conv_out, d_gating, before_ext, after_ext, g_taps, d_upper_t, g_taps_t
):
    place = locate(lengths)
    first_frame, length = place[0], place[1]
    conv_out[...] = conv_in[...]
    d_gating[...] = d_gating_in[...]
    g_taps[...] = g_taps_in[...]
    before_ext[:, 16:] = jnp.zeros((16, 16, 128), F32)
    after_ext[:, :16] = jnp.zeros((16, 16, 128), F32)
    for block in range(16):
        before_ext[block, :16] = before[:, 128 * block : 128 * block + 128].astype(F32)
        after_ext[block, 16:] = after[:, 128 * block : 128 * block + 128].astype(F32)

    def chunk(index, _):
        lanes = pl.ds(pl.multiple_of(index * 128, 128), 128)
        for ext, first, skip in ((before_ext, 0, 0), (after_ext, 112, 16)):
            own = d_conv[first : first + 16, lanes].astype(F32)
            forward = conv_out[first : first + 16, lanes]
            backward = d_gating[first : first + 16, lanes]
            for step in range(1, 16):
                offset = step + skip
                part = ext[index, pl.ds(step, 16), :]
                forward = forward + taps[offset - 1 : offset, lanes] * part
                g_taps[offset - 1 : offset, lanes] += jnp.sum(part * own, axis=0, keepdims=True)
                part = ext[index + 8, pl.ds(step, 16), :]
                backward = backward + taps[TAPS - offset : TAPS - offset + 1, lanes] * part
            conv_out[first : first + 16, lanes] = forward
            d_gating[first : first + 16, lanes] = backward
        return 0

    lax.fori_loop(0, 8, chunk, 0)
    conv = conv_out[...]
    gated = (resid[...].astype(F32) * conv).astype(BF16)
    rows = first_frame + lax.broadcasted_iota(jnp.int32, (ROWS, 1024), 0)
    d_gate = jnp.where(rows < length, d_gating[...], 0.0)
    d_gate = norm_back(d_gate, unit[...], inverse[:, :1])
    left = (d_gated[...].astype(F32) * conv * slope[:, :1024]).astype(BF16)
    right = (d_gate * slope[:, 1024:]).astype(BF16)
    d_upper[:, :1024] = left
    d_upper[:, 1024:] = right
    d_upper_t[:1024] = left.T
    d_upper_t[1024:] = right.T
    turned = jnp.concatenate([g_taps[...], jnp.zeros((96, 1024), F32)], axis=0).T.reshape(32, 32, 128)
    g_taps_t[...] = (turned[:, :16, :] + pltpu.roll(turned[:, 16:, :], 32, 2)).astype(BF16)
    for turn, ref in enumerate((out_0, out_1, out_2, out_3)):
        x = (place[4] + turn) & 3
        for m in range(8):
            ref[64 * m : 64 * m + 64] = d_upper_t[span(4 * m + x, 64), :]
            ref[576 + 128 * m : 704 + 128 * m] = gated[:, 128 * m : 128 * m + 128]
        for pair in range(4):
            right = pltpu.roll(g_taps_t[8 * pair + 4 + x].astype(F32), 64, 1)
            ref[512 + 16 * pair : 528 + 16 * pair] = (g_taps_t[8 * pair + x].astype(F32) + right).astype(BF16)


def own_columns(array, core, width):
    parts = [
        array[:, pl.ds(pl.multiple_of(2 * width * z + width * core, width), width)] for z in range(4)
    ]
    return jnp.concatenate(parts, axis=1)


def gate_grads_kernel(
    lengths, normed, cot_0, cot_1, cot_2, cot_3, gate_0, gate_1, gate_2, gate_3,
    keep, send, cot_own, d_upper_t, gated
):
    place = locate(lengths)
    x, core = place[4], place[2]
    gates = (gate_0, gate_1, gate_2, gate_3)
    g_taps = gate_0[512:576].astype(F32)
    for ref in gates[1:]:
        g_taps = g_taps + ref[512:576].astype(F32)
    left = g_taps.reshape(4, 16, 128)
    g_taps = jnp.stack([left, pltpu.roll(left, 64, 2)], axis=1).reshape(8, 16, 128).astype(BF16)
    for turn, (gate, cot) in enumerate(zip(gates, (cot_0, cot_1, cot_2, cot_3))):
        here = span(slot(place, turn), 128)
        d_upper_t[:, here] = gate[:512]
        for block in range(8):
            gated[here, 128 * block : 128 * block + 128] = gate[576 + 128 * block : 704 + 128 * block]
        cot_own[:128, here] = cot[:, 1152:1280]
        cot_own[128:, here] = cot[:, 1280:]
    for parity, out in ((core, keep), (1 - core, send)):
        grad = dot(d_upper_t[...], own_columns(normed, parity, 128))
        out[:, :64, :] = grad.astype(BF16).reshape(8, 64, 512)
        grad = dot(cot_own[...], own_columns(gated, parity, 128))
        out[:, 64:96, :] = grad.astype(BF16).reshape(8, 32, 512)
        for z in range(4):
            out[:, 96:, 128 * z : 128 * z + 128] = g_taps


def attention_grads_kernel(
    lengths, normed, cot_own, far_0, far_1, far_2, far_3,
    keep, send, context, rows_t
):
    place = locate(lengths)
    core = place[2]
    for turn, far in enumerate((far_0, far_1, far_2, far_3)):
        for block in range(GROUP):
            tokens = slice(128 * block, 128 * block + 128)
            context[tokens, span(slot(place, turn), 128)] = far[96:224, tokens]
    for x in range(4):

        @pl.when(place[4] == x)
        def _():
            for turn, far in enumerate((far_0, far_1, far_2, far_3)):
                for index, (_, there) in enumerate(unit_rows_of((x - turn) % 4, x)):
                    rows_t[16 * there : 16 * there + 16] = far[16 * index : 16 * index + 16]

    lane = lax.broadcasted_iota(jnp.int32, (512, 128), 1)
    blocks, swapped = [], []
    for z in range(4):
        block = context[:, 128 * z : 128 * z + 128].astype(F32)
        blocks.append(block)
        swapped.append(pltpu.roll(block, HEAD, 1))
    lane_out = lax.broadcasted_iota(jnp.int32, (8, 16, 512), 2)
    for parity, out in ((core, keep), (1 - core, send)):
        grad = dot(rows_t[...], own_columns(normed, parity, 128))
        out[:, :48, :] = grad.astype(BF16).reshape(8, 48, 512)
        mine = (lane < HEAD) == (parity == 0)
        doubled = jnp.concatenate(
            [jnp.where(mine, block, other) for block, other in zip(blocks, swapped)], axis=1
        ).astype(BF16)
        grad = dot(cot_own[...], doubled).reshape(8, 32, 512)
        out[:, 48:, :] = jnp.where((lane_out & 127) < HEAD, grad[:, :16], grad[:, 16:]).astype(BF16)


def attend_kernel(
    lengths, queries, kv, before, after, cot_0, cot_1, cot_2, cot_3, context_out, d_query, d_before, d_after, d_own,
    d_contexts, key, value, key_t, value_t, scores, weights, d_scores, d_key, d_value
):
    place = locate(lengths)
    group_first, length = place[3], place[1]
    for turn, ref in enumerate((cot_0, cot_1, cot_2, cot_3)):
        d_contexts[slot(place, turn)] = ref[:, 1024:1152]
    for part, ref in enumerate((before, kv, after)):
        for piece in range(GROUP):
            start = 512 * part + ROWS * piece
            key_block = ref[piece, :, :128]
            value_block = ref[piece, :, 128:]
            key[start : start + ROWS] = key_block
            value[start : start + ROWS] = value_block
            key_t[:, start : start + ROWS] = key_block.T
            value_t[:, start : start + ROWS] = value_block.T
    d_key[...] = jnp.zeros_like(d_key)
    d_value[...] = jnp.zeros_like(d_value)
    lane = lax.broadcasted_iota(jnp.int32, (ROWS, 128), 1)
    first_head = lane < HEAD
    query_index = lax.broadcasted_iota(jnp.int32, (1, 256), 1)
    query_index = jnp.where(query_index < ROWS, query_index, query_index - ROWS)
    chunks = WINDOW // 128
    for block in range(GROUP):
        base = ROWS * block
        low = jnp.maximum(query_index, 512 - group_first - base)
        high = jnp.minimum(query_index + 1024, length - group_first + 511 - base)
        query = queries[block].astype(F32) * 0.125
        d_context = d_contexts[block].astype(F32)
        zero = jnp.zeros_like(query)
        query_pair = jnp.concatenate(
            [jnp.where(first_head, query, zero), jnp.where(first_head, zero, query)], axis=0
        ).astype(BF16)
        d_pair = jnp.concatenate(
            [jnp.where(first_head, d_context, zero), jnp.where(first_head, zero, d_context)], axis=0
        ).astype(BF16)

        def allowed_of(index):
            position = 128 * index + lax.broadcasted_iota(jnp.int32, (128, 256), 0)
            if 0 < index < chunks - 1:
                last = length - group_first + 511 - base
                return position <= jnp.where(128 * index >= 512 - group_first - base, last, -1)
            return (position >= low) & (position <= high)

        peak = jnp.full((128, 256), NEG_LARGE, F32)
        for index in range(chunks):
            part = dot(key[base + 128 * index : base + 128 * index + 128], query_pair, 1, 1)
            part = jnp.where(allowed_of(index), part, NEG_LARGE)
            scores[128 * index : 128 * index + 128] = part
            peak = jnp.maximum(peak, part)
        peak = jnp.max(peak, axis=0, keepdims=True)
        total = jnp.zeros((128, 256), F32)
        for index in range(chunks):
            part = scores[128 * index : 128 * index + 128]
            part = jnp.exp(part - peak)
            scores[128 * index : 128 * index + 128] = part
            total = total + part
        some = jnp.maximum(low, 0) <= jnp.minimum(high, WINDOW - 1)
        scale = jnp.where(some, 1.0 / jnp.maximum(jnp.sum(total, axis=0, keepdims=True), 1.0), 0.0)
        for index in range(chunks):
            part = scores[128 * index : 128 * index + 128] * scale
            weights[128 * index : 128 * index + 128] = part.astype(BF16)
        wide = dot(value_t[:, base : base + WINDOW], weights[...])
        context_t = jnp.concatenate([wide[:HEAD, :128], wide[HEAD:, 128:]], axis=0)
        context_out[block] = context_t.T.astype(BF16)
        product = context_t * d_context.T
        row_dot = jnp.concatenate(
            [
                jnp.sum(product[:HEAD], axis=0, keepdims=True),
                jnp.sum(product[HEAD:], axis=0, keepdims=True),
            ],
            axis=1,
        )
        for index in range(chunks):
            part = dot(value[base + 128 * index : base + 128 * index + 128], d_pair, 1, 1)
            part = weights[128 * index : 128 * index + 128].astype(F32) * (part - row_dot)
            d_scores[128 * index : 128 * index + 128] = part.astype(BF16)
        wide = dot(key_t[:, base : base + WINDOW], d_scores[...])
        d_query_t = jnp.concatenate([wide[:HEAD, :128], wide[HEAD:, 128:]], axis=0)
        d_query[:, base : base + 128] = (d_query_t * 0.125).astype(BF16)
        d_key[base : base + WINDOW] += dot(d_scores[...], query_pair)
        d_value[base : base + WINDOW] += dot(weights[...], d_pair)
    for piece in range(GROUP):
        for part, ref in enumerate((d_before, d_own, d_after)):
            start = 512 * part + ROWS * piece
            ref[piece, :, :128] = d_key[start : start + ROWS].astype(ref.dtype)
            ref[piece, :, 128:] = d_value[start : start + ROWS].astype(ref.dtype)


def unit_rows_of(source, target):
    units = [32 * part + 8 * source + row for part in range(3) for row in range(8)]
    wanted = [unit for unit in units if (unit // 3) % 4 == target]
    return [(units.index(unit), unit // 12 * 3 + unit % 3) for unit in wanted]


def join_kernel(
    lengths, context, d_query, own, from_before, from_after,
    unit_0, unit_1, unit_2, unit_3, joined_t
):
    place = locate(lengths)
    joined_t[:128] = d_query[...]
    for piece in range(GROUP):
        total = own[piece] + from_before[piece].astype(F32) + from_after[piece].astype(F32)
        total = total.astype(BF16)
        joined_t[128:256, 128 * piece : 128 * piece + 128] = total[:, :128].T
        joined_t[256:, 128 * piece : 128 * piece + 128] = total[:, 128:].T
    for turn, ref in enumerate((unit_0, unit_1, unit_2, unit_3)):
        for block in range(GROUP):
            lanes = slice(128 * block, 128 * block + 128)
            ref[96:224, lanes] = context[block]
            ref[224:, lanes] = joined_t[96 * block : 96 * block + 96, span((place[4] + turn) & 3, 128)]
    for x in range(4):

        @pl.when(place[4] == x)
        def _():
            for turn, ref in enumerate((unit_0, unit_1, unit_2, unit_3)):
                for index, (here, _) in enumerate(unit_rows_of(x, (x + turn) % 4)):
                    ref[16 * index : 16 * index + 16] = joined_t[16 * here : 16 * here + 16]


def gate_rows_kernel(frames, gate, d_upper, w_up, w_down, layer_part, d_normed):
    gated = jnp.concatenate([gate[576 + 128 * m : 704 + 128 * m] for m in range(8)], axis=1)
    layer_part[...] = frames[...].astype(F32) + dot(gated, w_down[...])
    d_normed[...] = dot(d_upper[...], w_up[...], 1, 1)


def rows_kernel(
    lengths, frames, cotangent, far_0, far_1, far_2, far_3, layer_part, d_normed,
    w_qkv, w_out, layer_out, d_frames, context, joined_t, back
):
    place = locate(lengths)
    for turn, far in enumerate((far_0, far_1, far_2, far_3)):
        pair = slot(place, turn)
        context[:, span(pair, 128)] = far[96:224, span(place[4], 128)]
        for block in range(4):
            back[96 * block : 96 * block + 96] = far[224:, 128 * block : 128 * block + 128]
        for part in range(3):
            joined_t[span(pair + 4 * part, 128), :] = back[128 * part : 128 * part + 128]
    layer_out[...] = (layer_part[...] + dot(context[...], w_out[...])).astype(BF16)
    unit_rows, inverse = normalize(frames[...].astype(F32))
    d_rows = d_normed[...] + dot(joined_t[...].T, w_qkv[...], 1, 1)
    d_frames[...] = (cotangent[...].astype(F32) + norm_back(d_rows, unit_rows, inverse)).astype(BF16)


def add_kernel(near, far, out):
    out[...] = (near[...].astype(F32) + far[...].astype(F32)).astype(BF16)


def turn_add_kernel(lengths, near, far, out_0, out_1, out_2, out_3):
    place = locate(lengths)
    for turn, ref in enumerate((out_0, out_1, out_2, out_3)):
        for z_low in range(2):
            m = 4 * z_low + ((place[6] + turn) & 3)
            ref[z_low] = (near[m].astype(F32) + far[m].astype(F32)).astype(BF16)


def gate_sum_kernel(lengths, part_0, part_1, part_2, part_3, keep, send):
    place = locate(lengths)
    for out, z_low in ((keep, place[7]), (send, 1 - place[7])):
        total = part_0[z_low].astype(F32)
        for part in (part_1, part_2, part_3):
            total = total + part[z_low].astype(F32)
        out[...] = total.astype(BF16)


def chunk_sum_kernel(lengths, gate, gate_far, parts, out_0, out_1, out_2, out_3, total):
    place = locate(lengths)
    for first in range(0, 176, 16):
        rows = slice(first, first + 16)
        if first < 112:
            acc = gate[rows].astype(F32) + gate_far[rows].astype(F32)
        else:
            acc = parts[0, first - 112 : first - 96].astype(F32)
            for source in range(1, 8):
                acc = acc + parts[source, first - 112 : first - 96].astype(F32)
        for z in range(4):
            total[z, rows, :] = acc[:, 128 * z : 128 * z + 128].astype(BF16)
    for turn, ref in enumerate((out_0, out_1, out_2, out_3)):
        ref[...] = total[(place[5] + turn) & 3]


def final_kernel(lengths, part_0, part_1, part_2, part_3, g_qkv_t, g_out_t, g_up_t, g_down_t, g_taps, ordered):
    place = locate(lengths)
    for turn, ref in enumerate((part_0, part_1, part_2, part_3)):
        ordered[(place[5] + 4 - turn) & 3] = ref[...].astype(F32)
    total = (ordered[0] + ordered[1]) + (ordered[2] + ordered[3])
    g_up_t[...] = total[:64]
    g_down_t[...] = total[64:96]
    turned = total[96:112].T
    g_taps[...] = jnp.concatenate([turned[:TAPS], turned[32 : 32 + TAPS]], axis=1)
    g_qkv_t[...] = total[112:160]
    g_out_t[:16] = total[160:, :HEAD]
    g_out_t[16:] = total[160:, HEAD:]


SEQ = ("z_low", "y", "x")


def shift(array, by):
    return lax.ppermute(array, SEQ, [(i, i + by) for i in range(32) if 0 <= i + by < 32])


def other_core(array):
    return lax.ppermute(array, "core", [(0, 1), (1, 0)])


def turn_x(pieces):
    return [pieces[0]] + [
        lax.ppermute(pieces[by], "x", [(i, (i + by) % 4) for i in range(4)]) for by in range(1, 4)
    ]


def turn_y(pieces):
    return [pieces[0]] + [
        lax.ppermute(pieces[by], "y", [(i, (i + by) % 4) for i in range(4)]) for by in range(1, 4)
    ]


def turn_z(pieces):
    return [pieces[0]] + [
        lax.ppermute(pieces[by], "z_high", [(i, (i + by) % 4) for i in range(4)]) for by in range(1, 4)
    ]


def local(frames, cotangent, lengths, w_qkv, w_out, w_up, w_down, conv_kernel):
    frames, cotangent = frames[0], cotangent[0]
    wide = ((ROWS, 1024), BF16)
    wide_f = ((ROWS, 1024), F32)
    quad = ((4, ROWS, 256), BF16)
    piece = ((ROWS, 1408), BF16)
    pieces = call(
        send_kernel, [piece] * 4, [pltpu.VMEM((ROWS, 512), BF16), pltpu.VMEM((1024, ROWS), BF16)], scalars=1
    )(lengths, *in_hbm(frames, cotangent, w_out))
    pieces, frames_later = lax.optimization_barrier((pieces, frames))
    in_x = turn_x(pieces)
    resid, d_gated, gating, d_conv, unit, inverse, slope, top, bottom = call(
        gate_kernel,
        [wide, wide, wide, wide, wide_f, ((ROWS, 128), F32), ((ROWS, 2048), F32),
         ((16, 2048), BF16), ((16, 2048), BF16)],
        [pltpu.VMEM((2, 1024, 1024), BF16), pltpu.VMEM((1024, 1024), BF16), pltpu.SemaphoreType.DMA((3,))],
        scalars=1,
        left=2,
    )(lengths, *in_hbm(frames_later, cotangent, w_up, w_down))
    before, after = shift(bottom, 1), shift(top, -1)
    conv_in, d_gating_in, g_taps_in = call(
        conv_inner_kernel,
        [wide_f, wide_f, ((32, 1024), F32)],
        [pltpu.VMEM((8, 160, 128), F32), pltpu.VMEM((8, 160, 128), F32), pltpu.VMEM((32, 8, 1024), F32)],
    )(gating, d_conv, conv_kernel)
    in_x, conv_in, before, after = lax.optimization_barrier((in_x, conv_in, before, after))
    normed, query, kv = call(
        project_kernel, [((512, 1024), BF16), ((4, ROWS, 128), BF16), quad], scalars=1
    )(lengths, *in_x, w_qkv)
    kv_before, kv_after = shift(kv, 4), shift(kv, -4)
    conv_in, kv = lax.optimization_barrier((conv_in, kv))
    gate = ((1600, 128), BF16)
    d_upper, *gate_x = call(
        conv_outer_kernel,
        [((ROWS, 2048), BF16, HBM), gate, gate, gate, gate],
        [pltpu.VMEM((ROWS, 1024), F32), pltpu.VMEM((ROWS, 1024), F32),
         pltpu.VMEM((16, 32, 128), F32), pltpu.VMEM((16, 32, 128), F32),
         pltpu.VMEM((32, 1024), F32), pltpu.VMEM((2048, ROWS), BF16), pltpu.VMEM((32, 16, 128), BF16)],
        scalars=1,
    )(lengths, conv_in, d_gating_in, g_taps_in, d_conv, resid, d_gated, unit, inverse, slope, before, after, conv_kernel)
    gate_x, kv_before = lax.optimization_barrier((gate_x, kv_before))
    gate_x = turn_x(gate_x)
    context, d_query, d_before, d_after, d_own = call(
        attend_kernel,
        [((4, ROWS, 128), BF16), ((ROWS, 512), BF16), quad, quad, ((4, ROWS, 256), F32)],
        [pltpu.VMEM((4, ROWS, 128), BF16),
         pltpu.VMEM((1536, 128), BF16), pltpu.VMEM((1536, 128), BF16),
         pltpu.VMEM((128, 1536), BF16), pltpu.VMEM((128, 1536), BF16),
         pltpu.VMEM((WINDOW, 256), F32), pltpu.VMEM((WINDOW, 256), BF16), pltpu.VMEM((WINDOW, 256), BF16),
         pltpu.VMEM((1536, 128), F32), pltpu.VMEM((1536, 128), F32)],
        scalars=1,
    )(lengths, query, kv, kv_before, kv_after, *in_x)
    from_before, from_after = shift(d_after, 4), shift(d_before, -4)
    frames_later, d_own = lax.optimization_barrier((frames, d_own))
    layer_part, d_normed = call(gate_rows_kernel, [wide_f + (HBM,), wide_f + (HBM,)])(
        *in_hbm(frames_later), gate_x[0], *in_hbm(d_upper), w_up, w_down
    )
    gate_x, d_normed, d_own = lax.optimization_barrier((gate_x, d_normed, d_own))
    far = call(join_kernel, [((320, 512), BF16)] * 4, [pltpu.VMEM((384, 512), BF16)], scalars=1)(
        lengths, context, d_query, d_own, from_before, from_after
    )
    far, gate_x = lax.optimization_barrier((far, gate_x))
    far_x = turn_x(far)
    keep, send, cot_own = call(
        gate_grads_kernel,
        [((8, 112, 512), BF16), ((8, 112, 512), BF16), ((256, 512), BF16)],
        [pltpu.VMEM((512, 512), BF16), pltpu.VMEM((512, 1024), BF16)],
        scalars=1,
    )(lengths, normed, *in_x, *gate_x)
    gate_y = turn_y(
        call(turn_add_kernel, [((2, 112, 512), BF16)] * 4, scalars=1)(lengths, keep, other_core(send))
    )
    far_x, gate_y = lax.optimization_barrier((far_x, gate_y))
    attention_keep, send = call(
        attention_grads_kernel,
        [((8, 64, 512), BF16), ((8, 64, 512), BF16)],
        [pltpu.VMEM((512, 512), BF16), pltpu.VMEM((384, 512), BF16)],
        scalars=1,
    )(lengths, normed, cot_own, *far_x)
    send, gate_y = lax.optimization_barrier((send, gate_y))
    gate_keep, gate_send = call(gate_sum_kernel, [((112, 512), BF16, HBM)] * 2, scalars=1)(lengths, *gate_y)
    attention_keep, gate_send = lax.optimization_barrier((attention_keep, gate_send))
    (parts,) = call(add_kernel, [((8, 64, 512), BF16, HBM)])(attention_keep, other_core(send))
    parts = lax.all_to_all(parts, ("z_low", "y"), 0, 0)
    gate_far = lax.ppermute(gate_send, "z_low", [(0, 1), (1, 0)])
    layer_out, d_frames = call(
        rows_kernel,
        [wide, wide],
        [pltpu.VMEM((ROWS, 512), BF16), pltpu.VMEM((1536, ROWS), BF16), pltpu.VMEM((384, ROWS), BF16)],
        scalars=1,
    )(
        lengths, frames, cotangent, *far_x, layer_part, d_normed, *in_hbm(w_qkv, w_out)
    )
    parts, layer_out, d_frames = lax.optimization_barrier((parts, layer_out, d_frames))
    parts = call(
        chunk_sum_kernel, [((176, 128), BF16)] * 4, [pltpu.VMEM((4, 176, 128), BF16)], scalars=1
    )(lengths, gate_keep, gate_far, parts)
    g_qkv, g_out, g_up, g_down, g_kernel = call(
        final_kernel,
        [((48, 128), F32), ((32, HEAD), F32), ((64, 128), F32), ((32, 128), F32), ((TAPS, 32), F32)],
        [pltpu.VMEM((4, 176, 128), F32)],
        scalars=1,
    )(lengths, *turn_z(parts))
    return (layer_out[None], d_frames[None], g_qkv.T, g_out.T, g_up.T, g_down.T, g_kernel)


def solution(mesh):
    split = Mesh(mesh.devices.reshape(2, 4, 4, 4, 2), SEQ + ("z_high", "core"))
    dp = ("z_high", "core")
    return jax.shard_map(
        local,
        mesh=split,
        in_specs=(P(dp, SEQ, None), P(dp, SEQ, None), P(dp), P(), P(), P(), P(), P()),
        out_specs=(
            P(dp, SEQ, None),
            P(dp, SEQ, None),
            P(dp, SEQ),
            P(dp, SEQ),
            P(dp, SEQ),
            P(dp, SEQ),
            P(None, SEQ),
        ),
        check_vma=False,
    )
```

```python
import jax
import jax.numpy as jnp
from jax import lax
from jax.experimental import pallas as pl
from jax.experimental.pallas import tpu as pltpu
from jax.sharding import Mesh, PartitionSpec as P

HEAD = 64
BAND = 512
ROWS = 128
GROUP = 4
WINDOW = 2 * BAND + ROWS
MARGIN = 15
TAPS = 31

EPSILON = 1e-05
NEG_LARGE = -3e38
HALF_ROOT = 0.7071067811865476
NORMAL_PEAK = 0.3989422804014327

BF16 = jnp.bfloat16
F32 = jnp.float32
HBM = pltpu.HBM
VMEM_LIMIT = 24 * 2**20


def call(body, outs, scratch=(), scalars=0, left=0):
    def run(*args):
        specs = [pl.BlockSpec(memory_space=pltpu.SMEM)] * scalars
        specs += [pl.BlockSpec(memory_space=pltpu.VMEM)] * (len(args) - scalars - left)
        specs += [pl.BlockSpec(memory_space=HBM)] * left
        return pl.pallas_call(
            body,
            out_shape=[
                HBM(*out[:2]) if len(out) > 2 else jax.ShapeDtypeStruct(*out) for out in outs
            ],
            in_specs=specs,
            out_specs=[pl.BlockSpec(memory_space=pltpu.VMEM)] * len(outs),
            scratch_shapes=list(scratch),
            compiler_params=pltpu.CompilerParams(vmem_limit_bytes=VMEM_LIMIT),
        )(*args)

    return run


def in_hbm(*arrays):
    return [pltpu.with_memory_space_constraint(array, HBM) for array in arrays]


def dot(left, right, left_dim=1, right_dim=0):
    return lax.dot_general(
        left, right, (((left_dim,), (right_dim,)), ((), ())), preferred_element_type=F32
    )


def normalize(values):
    centred = values - jnp.mean(values, axis=-1, keepdims=True)
    inverse = lax.rsqrt(jnp.mean(centred * centred, axis=-1, keepdims=True) + EPSILON)
    return (centred * inverse, inverse)


def norm_back(gradient, unit_rows, inverse):
    return inverse * (
        gradient
        - jnp.mean(gradient, axis=-1, keepdims=True)
        - unit_rows * jnp.mean(gradient * unit_rows, axis=-1, keepdims=True)
    )


def locate(lengths):
    z_low, y, x = lax.axis_index("z_low"), lax.axis_index("y"), lax.axis_index("x")
    row = 4 * z_low + y
    return ((4 * row + x) * ROWS, lengths[0], lax.axis_index("core"), row * (GROUP * ROWS), x, lax.axis_index("z_high"), y, z_low)


def slot(place, turn):
    return (place[4] + 4 - turn) & 3


def span(index, size):
    return pl.ds(pl.multiple_of(index * size, size), size)


def send_kernel(lengths, frames, cotangent, w_out, out_0, out_1, out_2, out_3, d_context, cot_t):
    place = locate(lengths)
    d_context[...] = dot(cotangent[...], w_out[...], 1, 1).astype(BF16)
    cot_t[...] = cotangent[...].T
    for turn, ref in enumerate((out_0, out_1, out_2, out_3)):
        x = (place[4] + turn) & 3
        ref[:, :1024] = frames[...]
        ref[:, 1024:1152] = d_context[:, span(x, 128)]
        for m in range(8):
            lanes = slice(1152 + 128 * (m // 4), 1280 + 128 * (m // 4))
            ref[32 * (m % 4) : 32 * (m % 4) + 32, lanes] = cot_t[span(4 * m + x, 32), :]


def project_kernel(lengths, frames_0, frames_1, frames_2, frames_3, w_qkv, normed, query, kv):
    place = locate(lengths)
    x = place[4]
    for turn, ref in enumerate((frames_0, frames_1, frames_2, frames_3)):
        unit_rows, _ = normalize(ref[:, :1024].astype(F32))
        normed[span(slot(place, turn), ROWS), :] = unit_rows.astype(BF16)
    weight = jnp.concatenate([w_qkv[:, span(x + 4 * part, 128)] for part in range(3)], axis=1)
    joined = dot(normed[...], weight).astype(BF16)
    query[...] = joined[:, :128].reshape(4, ROWS, 128)
    kv[...] = joined[:, 128:].reshape(4, ROWS, 256)


def gate_kernel(
    lengths, frames, cotangent, w_up, w_down,
    resid, d_gated, gating, d_conv, unit, inverse, slope, top, bottom,
    up, down, copied
):
    place = locate(lengths)
    first_frame, length = place[0], place[1]
    copies = [
        pltpu.make_async_copy(w_up.at[:, pl.ds(1024 * half, 1024)], up.at[half], copied.at[half]) for half in (1, 0)
    ] + [pltpu.make_async_copy(w_down, down, copied.at[2])]
    for copy in copies:
        copy.start()
    unit_rows, _ = normalize(frames[...].astype(F32))
    unit_rows = unit_rows.astype(BF16)
    hidden = [None, None]
    for half, copy in ((1, copies[0]), (0, copies[1])):
        copy.wait()
        upper = dot(unit_rows, up[half])
        phi = 0.5 * (1.0 + lax.erf(upper * HALF_ROOT))
        slope[:, 1024 * half : 1024 * half + 1024] = phi + upper * jnp.exp(-0.5 * upper * upper) * NORMAL_PEAK
        hidden[half] = (upper * phi).astype(BF16)
    gate_unit, gate_inv = normalize(hidden[1].astype(F32))
    unit[...] = gate_unit
    inverse[...] = jnp.broadcast_to(gate_inv, inverse.shape)
    rows = first_frame + lax.broadcasted_iota(jnp.int32, (ROWS, 1024), 0)
    masked = jnp.where(rows < length, gate_unit, 0.0).astype(BF16)
    gating[...] = masked
    resid[...] = hidden[0]
    copies[2].wait()
    back = dot(cotangent[...], down[...], 1, 1).astype(BF16)
    d_gated[...] = back
    conv_back = (back.astype(F32) * hidden[0].astype(F32)).astype(BF16)
    d_conv[...] = conv_back
    top[:, :1024] = masked[:16]
    top[:, 1024:] = conv_back[:16]
    bottom[:, :1024] = masked[112:]
    bottom[:, 1024:] = conv_back[112:]


def conv_inner_kernel(gating, d_conv, taps, conv_out, d_gating, g_taps, gate_ext, conv_ext, sums):
    for ext, ref in ((gate_ext, gating), (conv_ext, d_conv)):
        ext[:, :16] = jnp.zeros((8, 16, 128), F32)
        ext[:, 144:] = jnp.zeros((8, 16, 128), F32)
        for block in range(8):
            ext[block, 16:144] = ref[:, 128 * block : 128 * block + 128].astype(F32)
    sums[...] = jnp.zeros_like(sums)

    def chunk(index, _):
        lanes = pl.ds(pl.multiple_of(index * 128, 128), 128)
        for first in (0, 64):
            own = conv_ext[index, 16 + first : 80 + first, :]
            forward = jnp.zeros((64, 128), F32)
            for shift in range(8):
                moved = gate_ext[index, pl.ds(first + shift, 88), :]
                for step in range(4):
                    offset = 8 * step + shift
                    if 1 <= offset <= TAPS:
                        part = moved[8 * step : 8 * step + 64]
                        forward = forward + taps[offset - 1 : offset, lanes] * part
                        sums[offset - 1, :, lanes] += jnp.sum((part * own).reshape(8, 8, 128), axis=0)
            conv_out[first : first + 64, lanes] = forward
            backward = jnp.zeros((64, 128), F32)
            for shift in range(8):
                moved = conv_ext[index, pl.ds(first + shift, 88), :]
                for step in range(4):
                    offset = 8 * step + shift
                    if 1 <= offset <= TAPS:
                        part = moved[8 * step : 8 * step + 64]
                        backward = backward + taps[TAPS - offset : TAPS - offset + 1, lanes] * part
            d_gating[first : first + 64, lanes] = backward
        return 0

    lax.fori_loop(0, 8, chunk, 0)
    g_taps[...] = jnp.sum(sums[...], axis=1)


def conv_outer_kernel(
    lengths, conv_in, d_gating_in, g_taps_in, d_conv, resid, d_gated, unit, inverse, slope, before, after, taps,
    d_upper, out_0, out_1, out_2, out_3, conv_out, d_gating, before_ext, after_ext, g_taps, d_upper_t, g_taps_t
):
    place = locate(lengths)
    first_frame, length = place[0], place[1]
    conv_out[...] = conv_in[...]
    d_gating[...] = d_gating_in[...]
    g_taps[...] = g_taps_in[...]
    before_ext[:, 16:] = jnp.zeros((16, 16, 128), F32)
    after_ext[:, :16] = jnp.zeros((16, 16, 128), F32)
    for block in range(16):
        before_ext[block, :16] = before[:, 128 * block : 128 * block + 128].astype(F32)
        after_ext[block, 16:] = after[:, 128 * block : 128 * block + 128].astype(F32)

    def chunk(index, _):
        lanes = pl.ds(pl.multiple_of(index * 128, 128), 128)
        for ext, first, skip in ((before_ext, 0, 0), (after_ext, 112, 16)):
            own = d_conv[first : first + 16, lanes].astype(F32)
            forward = conv_out[first : first + 16, lanes]
            backward = d_gating[first : first + 16, lanes]
            for step in range(1, 16):
                offset = step + skip
                part = ext[index, pl.ds(step, 16), :]
                forward = forward + taps[offset - 1 : offset, lanes] * part
                g_taps[offset - 1 : offset, lanes] += jnp.sum(part * own, axis=0, keepdims=True)
                part = ext[index + 8, pl.ds(step, 16), :]
                backward = backward + taps[TAPS - offset : TAPS - offset + 1, lanes] * part
            conv_out[first : first + 16, lanes] = forward
            d_gating[first : first + 16, lanes] = backward
        return 0

    lax.fori_loop(0, 8, chunk, 0)
    conv = conv_out[...]
    gated = (resid[...].astype(F32) * conv).astype(BF16)
    rows = first_frame + lax.broadcasted_iota(jnp.int32, (ROWS, 1024), 0)
    d_gate = jnp.where(rows < length, d_gating[...], 0.0)
    d_gate = norm_back(d_gate, unit[...], inverse[:, :1])
    left = (d_gated[...].astype(F32) * conv * slope[:, :1024]).astype(BF16)
    right = (d_gate * slope[:, 1024:]).astype(BF16)
    d_upper[:, :1024] = left
    d_upper[:, 1024:] = right
    d_upper_t[:1024] = left.T
    d_upper_t[1024:] = right.T
    turned = jnp.concatenate([g_taps[...], jnp.zeros((96, 1024), F32)], axis=0).T.reshape(32, 32, 128)
    g_taps_t[...] = (turned[:, :16, :] + pltpu.roll(turned[:, 16:, :], 32, 2)).astype(BF16)
    for turn, ref in enumerate((out_0, out_1, out_2, out_3)):
        x = (place[4] + turn) & 3
        for m in range(8):
            ref[64 * m : 64 * m + 64] = d_upper_t[span(4 * m + x, 64), :]
            ref[576 + 128 * m : 704 + 128 * m] = gated[:, 128 * m : 128 * m + 128]
        for pair in range(4):
            right = pltpu.roll(g_taps_t[8 * pair + 4 + x].astype(F32), 64, 1)
            ref[512 + 16 * pair : 528 + 16 * pair] = (g_taps_t[8 * pair + x].astype(F32) + right).astype(BF16)


def own_columns(array, core, width):
    parts = [
        array[:, pl.ds(pl.multiple_of(2 * width * z + width * core, width), width)] for z in range(4)
    ]
    return jnp.concatenate(parts, axis=1)


def gate_grads_kernel(
    lengths, normed, cot_0, cot_1, cot_2, cot_3, gate_0, gate_1, gate_2, gate_3,
    keep, send, cot_own, d_upper_t, gated
):
    place = locate(lengths)
    x, core = place[4], place[2]
    gates = (gate_0, gate_1, gate_2, gate_3)
    g_taps = gate_0[512:576].astype(F32)
    for ref in gates[1:]:
        g_taps = g_taps + ref[512:576].astype(F32)
    left = g_taps.reshape(4, 16, 128)
    g_taps = jnp.stack([left, pltpu.roll(left, 64, 2)], axis=1).reshape(8, 16, 128).astype(BF16)
    for turn, (gate, cot) in enumerate(zip(gates, (cot_0, cot_1, cot_2, cot_3))):
        here = span(slot(place, turn), 128)
        d_upper_t[:, here] = gate[:512]
        for block in range(8):
            gated[here, 128 * block : 128 * block + 128] = gate[576 + 128 * block : 704 + 128 * block]
        cot_own[:128, here] = cot[:, 1152:1280]
        cot_own[128:, here] = cot[:, 1280:]
    for parity, out in ((core, keep), (1 - core, send)):
        grad = dot(d_upper_t[...], own_columns(normed, parity, 128))
        out[:, :64, :] = grad.astype(BF16).reshape(8, 64, 512)
        grad = dot(cot_own[...], own_columns(gated, parity, 128))
        out[:, 64:96, :] = grad.astype(BF16).reshape(8, 32, 512)
        for z in range(4):
            out[:, 96:, 128 * z : 128 * z + 128] = g_taps


def attention_grads_kernel(
    lengths, normed, cot_own, far_0, far_1, far_2, far_3,
    keep, send, context, rows_t
):
    place = locate(lengths)
    core = place[2]
    for turn, far in enumerate((far_0, far_1, far_2, far_3)):
        for block in range(GROUP):
            tokens = slice(128 * block, 128 * block + 128)
            context[tokens, span(slot(place, turn), 128)] = far[96:224, tokens]
    for x in range(4):

        @pl.when(place[4] == x)
        def _():
            for turn, far in enumerate((far_0, far_1, far_2, far_3)):
                for index, (_, there) in enumerate(unit_rows_of((x - turn) % 4, x)):
                    rows_t[16 * there : 16 * there + 16] = far[16 * index : 16 * index + 16]

    lane = lax.broadcasted_iota(jnp.int32, (512, 128), 1)
    blocks, swapped = [], []
    for z in range(4):
        block = context[:, 128 * z : 128 * z + 128].astype(F32)
        blocks.append(block)
        swapped.append(pltpu.roll(block, HEAD, 1))
    lane_out = lax.broadcasted_iota(jnp.int32, (8, 16, 512), 2)
    for parity, out in ((core, keep), (1 - core, send)):
        grad = dot(rows_t[...], own_columns(normed, parity, 128))
        out[:, :48, :] = grad.astype(BF16).reshape(8, 48, 512)
        mine = (lane < HEAD) == (parity == 0)
        doubled = jnp.concatenate(
            [jnp.where(mine, block, other) for block, other in zip(blocks, swapped)], axis=1
        ).astype(BF16)
        grad = dot(cot_own[...], doubled).reshape(8, 32, 512)
        out[:, 48:, :] = jnp.where((lane_out & 127) < HEAD, grad[:, :16], grad[:, 16:]).astype(BF16)


def attend_kernel(
    lengths, queries, kv, before, after, cot_0, cot_1, cot_2, cot_3, context_out, d_query, d_before, d_after, d_own,
    d_contexts, key, value, key_t, value_t, scores, weights, d_scores, d_key, d_value
):
    place = locate(lengths)
    group_first, length = place[3], place[1]
    for turn, ref in enumerate((cot_0, cot_1, cot_2, cot_3)):
        d_contexts[slot(place, turn)] = ref[:, 1024:1152]
    for part, ref in enumerate((before, kv, after)):
        for piece in range(GROUP):
            start = 512 * part + ROWS * piece
            key_block = ref[piece, :, :128]
            value_block = ref[piece, :, 128:]
            key[start : start + ROWS] = key_block
            value[start : start + ROWS] = value_block
            key_t[:, start : start + ROWS] = key_block.T
            value_t[:, start : start + ROWS] = value_block.T
    d_key[...] = jnp.zeros_like(d_key)
    d_value[...] = jnp.zeros_like(d_value)
    lane = lax.broadcasted_iota(jnp.int32, (ROWS, 128), 1)
    first_head = lane < HEAD
    query_index = lax.broadcasted_iota(jnp.int32, (1, 256), 1)
    query_index = jnp.where(query_index < ROWS, query_index, query_index - ROWS)
    chunks = WINDOW // 128
    for block in range(GROUP):
        base = ROWS * block
        low = jnp.maximum(query_index, 512 - group_first - base)
        high = jnp.minimum(query_index + 1024, length - group_first + 511 - base)
        query = queries[block].astype(F32) * 0.125
        d_context = d_contexts[block].astype(F32)
        zero = jnp.zeros_like(query)
        query_pair = jnp.concatenate(
            [jnp.where(first_head, query, zero), jnp.where(first_head, zero, query)], axis=0
        ).astype(BF16)
        d_pair = jnp.concatenate(
            [jnp.where(first_head, d_context, zero), jnp.where(first_head, zero, d_context)], axis=0
        ).astype(BF16)

        def allowed_of(index):
            position = 128 * index + lax.broadcasted_iota(jnp.int32, (128, 256), 0)
            if 0 < index < chunks - 1:
                last = length - group_first + 511 - base
                return position <= jnp.where(128 * index >= 512 - group_first - base, last, -1)
            return (position >= low) & (position <= high)

        peak = jnp.full((128, 256), NEG_LARGE, F32)
        for index in range(chunks):
            part = dot(key[base + 128 * index : base + 128 * index + 128], query_pair, 1, 1)
            part = jnp.where(allowed_of(index), part, NEG_LARGE)
            scores[128 * index : 128 * index + 128] = part
            peak = jnp.maximum(peak, part)
        peak = jnp.max(peak, axis=0, keepdims=True)
        total = jnp.zeros((128, 256), F32)
        for index in range(chunks):
            part = scores[128 * index : 128 * index + 128]
            part = jnp.exp(part - peak)
            scores[128 * index : 128 * index + 128] = part
            total = total + part
        some = jnp.maximum(low, 0) <= jnp.minimum(high, WINDOW - 1)
        scale = jnp.where(some, 1.0 / jnp.maximum(jnp.sum(total, axis=0, keepdims=True), 1.0), 0.0)
        for index in range(chunks):
            part = scores[128 * index : 128 * index + 128] * scale
            weights[128 * index : 128 * index + 128] = part.astype(BF16)
        wide = dot(value_t[:, base : base + WINDOW], weights[...])
        context_t = jnp.concatenate([wide[:HEAD, :128], wide[HEAD:, 128:]], axis=0)
        context_out[block] = context_t.T.astype(BF16)
        product = context_t * d_context.T
        row_dot = jnp.concatenate(
            [
                jnp.sum(product[:HEAD], axis=0, keepdims=True),
                jnp.sum(product[HEAD:], axis=0, keepdims=True),
            ],
            axis=1,
        )
        for index in range(chunks):
            part = dot(value[base + 128 * index : base + 128 * index + 128], d_pair, 1, 1)
            part = weights[128 * index : 128 * index + 128].astype(F32) * (part - row_dot)
            d_scores[128 * index : 128 * index + 128] = part.astype(BF16)
        wide = dot(key_t[:, base : base + WINDOW], d_scores[...])
        d_query_t = jnp.concatenate([wide[:HEAD, :128], wide[HEAD:, 128:]], axis=0)
        d_query[:, base : base + 128] = (d_query_t * 0.125).astype(BF16)
        d_key[base : base + WINDOW] += dot(d_scores[...], query_pair)
        d_value[base : base + WINDOW] += dot(weights[...], d_pair)
    for piece in range(GROUP):
        for part, ref in enumerate((d_before, d_own, d_after)):
            start = 512 * part + ROWS * piece
            ref[piece, :, :128] = d_key[start : start + ROWS].astype(ref.dtype)
            ref[piece, :, 128:] = d_value[start : start + ROWS].astype(ref.dtype)


def unit_rows_of(source, target):
    units = [32 * part + 8 * source + row for part in range(3) for row in range(8)]
    wanted = [unit for unit in units if (unit // 3) % 4 == target]
    return [(units.index(unit), unit // 12 * 3 + unit % 3) for unit in wanted]


def join_kernel(
    lengths, context, d_query, own, from_before, from_after,
    unit_0, unit_1, unit_2, unit_3, joined_t
):
    place = locate(lengths)
    joined_t[:128] = d_query[...]
    for piece in range(GROUP):
        total = own[piece] + from_before[piece].astype(F32) + from_after[piece].astype(F32)
        total = total.astype(BF16)
        joined_t[128:256, 128 * piece : 128 * piece + 128] = total[:, :128].T
        joined_t[256:, 128 * piece : 128 * piece + 128] = total[:, 128:].T
    for turn, ref in enumerate((unit_0, unit_1, unit_2, unit_3)):
        for block in range(GROUP):
            lanes = slice(128 * block, 128 * block + 128)
            ref[96:224, lanes] = context[block]
            ref[224:, lanes] = joined_t[96 * block : 96 * block + 96, span((place[4] + turn) & 3, 128)]
    for x in range(4):

        @pl.when(place[4] == x)
        def _():
            for turn, ref in enumerate((unit_0, unit_1, unit_2, unit_3)):
                for index, (here, _) in enumerate(unit_rows_of(x, (x + turn) % 4)):
                    ref[16 * index : 16 * index + 16] = joined_t[16 * here : 16 * here + 16]


def gate_rows_kernel(frames, gate, d_upper, w_up, w_down, layer_part, d_normed):
    gated = jnp.concatenate([gate[576 + 128 * m : 704 + 128 * m] for m in range(8)], axis=1)
    layer_part[...] = frames[...].astype(F32) + dot(gated, w_down[...])
    d_normed[...] = dot(d_upper[...], w_up[...], 1, 1)


def rows_kernel(
    lengths, frames, cotangent, far_0, far_1, far_2, far_3, layer_part, d_normed,
    w_qkv, w_out, layer_out, d_frames, context, joined_t, back
):
    place = locate(lengths)
    for turn, far in enumerate((far_0, far_1, far_2, far_3)):
        pair = slot(place, turn)
        context[:, span(pair, 128)] = far[96:224, span(place[4], 128)]
        for block in range(4):
            back[96 * block : 96 * block + 96] = far[224:, 128 * block : 128 * block + 128]
        for part in range(3):
            joined_t[span(pair + 4 * part, 128), :] = back[128 * part : 128 * part + 128]
    layer_out[...] = (layer_part[...] + dot(context[...], w_out[...])).astype(BF16)
    unit_rows, inverse = normalize(frames[...].astype(F32))
    d_rows = d_normed[...] + dot(joined_t[...].T, w_qkv[...], 1, 1)
    d_frames[...] = (cotangent[...].astype(F32) + norm_back(d_rows, unit_rows, inverse)).astype(BF16)


def add_kernel(near, far, out):
    out[...] = (near[...].astype(F32) + far[...].astype(F32)).astype(BF16)


def turn_add_kernel(lengths, near, far, out_0, out_1, out_2, out_3):
    place = locate(lengths)
    for turn, ref in enumerate((out_0, out_1, out_2, out_3)):
        for z_low in range(2):
            m = 4 * z_low + ((place[6] + turn) & 3)
            ref[z_low] = (near[m].astype(F32) + far[m].astype(F32)).astype(BF16)


def gate_sum_kernel(lengths, part_0, part_1, part_2, part_3, keep, send):
    place = locate(lengths)
    for out, z_low in ((keep, place[7]), (send, 1 - place[7])):
        total = part_0[z_low].astype(F32)
        for part in (part_1, part_2, part_3):
            total = total + part[z_low].astype(F32)
        out[...] = total.astype(BF16)


def chunk_sum_kernel(lengths, gate, gate_far, parts, out_0, out_1, out_2, out_3, total):
    place = locate(lengths)
    for first in range(0, 176, 16):
        rows = slice(first, first + 16)
        if first < 112:
            acc = gate[rows].astype(F32) + gate_far[rows].astype(F32)
        else:
            acc = parts[0, first - 112 : first - 96].astype(F32)
            for source in range(1, 8):
                acc = acc + parts[source, first - 112 : first - 96].astype(F32)
        for z in range(4):
            total[z, rows, :] = acc[:, 128 * z : 128 * z + 128].astype(BF16)
    for turn, ref in enumerate((out_0, out_1, out_2, out_3)):
        ref[...] = total[(place[5] + turn) & 3]


def final_kernel(lengths, part_0, part_1, part_2, part_3, g_qkv_t, g_out_t, g_up_t, g_down_t, g_taps, ordered):
    place = locate(lengths)
    for turn, ref in enumerate((part_0, part_1, part_2, part_3)):
        ordered[(place[5] + 4 - turn) & 3] = ref[...].astype(F32)
    total = (ordered[0] + ordered[1]) + (ordered[2] + ordered[3])
    g_up_t[...] = total[:64]
    g_down_t[...] = total[64:96]
    turned = total[96:112].T
    g_taps[...] = jnp.concatenate([turned[:TAPS], turned[32 : 32 + TAPS]], axis=1)
    g_qkv_t[...] = total[112:160]
    g_out_t[:16] = total[160:, :HEAD]
    g_out_t[16:] = total[160:, HEAD:]


SEQ = ("z_low", "y", "x")


def shift(array, by):
    return lax.ppermute(array, SEQ, [(i, i + by) for i in range(32) if 0 <= i + by < 32])


def other_core(array):
    return lax.ppermute(array, "core", [(0, 1), (1, 0)])


def turn_x(pieces):
    return [pieces[0]] + [
        lax.ppermute(pieces[by], "x", [(i, (i + by) % 4) for i in range(4)]) for by in range(1, 4)
    ]


def turn_y(pieces):
    return [pieces[0]] + [
        lax.ppermute(pieces[by], "y", [(i, (i + by) % 4) for i in range(4)]) for by in range(1, 4)
    ]


def turn_z(pieces):
    return [pieces[0]] + [
        lax.ppermute(pieces[by], "z_high", [(i, (i + by) % 4) for i in range(4)]) for by in range(1, 4)
    ]


def local(frames, cotangent, lengths, w_qkv, w_out, w_up, w_down, conv_kernel):
    frames, cotangent = frames[0], cotangent[0]
    wide = ((ROWS, 1024), BF16)
    wide_f = ((ROWS, 1024), F32)
    quad = ((4, ROWS, 256), BF16)
    piece = ((ROWS, 1408), BF16)
    pieces = call(
        send_kernel, [piece] * 4, [pltpu.VMEM((ROWS, 512), BF16), pltpu.VMEM((1024, ROWS), BF16)], scalars=1
    )(lengths, *in_hbm(frames, cotangent, w_out))
    pieces, frames_later = lax.optimization_barrier((pieces, frames))
    in_x = turn_x(pieces)
    resid, d_gated, gating, d_conv, unit, inverse, slope, top, bottom = call(
        gate_kernel,
        [wide, wide, wide, wide, wide_f, ((ROWS, 128), F32), ((ROWS, 2048), F32),
         ((16, 2048), BF16), ((16, 2048), BF16)],
        [pltpu.VMEM((2, 1024, 1024), BF16), pltpu.VMEM((1024, 1024), BF16), pltpu.SemaphoreType.DMA((3,))],
        scalars=1,
        left=2,
    )(lengths, *in_hbm(frames_later, cotangent, w_up, w_down))
    before, after = shift(bottom, 1), shift(top, -1)
    conv_in, d_gating_in, g_taps_in = call(
        conv_inner_kernel,
        [wide_f, wide_f, ((32, 1024), F32)],
        [pltpu.VMEM((8, 160, 128), F32), pltpu.VMEM((8, 160, 128), F32), pltpu.VMEM((32, 8, 1024), F32)],
    )(gating, d_conv, conv_kernel)
    in_x, conv_in, before, after = lax.optimization_barrier((in_x, conv_in, before, after))
    normed, query, kv = call(
        project_kernel, [((512, 1024), BF16), ((4, ROWS, 128), BF16), quad], scalars=1
    )(lengths, *in_x, w_qkv)
    kv_before, kv_after = shift(kv, 4), shift(kv, -4)
    conv_in, kv = lax.optimization_barrier((conv_in, kv))
    gate = ((1600, 128), BF16)
    d_upper, *gate_x = call(
        conv_outer_kernel,
        [((ROWS, 2048), BF16, HBM), gate, gate, gate, gate],
        [pltpu.VMEM((ROWS, 1024), F32), pltpu.VMEM((ROWS, 1024), F32),
         pltpu.VMEM((16, 32, 128), F32), pltpu.VMEM((16, 32, 128), F32),
         pltpu.VMEM((32, 1024), F32), pltpu.VMEM((2048, ROWS), BF16), pltpu.VMEM((32, 16, 128), BF16)],
        scalars=1,
    )(lengths, conv_in, d_gating_in, g_taps_in, d_conv, resid, d_gated, unit, inverse, slope, before, after, conv_kernel)
    gate_x, kv_before = lax.optimization_barrier((gate_x, kv_before))
    gate_x = turn_x(gate_x)
    context, d_query, d_before, d_after, d_own = call(
        attend_kernel,
        [((4, ROWS, 128), BF16), ((ROWS, 512), BF16), quad, quad, ((4, ROWS, 256), F32)],
        [pltpu.VMEM((4, ROWS, 128), BF16),
         pltpu.VMEM((1536, 128), BF16), pltpu.VMEM((1536, 128), BF16),
         pltpu.VMEM((128, 1536), BF16), pltpu.VMEM((128, 1536), BF16),
         pltpu.VMEM((WINDOW, 256), F32), pltpu.VMEM((WINDOW, 256), BF16), pltpu.VMEM((WINDOW, 256), BF16),
         pltpu.VMEM((1536, 128), F32), pltpu.VMEM((1536, 128), F32)],
        scalars=1,
    )(lengths, query, kv, kv_before, kv_after, *in_x)
    from_before, from_after = shift(d_after, 4), shift(d_before, -4)
    frames_later, d_own = lax.optimization_barrier((frames, d_own))
    layer_part, d_normed = call(gate_rows_kernel, [wide_f + (HBM,), wide_f + (HBM,)])(
        *in_hbm(frames_later), gate_x[0], *in_hbm(d_upper), w_up, w_down
    )
    gate_x, d_normed, d_own = lax.optimization_barrier((gate_x, d_normed, d_own))
    far = call(join_kernel, [((320, 512), BF16)] * 4, [pltpu.VMEM((384, 512), BF16)], scalars=1)(
        lengths, context, d_query, d_own, from_before, from_after
    )
    far, gate_x = lax.optimization_barrier((far, gate_x))
    far_x = turn_x(far)
    keep, send, cot_own = call(
        gate_grads_kernel,
        [((8, 112, 512), BF16), ((8, 112, 512), BF16), ((256, 512), BF16)],
        [pltpu.VMEM((512, 512), BF16), pltpu.VMEM((512, 1024), BF16)],
        scalars=1,
    )(lengths, normed, *in_x, *gate_x)
    gate_y = turn_y(
        call(turn_add_kernel, [((2, 112, 512), BF16)] * 4, scalars=1)(lengths, keep, other_core(send))
    )
    far_x, gate_y[1] = lax.optimization_barrier((far_x, gate_y[1]))
    attention_keep, send = call(
        attention_grads_kernel,
        [((8, 64, 512), BF16), ((8, 64, 512), BF16)],
        [pltpu.VMEM((512, 512), BF16), pltpu.VMEM((384, 512), BF16)],
        scalars=1,
    )(lengths, normed, cot_own, *far_x)
    attention_keep, gate_y = lax.optimization_barrier((attention_keep, gate_y))
    gate_keep, gate_send = call(gate_sum_kernel, [((112, 512), BF16, HBM)] * 2, scalars=1)(lengths, *gate_y)
    attention_keep, gate_send = lax.optimization_barrier((attention_keep, gate_send))
    (parts,) = call(add_kernel, [((8, 64, 512), BF16, HBM)])(attention_keep, other_core(send))
    parts = lax.all_to_all(parts, ("z_low", "y"), 0, 0)
    gate_far = lax.ppermute(gate_send, "z_low", [(0, 1), (1, 0)])
    layer_out, d_frames = call(
        rows_kernel,
        [wide, wide],
        [pltpu.VMEM((ROWS, 512), BF16), pltpu.VMEM((1536, ROWS), BF16), pltpu.VMEM((384, ROWS), BF16)],
        scalars=1,
    )(
        lengths, frames, cotangent, *far_x, layer_part, d_normed, *in_hbm(w_qkv, w_out)
    )
    parts, layer_out, d_frames = lax.optimization_barrier((parts, layer_out, d_frames))
    parts = call(
        chunk_sum_kernel, [((176, 128), BF16)] * 4, [pltpu.VMEM((4, 176, 128), BF16)], scalars=1
    )(lengths, gate_keep, gate_far, parts)
    g_qkv, g_out, g_up, g_down, g_kernel = call(
        final_kernel,
        [((48, 128), F32), ((32, HEAD), F32), ((64, 128), F32), ((32, 128), F32), ((TAPS, 32), F32)],
        [pltpu.VMEM((4, 176, 128), F32)],
        scalars=1,
    )(lengths, *turn_z(parts))
    return (layer_out[None], d_frames[None], g_qkv.T, g_out.T, g_up.T, g_down.T, g_kernel)


def solution(mesh):
    split = Mesh(mesh.devices.reshape(2, 4, 4, 4, 2), SEQ + ("z_high", "core"))
    dp = ("z_high", "core")
    return jax.shard_map(
        local,
        mesh=split,
        in_specs=(P(dp, SEQ, None), P(dp, SEQ, None), P(dp), P(), P(), P(), P(), P()),
        out_specs=(
            P(dp, SEQ, None),
            P(dp, SEQ, None),
            P(dp, SEQ),
            P(dp, SEQ),
            P(dp, SEQ),
            P(dp, SEQ),
            P(None, SEQ),
        ),
        check_vma=False,
    )
```

```python
import jax
import jax.numpy as jnp
from jax import lax
from jax.experimental import pallas as pl
from jax.experimental.pallas import tpu as pltpu
from jax.sharding import Mesh, PartitionSpec as P

HEAD = 64
BAND = 512
ROWS = 128
GROUP = 4
WINDOW = 2 * BAND + ROWS
MARGIN = 15
TAPS = 31

EPSILON = 1e-05
NEG_LARGE = -3e38
HALF_ROOT = 0.7071067811865476
NORMAL_PEAK = 0.3989422804014327

BF16 = jnp.bfloat16
F32 = jnp.float32
HBM = pltpu.HBM
VMEM_LIMIT = 24 * 2**20


def call(body, outs, scratch=(), scalars=0, left=0):
    def run(*args):
        specs = [pl.BlockSpec(memory_space=pltpu.SMEM)] * scalars
        specs += [pl.BlockSpec(memory_space=pltpu.VMEM)] * (len(args) - scalars - left)
        specs += [pl.BlockSpec(memory_space=HBM)] * left
        return pl.pallas_call(
            body,
            out_shape=[
                HBM(*out[:2]) if len(out) > 2 else jax.ShapeDtypeStruct(*out) for out in outs
            ],
            in_specs=specs,
            out_specs=[pl.BlockSpec(memory_space=pltpu.VMEM)] * len(outs),
            scratch_shapes=list(scratch),
            compiler_params=pltpu.CompilerParams(vmem_limit_bytes=VMEM_LIMIT),
        )(*args)

    return run


def in_hbm(*arrays):
    return [pltpu.with_memory_space_constraint(array, HBM) for array in arrays]


def dot(left, right, left_dim=1, right_dim=0):
    return lax.dot_general(
        left, right, (((left_dim,), (right_dim,)), ((), ())), preferred_element_type=F32
    )


def normalize(values):
    centred = values - jnp.mean(values, axis=-1, keepdims=True)
    inverse = lax.rsqrt(jnp.mean(centred * centred, axis=-1, keepdims=True) + EPSILON)
    return (centred * inverse, inverse)


def norm_back(gradient, unit_rows, inverse):
    return inverse * (
        gradient
        - jnp.mean(gradient, axis=-1, keepdims=True)
        - unit_rows * jnp.mean(gradient * unit_rows, axis=-1, keepdims=True)
    )


def locate(lengths):
    z_low, y, x = lax.axis_index("z_low"), lax.axis_index("y"), lax.axis_index("x")
    row = 4 * z_low + y
    return ((4 * row + x) * ROWS, lengths[0], lax.axis_index("core"), row * (GROUP * ROWS), x, lax.axis_index("z_high"), y, z_low)


def slot(place, turn):
    return (place[4] + 4 - turn) & 3


def span(index, size):
    return pl.ds(pl.multiple_of(index * size, size), size)


def send_kernel(lengths, frames, cotangent, w_out, out_0, out_1, out_2, out_3, d_context, cot_t):
    place = locate(lengths)
    d_context[...] = dot(cotangent[...], w_out[...], 1, 1).astype(BF16)
    cot_t[...] = cotangent[...].T
    for turn, ref in enumerate((out_0, out_1, out_2, out_3)):
        x = (place[4] + turn) & 3
        ref[:, :1024] = frames[...]
        ref[:, 1024:1152] = d_context[:, span(x, 128)]
        for m in range(8):
            lanes = slice(1152 + 128 * (m // 4), 1280 + 128 * (m // 4))
            ref[32 * (m % 4) : 32 * (m % 4) + 32, lanes] = cot_t[span(4 * m + x, 32), :]


def project_kernel(lengths, frames_0, frames_1, frames_2, frames_3, w_qkv, normed, query, kv):
    place = locate(lengths)
    x = place[4]
    for turn, ref in enumerate((frames_0, frames_1, frames_2, frames_3)):
        unit_rows, _ = normalize(ref[:, :1024].astype(F32))
        normed[span(slot(place, turn), ROWS), :] = unit_rows.astype(BF16)
    weight = jnp.concatenate([w_qkv[:, span(x + 4 * part, 128)] for part in range(3)], axis=1)
    joined = dot(normed[...], weight).astype(BF16)
    query[...] = joined[:, :128].reshape(4, ROWS, 128)
    kv[...] = joined[:, 128:].reshape(4, ROWS, 256)


def gate_kernel(
    lengths, frames, cotangent, w_up, w_down,
    resid, d_gated, gating, d_conv, unit, inverse, slope, top, bottom,
    up, down, copied
):
    place = locate(lengths)
    first_frame, length = place[0], place[1]
    copies = [
        pltpu.make_async_copy(w_up.at[:, pl.ds(1024 * half, 1024)], up.at[half], copied.at[half]) for half in (1, 0)
    ] + [pltpu.make_async_copy(w_down, down, copied.at[2])]
    for copy in copies:
        copy.start()
    unit_rows, _ = normalize(frames[...].astype(F32))
    unit_rows = unit_rows.astype(BF16)
    hidden = [None, None]
    for half, copy in ((1, copies[0]), (0, copies[1])):
        copy.wait()
        upper = dot(unit_rows, up[half])
        phi = 0.5 * (1.0 + lax.erf(upper * HALF_ROOT))
        slope[:, 1024 * half : 1024 * half + 1024] = phi + upper * jnp.exp(-0.5 * upper * upper) * NORMAL_PEAK
        hidden[half] = (upper * phi).astype(BF16)
    gate_unit, gate_inv = normalize(hidden[1].astype(F32))
    unit[...] = gate_unit
    inverse[...] = jnp.broadcast_to(gate_inv, inverse.shape)
    rows = first_frame + lax.broadcasted_iota(jnp.int32, (ROWS, 1024), 0)
    masked = jnp.where(rows < length, gate_unit, 0.0).astype(BF16)
    gating[...] = masked
    resid[...] = hidden[0]
    copies[2].wait()
    back = dot(cotangent[...], down[...], 1, 1).astype(BF16)
    d_gated[...] = back
    conv_back = (back.astype(F32) * hidden[0].astype(F32)).astype(BF16)
    d_conv[...] = conv_back
    top[:, :1024] = masked[:16]
    top[:, 1024:] = conv_back[:16]
    bottom[:, :1024] = masked[112:]
    bottom[:, 1024:] = conv_back[112:]


def conv_inner_kernel(gating, d_conv, taps, conv_out, d_gating, g_taps, gate_ext, conv_ext, sums):
    for ext, ref in ((gate_ext, gating), (conv_ext, d_conv)):
        ext[:, :16] = jnp.zeros((8, 16, 128), F32)
        ext[:, 144:] = jnp.zeros((8, 16, 128), F32)
        for block in range(8):
            ext[block, 16:144] = ref[:, 128 * block : 128 * block + 128].astype(F32)
    sums[...] = jnp.zeros_like(sums)

    def chunk(index, _):
        lanes = pl.ds(pl.multiple_of(index * 128, 128), 128)
        for first in (0, 64):
            own = conv_ext[index, 16 + first : 80 + first, :]
            forward = jnp.zeros((64, 128), F32)
            for shift in range(8):
                moved = gate_ext[index, pl.ds(first + shift, 88), :]
                for step in range(4):
                    offset = 8 * step + shift
                    if 1 <= offset <= TAPS:
                        part = moved[8 * step : 8 * step + 64]
                        forward = forward + taps[offset - 1 : offset, lanes] * part
                        sums[offset - 1, :, lanes] += jnp.sum((part * own).reshape(8, 8, 128), axis=0)
            conv_out[first : first + 64, lanes] = forward
            backward = jnp.zeros((64, 128), F32)
            for shift in range(8):
                moved = conv_ext[index, pl.ds(first + shift, 88), :]
                for step in range(4):
                    offset = 8 * step + shift
                    if 1 <= offset <= TAPS:
                        part = moved[8 * step : 8 * step + 64]
                        backward = backward + taps[TAPS - offset : TAPS - offset + 1, lanes] * part
            d_gating[first : first + 64, lanes] = backward
        return 0

    lax.fori_loop(0, 8, chunk, 0)
    g_taps[...] = jnp.sum(sums[...], axis=1)


def conv_outer_kernel(
    lengths, conv_in, d_gating_in, g_taps_in, d_conv, resid, d_gated, unit, inverse, slope, before, after, taps,
    d_upper, out_0, out_1, out_2, out_3, conv_out, d_gating, before_ext, after_ext, g_taps, d_upper_t, g_taps_t
):
    place = locate(lengths)
    first_frame, length = place[0], place[1]
    conv_out[...] = conv_in[...]
    d_gating[...] = d_gating_in[...]
    g_taps[...] = g_taps_in[...]
    before_ext[:, 16:] = jnp.zeros((16, 16, 128), F32)
    after_ext[:, :16] = jnp.zeros((16, 16, 128), F32)
    for block in range(16):
        before_ext[block, :16] = before[:, 128 * block : 128 * block + 128].astype(F32)
        after_ext[block, 16:] = after[:, 128 * block : 128 * block + 128].astype(F32)

    def chunk(index, _):
        lanes = pl.ds(pl.multiple_of(index * 128, 128), 128)
        for ext, first, skip in ((before_ext, 0, 0), (after_ext, 112, 16)):
            own = d_conv[first : first + 16, lanes].astype(F32)
            forward = conv_out[first : first + 16, lanes]
            backward = d_gating[first : first + 16, lanes]
            for step in range(1, 16):
                offset = step + skip
                part = ext[index, pl.ds(step, 16), :]
                forward = forward + taps[offset - 1 : offset, lanes] * part
                g_taps[offset - 1 : offset, lanes] += jnp.sum(part * own, axis=0, keepdims=True)
                part = ext[index + 8, pl.ds(step, 16), :]
                backward = backward + taps[TAPS - offset : TAPS - offset + 1, lanes] * part
            conv_out[first : first + 16, lanes] = forward
            d_gating[first : first + 16, lanes] = backward
        return 0

    lax.fori_loop(0, 8, chunk, 0)
    conv = conv_out[...]
    gated = (resid[...].astype(F32) * conv).astype(BF16)
    rows = first_frame + lax.broadcasted_iota(jnp.int32, (ROWS, 1024), 0)
    d_gate = jnp.where(rows < length, d_gating[...], 0.0)
    d_gate = norm_back(d_gate, unit[...], inverse[:, :1])
    left = (d_gated[...].astype(F32) * conv * slope[:, :1024]).astype(BF16)
    right = (d_gate * slope[:, 1024:]).astype(BF16)
    d_upper[:, :1024] = left
    d_upper[:, 1024:] = right
    d_upper_t[:1024] = left.T
    d_upper_t[1024:] = right.T
    turned = jnp.concatenate([g_taps[...], jnp.zeros((96, 1024), F32)], axis=0).T.reshape(32, 32, 128)
    g_taps_t[...] = (turned[:, :16, :] + pltpu.roll(turned[:, 16:, :], 32, 2)).astype(BF16)
    for turn, ref in enumerate((out_0, out_1, out_2, out_3)):
        x = (place[4] + turn) & 3
        for m in range(8):
            ref[64 * m : 64 * m + 64] = d_upper_t[span(4 * m + x, 64), :]
            ref[576 + 128 * m : 704 + 128 * m] = gated[:, 128 * m : 128 * m + 128]
        for pair in range(4):
            right = pltpu.roll(g_taps_t[8 * pair + 4 + x].astype(F32), 64, 1)
            ref[512 + 16 * pair : 528 + 16 * pair] = (g_taps_t[8 * pair + x].astype(F32) + right).astype(BF16)


def own_columns(array, core, width):
    parts = [
        array[:, pl.ds(pl.multiple_of(2 * width * z + width * core, width), width)] for z in range(4)
    ]
    return jnp.concatenate(parts, axis=1)


def gate_grads_kernel(
    lengths, normed, cot_0, cot_1, cot_2, cot_3, gate_0, gate_1, gate_2, gate_3,
    keep, send, cot_own, d_upper_t, gated
):
    place = locate(lengths)
    x, core = place[4], place[2]
    gates = (gate_0, gate_1, gate_2, gate_3)
    g_taps = gate_0[512:576].astype(F32)
    for ref in gates[1:]:
        g_taps = g_taps + ref[512:576].astype(F32)
    left = g_taps.reshape(4, 16, 128)
    g_taps = jnp.stack([left, pltpu.roll(left, 64, 2)], axis=1).reshape(8, 16, 128).astype(BF16)
    for turn, (gate, cot) in enumerate(zip(gates, (cot_0, cot_1, cot_2, cot_3))):
        here = span(slot(place, turn), 128)
        d_upper_t[:, here] = gate[:512]
        for block in range(8):
            gated[here, 128 * block : 128 * block + 128] = gate[576 + 128 * block : 704 + 128 * block]
        cot_own[:128, here] = cot[:, 1152:1280]
        cot_own[128:, here] = cot[:, 1280:]
    for parity, out in ((core, keep), (1 - core, send)):
        grad = dot(d_upper_t[...], own_columns(normed, parity, 128))
        out[:, :64, :] = grad.astype(BF16).reshape(8, 64, 512)
        grad = dot(cot_own[...], own_columns(gated, parity, 128))
        out[:, 64:96, :] = grad.astype(BF16).reshape(8, 32, 512)
        for z in range(4):
            out[:, 96:, 128 * z : 128 * z + 128] = g_taps


def attention_grads_kernel(
    lengths, normed, cot_own, far_0, far_1, far_2, far_3,
    keep, send, context, rows_t
):
    place = locate(lengths)
    core = place[2]
    for turn, far in enumerate((far_0, far_1, far_2, far_3)):
        for block in range(GROUP):
            tokens = slice(128 * block, 128 * block + 128)
            context[tokens, span(slot(place, turn), 128)] = far[96:224, tokens]
    for x in range(4):

        @pl.when(place[4] == x)
        def _():
            for turn, far in enumerate((far_0, far_1, far_2, far_3)):
                for index, (_, there) in enumerate(unit_rows_of((x - turn) % 4, x)):
                    rows_t[16 * there : 16 * there + 16] = far[16 * index : 16 * index + 16]

    lane = lax.broadcasted_iota(jnp.int32, (512, 128), 1)
    blocks, swapped = [], []
    for z in range(4):
        block = context[:, 128 * z : 128 * z + 128].astype(F32)
        blocks.append(block)
        swapped.append(pltpu.roll(block, HEAD, 1))
    lane_out = lax.broadcasted_iota(jnp.int32, (8, 16, 512), 2)
    for parity, out in ((core, keep), (1 - core, send)):
        grad = dot(rows_t[...], own_columns(normed, parity, 128))
        out[:, :48, :] = grad.astype(BF16).reshape(8, 48, 512)
        mine = (lane < HEAD) == (parity == 0)
        doubled = jnp.concatenate(
            [jnp.where(mine, block, other) for block, other in zip(blocks, swapped)], axis=1
        ).astype(BF16)
        grad = dot(cot_own[...], doubled).reshape(8, 32, 512)
        out[:, 48:, :] = jnp.where((lane_out & 127) < HEAD, grad[:, :16], grad[:, 16:]).astype(BF16)


def attend_kernel(
    lengths, queries, kv, before, after, cot_0, cot_1, cot_2, cot_3, context_out, d_query, d_before, d_after, d_own,
    d_contexts, key, value, key_t, value_t, scores, weights, d_scores, d_key, d_value
):
    place = locate(lengths)
    group_first, length = place[3], place[1]
    for turn, ref in enumerate((cot_0, cot_1, cot_2, cot_3)):
        d_contexts[slot(place, turn)] = ref[:, 1024:1152]
    for part, ref in enumerate((before, kv, after)):
        for piece in range(GROUP):
            start = 512 * part + ROWS * piece
            key_block = ref[piece, :, :128]
            value_block = ref[piece, :, 128:]
            key[start : start + ROWS] = key_block
            value[start : start + ROWS] = value_block
            key_t[:, start : start + ROWS] = key_block.T
            value_t[:, start : start + ROWS] = value_block.T
    d_key[...] = jnp.zeros_like(d_key)
    d_value[...] = jnp.zeros_like(d_value)
    lane = lax.broadcasted_iota(jnp.int32, (ROWS, 128), 1)
    first_head = lane < HEAD
    query_index = lax.broadcasted_iota(jnp.int32, (1, 256), 1)
    query_index = jnp.where(query_index < ROWS, query_index, query_index - ROWS)
    chunks = WINDOW // 128
    for block in range(GROUP):
        base = ROWS * block
        low = jnp.maximum(query_index, 512 - group_first - base)
        high = jnp.minimum(query_index + 1024, length - group_first + 511 - base)
        query = queries[block].astype(F32) * 0.125
        d_context = d_contexts[block].astype(F32)
        zero = jnp.zeros_like(query)
        query_pair = jnp.concatenate(
            [jnp.where(first_head, query, zero), jnp.where(first_head, zero, query)], axis=0
        ).astype(BF16)
        d_pair = jnp.concatenate(
            [jnp.where(first_head, d_context, zero), jnp.where(first_head, zero, d_context)], axis=0
        ).astype(BF16)

        def allowed_of(index):
            position = 128 * index + lax.broadcasted_iota(jnp.int32, (128, 256), 0)
            if 0 < index < chunks - 1:
                last = length - group_first + 511 - base
                return position <= jnp.where(128 * index >= 512 - group_first - base, last, -1)
            return (position >= low) & (position <= high)

        peak = jnp.full((128, 256), NEG_LARGE, F32)
        for index in range(chunks):
            part = dot(key[base + 128 * index : base + 128 * index + 128], query_pair, 1, 1)
            part = jnp.where(allowed_of(index), part, NEG_LARGE)
            scores[128 * index : 128 * index + 128] = part
            peak = jnp.maximum(peak, part)
        peak = jnp.max(peak, axis=0, keepdims=True)
        total = jnp.zeros((128, 256), F32)
        for index in range(chunks):
            part = scores[128 * index : 128 * index + 128]
            part = jnp.exp(part - peak)
            scores[128 * index : 128 * index + 128] = part
            total = total + part
        some = jnp.maximum(low, 0) <= jnp.minimum(high, WINDOW - 1)
        scale = jnp.where(some, 1.0 / jnp.maximum(jnp.sum(total, axis=0, keepdims=True), 1.0), 0.0)
        for index in range(chunks):
            part = scores[128 * index : 128 * index + 128] * scale
            weights[128 * index : 128 * index + 128] = part.astype(BF16)
        wide = dot(value_t[:, base : base + WINDOW], weights[...])
        context_t = jnp.concatenate([wide[:HEAD, :128], wide[HEAD:, 128:]], axis=0)
        context_out[block] = context_t.T.astype(BF16)
        product = context_t * d_context.T
        row_dot = jnp.concatenate(
            [
                jnp.sum(product[:HEAD], axis=0, keepdims=True),
                jnp.sum(product[HEAD:], axis=0, keepdims=True),
            ],
            axis=1,
        )
        for index in range(chunks):
            part = dot(value[base + 128 * index : base + 128 * index + 128], d_pair, 1, 1)
            part = weights[128 * index : 128 * index + 128].astype(F32) * (part - row_dot)
            d_scores[128 * index : 128 * index + 128] = part.astype(BF16)
        wide = dot(key_t[:, base : base + WINDOW], d_scores[...])
        d_query_t = jnp.concatenate([wide[:HEAD, :128], wide[HEAD:, 128:]], axis=0)
        d_query[:, base : base + 128] = (d_query_t * 0.125).astype(BF16)
        d_key[base : base + WINDOW] += dot(d_scores[...], query_pair)
        d_value[base : base + WINDOW] += dot(weights[...], d_pair)
    for piece in range(GROUP):
        for part, ref in enumerate((d_before, d_own, d_after)):
            start = 512 * part + ROWS * piece
            ref[piece, :, :128] = d_key[start : start + ROWS].astype(ref.dtype)
            ref[piece, :, 128:] = d_value[start : start + ROWS].astype(ref.dtype)


def unit_rows_of(source, target):
    units = [32 * part + 8 * source + row for part in range(3) for row in range(8)]
    wanted = [unit for unit in units if (unit // 3) % 4 == target]
    return [(units.index(unit), unit // 12 * 3 + unit % 3) for unit in wanted]


def join_kernel(
    lengths, context, d_query, own, from_before, from_after,
    unit_0, unit_1, unit_2, unit_3, joined_t
):
    place = locate(lengths)
    joined_t[:128] = d_query[...]
    for piece in range(GROUP):
        total = own[piece] + from_before[piece].astype(F32) + from_after[piece].astype(F32)
        total = total.astype(BF16)
        joined_t[128:256, 128 * piece : 128 * piece + 128] = total[:, :128].T
        joined_t[256:, 128 * piece : 128 * piece + 128] = total[:, 128:].T
    for turn, ref in enumerate((unit_0, unit_1, unit_2, unit_3)):
        for block in range(GROUP):
            lanes = slice(128 * block, 128 * block + 128)
            ref[96:224, lanes] = context[block]
            ref[224:, lanes] = joined_t[96 * block : 96 * block + 96, span((place[4] + turn) & 3, 128)]
    for x in range(4):

        @pl.when(place[4] == x)
        def _():
            for turn, ref in enumerate((unit_0, unit_1, unit_2, unit_3)):
                for index, (here, _) in enumerate(unit_rows_of(x, (x + turn) % 4)):
                    ref[16 * index : 16 * index + 16] = joined_t[16 * here : 16 * here + 16]


def gate_rows_kernel(frames, gate, d_upper, w_up, w_down, layer_part, d_normed):
    gated = jnp.concatenate([gate[576 + 128 * m : 704 + 128 * m] for m in range(8)], axis=1)
    layer_part[...] = frames[...].astype(F32) + dot(gated, w_down[...])
    d_normed[...] = dot(d_upper[...], w_up[...], 1, 1)


def rows_kernel(
    lengths, frames, cotangent, far_0, far_1, far_2, far_3, layer_part, d_normed,
    w_qkv, w_out, layer_out, d_frames, context, joined_t, back
):
    place = locate(lengths)
    for turn, far in enumerate((far_0, far_1, far_2, far_3)):
        pair = slot(place, turn)
        context[:, span(pair, 128)] = far[96:224, span(place[4], 128)]
        for block in range(4):
            back[96 * block : 96 * block + 96] = far[224:, 128 * block : 128 * block + 128]
        for part in range(3):
            joined_t[span(pair + 4 * part, 128), :] = back[128 * part : 128 * part + 128]
    layer_out[...] = (layer_part[...] + dot(context[...], w_out[...])).astype(BF16)
    unit_rows, inverse = normalize(frames[...].astype(F32))
    d_rows = d_normed[...] + dot(joined_t[...].T, w_qkv[...], 1, 1)
    d_frames[...] = (cotangent[...].astype(F32) + norm_back(d_rows, unit_rows, inverse)).astype(BF16)


def add_kernel(near, far, out):
    out[...] = (near[...].astype(F32) + far[...].astype(F32)).astype(BF16)


def turn_add_kernel(lengths, near, far, out_0, out_1, out_2, out_3):
    place = locate(lengths)
    for turn, ref in enumerate((out_0, out_1, out_2, out_3)):
        for z_low in range(2):
            m = 4 * z_low + ((place[6] + turn) & 3)
            ref[z_low] = (near[m].astype(F32) + far[m].astype(F32)).astype(BF16)


def gate_sum_kernel(lengths, part_0, part_1, part_2, part_3, keep, send):
    place = locate(lengths)
    for out, z_low in ((keep, place[7]), (send, 1 - place[7])):
        total = part_0[z_low].astype(F32)
        for part in (part_1, part_2, part_3):
            total = total + part[z_low].astype(F32)
        out[...] = total.astype(BF16)


def chunk_sum_kernel(lengths, gate, gate_far, parts, out_0, out_1, out_2, out_3, total):
    place = locate(lengths)
    for first in range(0, 176, 16):
        rows = slice(first, first + 16)
        if first < 112:
            acc = gate[rows].astype(F32) + gate_far[rows].astype(F32)
        else:
            acc = parts[0, first - 112 : first - 96].astype(F32)
            for source in range(1, 8):
                acc = acc + parts[source, first - 112 : first - 96].astype(F32)
        for z in range(4):
            total[z, rows, :] = acc[:, 128 * z : 128 * z + 128].astype(BF16)
    for turn, ref in enumerate((out_0, out_1, out_2, out_3)):
        ref[...] = total[(place[5] + turn) & 3]


def final_kernel(lengths, part_0, part_1, part_2, part_3, g_qkv_t, g_out_t, g_up_t, g_down_t, g_taps, ordered):
    place = locate(lengths)
    for turn, ref in enumerate((part_0, part_1, part_2, part_3)):
        ordered[(place[5] + 4 - turn) & 3] = ref[...].astype(F32)
    total = (ordered[0] + ordered[1]) + (ordered[2] + ordered[3])
    g_up_t[...] = total[:64]
    g_down_t[...] = total[64:96]
    turned = total[96:112].T
    g_taps[...] = jnp.concatenate([turned[:TAPS], turned[32 : 32 + TAPS]], axis=1)
    g_qkv_t[...] = total[112:160]
    g_out_t[:16] = total[160:, :HEAD]
    g_out_t[16:] = total[160:, HEAD:]


SEQ = ("z_low", "y", "x")


def shift(array, by):
    return lax.ppermute(array, SEQ, [(i, i + by) for i in range(32) if 0 <= i + by < 32])


def other_core(array):
    return lax.ppermute(array, "core", [(0, 1), (1, 0)])


def turn_x(pieces):
    return [pieces[0]] + [
        lax.ppermute(pieces[by], "x", [(i, (i + by) % 4) for i in range(4)]) for by in range(1, 4)
    ]


def turn_y(pieces):
    return [pieces[0]] + [
        lax.ppermute(pieces[by], "y", [(i, (i + by) % 4) for i in range(4)]) for by in range(1, 4)
    ]


def turn_z(pieces):
    return [pieces[0]] + [
        lax.ppermute(pieces[by], "z_high", [(i, (i + by) % 4) for i in range(4)]) for by in range(1, 4)
    ]


def local(frames, cotangent, lengths, w_qkv, w_out, w_up, w_down, conv_kernel):
    frames, cotangent = frames[0], cotangent[0]
    wide = ((ROWS, 1024), BF16)
    wide_f = ((ROWS, 1024), F32)
    quad = ((4, ROWS, 256), BF16)
    piece = ((ROWS, 1408), BF16)
    pieces = call(
        send_kernel, [piece] * 4, [pltpu.VMEM((ROWS, 512), BF16), pltpu.VMEM((1024, ROWS), BF16)], scalars=1
    )(lengths, *in_hbm(frames, cotangent, w_out))
    pieces, frames_later = lax.optimization_barrier((pieces, frames))
    in_x = turn_x(pieces)
    resid, d_gated, gating, d_conv, unit, inverse, slope, top, bottom = call(
        gate_kernel,
        [wide, wide, wide, wide, wide_f, ((ROWS, 128), F32), ((ROWS, 2048), F32),
         ((16, 2048), BF16), ((16, 2048), BF16)],
        [pltpu.VMEM((2, 1024, 1024), BF16), pltpu.VMEM((1024, 1024), BF16), pltpu.SemaphoreType.DMA((3,))],
        scalars=1,
        left=2,
    )(lengths, *in_hbm(frames_later, cotangent, w_up, w_down))
    before, after = shift(bottom, 1), shift(top, -1)
    conv_in, d_gating_in, g_taps_in = call(
        conv_inner_kernel,
        [wide_f, wide_f, ((32, 1024), F32)],
        [pltpu.VMEM((8, 160, 128), F32), pltpu.VMEM((8, 160, 128), F32), pltpu.VMEM((32, 8, 1024), F32)],
    )(gating, d_conv, conv_kernel)
    in_x, conv_in, before, after = lax.optimization_barrier((in_x, conv_in, before, after))
    normed, query, kv = call(
        project_kernel, [((512, 1024), BF16), ((4, ROWS, 128), BF16), quad], scalars=1
    )(lengths, *in_x, w_qkv)
    kv_before, kv_after = shift(kv, 4), shift(kv, -4)
    conv_in, kv = lax.optimization_barrier((conv_in, kv))
    gate = ((1600, 128), BF16)
    d_upper, *gate_x = call(
        conv_outer_kernel,
        [((ROWS, 2048), BF16, HBM), gate, gate, gate, gate],
        [pltpu.VMEM((ROWS, 1024), F32), pltpu.VMEM((ROWS, 1024), F32),
         pltpu.VMEM((16, 32, 128), F32), pltpu.VMEM((16, 32, 128), F32),
         pltpu.VMEM((32, 1024), F32), pltpu.VMEM((2048, ROWS), BF16), pltpu.VMEM((32, 16, 128), BF16)],
        scalars=1,
    )(lengths, conv_in, d_gating_in, g_taps_in, d_conv, resid, d_gated, unit, inverse, slope, before, after, conv_kernel)
    gate_x, kv_before = lax.optimization_barrier((gate_x, kv_before))
    gate_x = turn_x(gate_x)
    context, d_query, d_before, d_after, d_own = call(
        attend_kernel,
        [((4, ROWS, 128), BF16), ((ROWS, 512), BF16), quad, quad, ((4, ROWS, 256), F32)],
        [pltpu.VMEM((4, ROWS, 128), BF16),
         pltpu.VMEM((1536, 128), BF16), pltpu.VMEM((1536, 128), BF16),
         pltpu.VMEM((128, 1536), BF16), pltpu.VMEM((128, 1536), BF16),
         pltpu.VMEM((WINDOW, 256), F32), pltpu.VMEM((WINDOW, 256), BF16), pltpu.VMEM((WINDOW, 256), BF16),
         pltpu.VMEM((1536, 128), F32), pltpu.VMEM((1536, 128), F32)],
        scalars=1,
    )(lengths, query, kv, kv_before, kv_after, *in_x)
    from_before, from_after = shift(d_after, 4), shift(d_before, -4)
    frames_later, d_own = lax.optimization_barrier((frames, d_own))
    layer_part, d_normed = call(gate_rows_kernel, [wide_f + (HBM,), wide_f + (HBM,)])(
        *in_hbm(frames_later), gate_x[0], *in_hbm(d_upper), w_up, w_down
    )
    gate_x, d_normed, d_own = lax.optimization_barrier((gate_x, d_normed, d_own))
    far = call(join_kernel, [((320, 512), BF16)] * 4, [pltpu.VMEM((384, 512), BF16)], scalars=1)(
        lengths, context, d_query, d_own, from_before, from_after
    )
    far, gate_x = lax.optimization_barrier((far, gate_x))
    far_x = turn_x(far)
    keep, send, cot_own = call(
        gate_grads_kernel,
        [((8, 112, 512), BF16), ((8, 112, 512), BF16), ((256, 512), BF16)],
        [pltpu.VMEM((512, 512), BF16), pltpu.VMEM((512, 1024), BF16)],
        scalars=1,
    )(lengths, normed, *in_x, *gate_x)
    gate_y = turn_y(
        call(turn_add_kernel, [((2, 112, 512), BF16)] * 4, scalars=1)(lengths, keep, other_core(send))
    )
    far_x, gate_y[1] = lax.optimization_barrier((far_x, gate_y[1]))
    attention_keep, send = call(
        attention_grads_kernel,
        [((8, 64, 512), BF16), ((8, 64, 512), BF16)],
        [pltpu.VMEM((512, 512), BF16), pltpu.VMEM((384, 512), BF16)],
        scalars=1,
    )(lengths, normed, cot_own, *far_x)
    send, gate_y = lax.optimization_barrier((send, gate_y))
    gate_keep, gate_send = call(gate_sum_kernel, [((112, 512), BF16, HBM)] * 2, scalars=1)(lengths, *gate_y)
    attention_keep, gate_send = lax.optimization_barrier((attention_keep, gate_send))
    (parts,) = call(add_kernel, [((8, 64, 512), BF16, HBM)])(attention_keep, other_core(send))
    parts = lax.all_to_all(parts, ("z_low", "y"), 0, 0)
    gate_far = lax.ppermute(gate_send, "z_low", [(0, 1), (1, 0)])
    layer_out, d_frames = call(
        rows_kernel,
        [wide, wide],
        [pltpu.VMEM((ROWS, 512), BF16), pltpu.VMEM((1536, ROWS), BF16), pltpu.VMEM((384, ROWS), BF16)],
        scalars=1,
    )(
        lengths, frames, cotangent, *far_x, layer_part, d_normed, *in_hbm(w_qkv, w_out)
    )
    parts, layer_out, d_frames = lax.optimization_barrier((parts, layer_out, d_frames))
    parts = call(
        chunk_sum_kernel, [((176, 128), BF16)] * 4, [pltpu.VMEM((4, 176, 128), BF16)], scalars=1
    )(lengths, gate_keep, gate_far, parts)
    g_qkv, g_out, g_up, g_down, g_kernel = call(
        final_kernel,
        [((48, 128), F32), ((32, HEAD), F32), ((64, 128), F32), ((32, 128), F32), ((TAPS, 32), F32)],
        [pltpu.VMEM((4, 176, 128), F32)],
        scalars=1,
    )(lengths, *turn_z(parts))
    return (layer_out[None], d_frames[None], g_qkv.T, g_out.T, g_up.T, g_down.T, g_kernel)


def solution(mesh):
    split = Mesh(mesh.devices.reshape(2, 4, 4, 4, 2), SEQ + ("z_high", "core"))
    dp = ("z_high", "core")
    return jax.shard_map(
        local,
        mesh=split,
        in_specs=(P(dp, SEQ, None), P(dp, SEQ, None), P(dp), P(), P(), P(), P(), P()),
        out_specs=(
            P(dp, SEQ, None),
            P(dp, SEQ, None),
            P(dp, SEQ),
            P(dp, SEQ),
            P(dp, SEQ),
            P(dp, SEQ),
            P(None, SEQ),
        ),
        check_vma=False,
    )
```
